32 devices in a mesh: dp: 8 (over z, x), tower: 4 (over y, core).
Axes of the slice: x: 2, y: 2, z: 4, core: 2. Of those that a mesh axis runs over, the one named last changes fastest.
Arguments:
- tokens: bfloat16 [4, 16, 512, 768], P('tower', 'dp'), may hold values from -6 to 6
- lengths: int32 [4, 16], P('tower', 'dp'), may hold values from 32 to 512, as said below
- positive: int32 [32], replicated, may hold values from 0 to 31, each once
- w_qkv: bfloat16 [768, 2304], replicated, may hold values from -0.21875 to 0.21875
- q_bias: float32 [768], replicated, may hold values from -3 to 3
- v_bias: float32 [768], replicated, may hold values from -3 to 3
- w_out: bfloat16 [768, 768], replicated, may hold values from -1.75 to 1.75
- out_bias: float32 [768], replicated, may hold values from -2 to 2
- norm1_gain: float32 [768], replicated, may hold values from 0.5 to 1.5
- norm1_bias: float32 [768], replicated, may hold values from -2 to 2
- w_up: bfloat16 [768, 3072], replicated, may hold values from -0.21875 to 0.21875
- up_bias: float32 [3072], replicated, may hold values from -3 to 3
- w_down: bfloat16 [3072, 768], replicated, may hold values from -0.109375 to 0.109375
- down_bias: float32 [768], replicated, may hold values from -2 to 2
- norm2_gain: float32 [768], replicated, may hold values from 0.5 to 1.5
- norm2_bias: float32 [768], replicated, may hold values from -0.5 to 0.5
Outputs:
- loss: float32 [], replicated
- grad_tokens: float32 [4, 16, 512, 768], P('tower', 'dp')
- grad_w_qkv: float32 [768, 2304], replicated
- grad_q_bias: float32 [768], replicated
- grad_v_bias: float32 [768], replicated
- grad_w_out: float32 [768, 768], replicated
- grad_out_bias: float32 [768], replicated
- grad_norm1_gain: float32 [768], replicated
- grad_norm1_bias: float32 [768], replicated
- grad_w_up: float32 [768, 3072], replicated
- grad_up_bias: float32 [3072], replicated
- grad_w_down: float32 [3072, 768], replicated
- grad_down_bias: float32 [768], replicated
- grad_norm2_gain: float32 [768], replicated
- grad_norm2_bias: float32 [768], replicated
The draws below stay inside these ranges and needn't reach their ends.
Inputs may be any that keep to these rules, and one draw needn't show every extreme that they name: `lengths`: one sequence has length exactly 512. Each passage is the positive of exactly one query.
All inputs are finite; a program needn't handle non-finite values.
Results may differ from the reference program's by a relative error of at most 0.0074.
Values sent between devices are 32-bit elements; how exact they have to be, the bound alone decides.
No kernel may reach another device: no remote copies, remote signals or barrier semaphores. Data moves between devices by JAX's collectives and lax.ppermute only.
A program may use at most 192 MiB of HBM per device.

```python
import jax
import jax.numpy as jnp
from jax import lax

HD = 64
D = 768
FF = 3072
LEN = 512
SEQ_DEV = 2
HALF = 16
PAIRS = 32
N_DP = 8


def draw_lengths(key, part):
    key = jax.random.fold_in(key, 7)
    first, second = jax.random.split(key)
    values = jax.random.randint(first, (4 * HALF,), max(LEN // 16, 1), LEN + 1)
    place = jax.random.randint(second, (), 0, 4 * HALF)
    values = jnp.where(jnp.arange(4 * HALF) == place, LEN, values)
    return values.reshape(4, HALF).astype(jnp.int32)


def steps_of(key, shape, pieces, smallest, largest):
    def one(position, blocks):
        steps = jax.random.uniform(jax.random.fold_in(jax.random.fold_in(key, 6), position), (blocks,), jnp.float32, smallest / len(pieces), largest / len(pieces))
        return jnp.repeat(jnp.exp(steps), shape[position] // blocks).reshape((-1,) + (1,) * (len(shape) - position - 1))

    level = one(*pieces[0])
    for cut in pieces[1:]:
        level = level * one(*cut)
    return level


def centred(rng, shape, scale, most, pieces=(), kind=jnp.bfloat16):
    loudness = steps_of(rng, shape, pieces, -0.22, 0.18) if pieces else 1.0
    entries = jax.random.normal(rng, shape, jnp.float32) * scale * loudness
    return jnp.minimum(jnp.maximum(entries, -most), most).astype(kind)


def setup_inputs(seed: int = 0) -> dict:
    key_list = jax.random.split(jax.random.key(seed), 17)
    return {
        "tokens": centred(key_list[0], (4, HALF, LEN, D), 1.0, 6.0, ((0, 4), (1, 8))),
        "lengths": draw_lengths(jax.random.fold_in(key_list[16], 71), 0),
        "positive": jax.random.permutation(key_list[2], PAIRS).astype(jnp.int32),
        "w_qkv": centred(key_list[3], (D, 3 * D), D ** -0.5, 0.21875),
        "q_bias": centred(key_list[4], (D,), 0.3, 3.0, (), jnp.float32),
        "v_bias": centred(key_list[5], (D,), 0.3, 3.0, (), jnp.float32),
        "w_out": centred(key_list[6], (D, D), (max(D * 8 // LEN, 1)) ** -0.5, 1.75),
        "out_bias": centred(key_list[7], (D,), 0.2, 2.0, (), jnp.float32),
        "norm1_gain": jnp.clip(1.0 + 0.1 * jax.random.normal(key_list[8], (D,), jnp.float32), 0.5, 1.5),
        "norm1_bias": centred(key_list[9], (D,), 0.2, 2.0, (), jnp.float32),
        "w_up": centred(key_list[10], (D, FF), D ** -0.5, 0.21875),
        "up_bias": centred(key_list[11], (FF,), 0.3, 3.0, (), jnp.float32),
        "w_down": centred(key_list[12], (FF, D), FF ** -0.5, 0.109375),
        "down_bias": centred(key_list[13], (D,), 0.2, 2.0, (), jnp.float32),
        "norm2_gain": jnp.clip(1.0 + 0.1 * jax.random.normal(key_list[14], (D,), jnp.float32), 0.5, 1.5),
        "norm2_bias": centred(key_list[15], (D,), 0.05, 0.5, (), jnp.float32),
    }


@jax.custom_vjp
def low(v):
    return lax.optimization_barrier(v.astype(jnp.bfloat16)).astype(jnp.float32)

@jax.custom_vjp
def low_back(v):
    return v

def low_keep(v):
    return (low(v), None)

def low_pass(kept, grad):
    return (grad,)

def back_keep(v):
    return (v, None)

def back_low(kept, grad):
    return (low(grad),)
low.defvjp(low_keep, low_pass)
low_back.defvjp(back_keep, back_low)
SOFTMAX_TEMP = 0.01
NORM_EPS = 1e-06
FULL_PRECISION = lax.Precision.HIGHEST

def layer_norm(value_matrix, gain, shift):
    centre = value_matrix - lax.optimization_barrier(jnp.mean(value_matrix, axis=-1, keepdims=True))
    spread = lax.optimization_barrier(jnp.mean(centre * centre, axis=-1, keepdims=True))
    return centre * lax.rsqrt(spread + NORM_EPS) * gain + shift

def unit_rows(value_matrix):
    return value_matrix * lax.rsqrt(lax.optimization_barrier(jnp.sum(value_matrix * value_matrix, axis=-1, keepdims=True)) + NORM_EPS)

def contrast(pooled, positive):
    width = pooled.shape[-1]
    query_batch = unit_rows(pooled[:2].reshape(-1, width))
    passage_batch = unit_rows(pooled[2:].reshape(-1, width))
    similarity_logits = jnp.dot(query_batch, passage_batch.T, precision=FULL_PRECISION) / SOFTMAX_TEMP
    highest = lax.optimization_barrier(jnp.max(similarity_logits, axis=1, keepdims=True))
    totals = highest[:, 0] + jnp.log(lax.optimization_barrier(jnp.sum(jnp.exp(similarity_logits - highest), axis=1)))
    picked = jnp.where(jnp.arange(similarity_logits.shape[1])[None, :] == positive[:, None], similarity_logits, 0.0)
    return jnp.mean(totals - lax.optimization_barrier(jnp.sum(picked, axis=1)))

def mixing(value_matrix, params, counts):
    w_qkv, q_bias, v_bias, w_out, out_bias, gain_one, shift_one, w_up, up_bias, w_down, down_bias, gain_two, shift_two = params
    number, span, width = value_matrix.shape
    heads = width // HD
    flat = value_matrix.reshape(number * span, width)
    bias = jnp.concatenate([q_bias, jnp.zeros_like(q_bias), v_bias])
    proj = low(low_back(jnp.dot(flat, w_qkv, precision=FULL_PRECISION) + bias))
    proj = proj.reshape(number, span, 3, heads, HD)
    scores = jnp.einsum('slhd,smhd->shlm', proj[:, :, 0], proj[:, :, 1], precision=FULL_PRECISION) * HD ** (-0.5)
    scores = low_back(scores)
    valid = jnp.arange(span)[None, :] < counts[:, None]
    scores = jnp.where(valid[:, None, None, :], scores, -1e+30)
    highest = lax.optimization_barrier(jnp.max(scores, axis=-1, keepdims=True))
    expo = jnp.exp(scores - highest)
    attention_probabilities = low(expo / lax.optimization_barrier(jnp.sum(expo, axis=-1, keepdims=True)))
    context_vectors = jnp.einsum('shlm,smhd->slhd', attention_probabilities, proj[:, :, 2], precision=FULL_PRECISION).reshape(number * span, width)
    context_vectors = low(low_back(context_vectors))
    attn = low_back(jnp.dot(context_vectors, w_out, precision=FULL_PRECISION) + out_bias)
    hidden = layer_norm(flat + attn, gain_one, shift_one)
    upper = low_back(jnp.dot(low(hidden), w_up, precision=FULL_PRECISION) + up_bias)
    active = low(jax.nn.gelu(upper, approximate=False))
    down = low_back(jnp.dot(active, w_down, precision=FULL_PRECISION) + down_bias)
    output = layer_norm(hidden + down, gain_two, shift_two).reshape(number, span, width)
    mask = valid.astype(jnp.float32)
    return lax.optimization_barrier(jnp.sum(output * mask[:, :, None], axis=1)) / counts[:, None].astype(jnp.float32)

def reference(tokens, lengths, positive, w_qkv, q_bias, v_bias, w_out, out_bias, norm1_gain, norm1_bias, w_up, up_bias, w_down, down_bias, norm2_gain, norm2_bias):
    params = (w_qkv.astype(jnp.float32), q_bias, v_bias, w_out.astype(jnp.float32), out_bias, norm1_gain, norm1_bias, w_up.astype(jnp.float32), up_bias, w_down.astype(jnp.float32), down_bias, norm2_gain, norm2_bias)
    groups = tokens.astype(jnp.float32).reshape(4 * N_DP, SEQ_DEV, LEN, D)
    counts = lengths.reshape(4 * N_DP, SEQ_DEV)

    def total(groups, params):
        block = jax.checkpoint(mixing)

        def step(carry, item):
            return (carry, block(item[0], params, item[1]))
        _, pooled = lax.scan(step, jnp.zeros((), jnp.float32), (groups, counts))
        return contrast(pooled.reshape(4, HALF, D), positive)
    loss, pull = jax.vjp(total, groups, params)
    grad_groups, grads = pull(jnp.ones((), jnp.float32))
    return (loss, grad_groups.reshape(4, HALF, LEN, D), grads[0], grads[1], grads[2], grads[3], grads[4], grads[5], grads[6], grads[7], grads[8], grads[9], grads[10], grads[11], grads[12])
```

```python
from functools import partial

import jax
import jax.numpy as jnp
from jax import lax
from jax.experimental import pallas as pl
from jax.experimental.pallas import tpu as pltpu
from jax.sharding import PartitionSpec as P

HD = 64
SOFTMAX_TEMP = 0.01
NORM_EPS = 1e-06
MASKED = -1e30
F32 = jnp.float32
BF16 = jnp.bfloat16
ROOT_HALF = 0.7071067811865476
INV_ROOT_2PI = 0.3989422804014327
MIB = 1024 * 1024

SMEM = pl.BlockSpec(memory_space=pltpu.SMEM)
VMEM = pl.BlockSpec(memory_space=pltpu.VMEM)
ANY = pl.BlockSpec(memory_space=pl.ANY)


LIGHT = pl.CostEstimate(flops=1, bytes_accessed=1, transcendentals=0)


def params():
    return pltpu.CompilerParams(vmem_limit_bytes=62 * MIB)


def call(body, dep, grid, in_specs, out_specs, out_shape, scratch=(), scalars=0, name=None):
    n_in = scalars + len(in_specs)

    def run(*refs):
        if dep is None:
            return body(*refs)
        return body(*refs[:n_in], *refs[n_in + 1:])

    spec = pltpu.PrefetchScalarGridSpec(
        num_scalar_prefetch=scalars, grid=grid, in_specs=list(in_specs) + ([] if dep is None else [ANY]),
        out_specs=out_specs, scratch_shapes=scratch)
    made = pl.pallas_call(run, grid_spec=spec, out_shape=out_shape, compiler_params=params(), cost_estimate=LIGHT, name=name)
    return made if dep is None else lambda *args: made(*args, dep)


def shape(dims, kind):
    return jax.ShapeDtypeStruct(dims, kind)


def line(cols, index=lambda *_: (0,)):
    return pl.BlockSpec((cols,), index)


def row(ref):
    return ref[...].reshape(1, -1)


def fixed(dims):
    return pl.BlockSpec(dims, lambda *_: (0,) * len(dims), pipeline_mode=pl.Buffered(1))


def dot(a, b, ca=1, cb=0):
    return lax.dot_general(a, b, (((ca,), (cb,)), ((), ())), preferred_element_type=F32)


def key_mask(count, span):
    place = lax.broadcasted_iota(jnp.int32, (span, 1), 0)
    return jnp.where(place < count, 0.0, MASKED)


def attend_body(seqs, span, group, counts, x, wq, wk, wv, qb, vb, q_out, k_out, v_out, ctx, lse):
    q_out[...] = (dot(x[...], wq[...]) + row(qb)).astype(BF16)
    k_out[...] = dot(x[...], wk[...]).astype(BF16)
    v_out[...] = (dot(x[...], wv[...]) + row(vb)).astype(BF16)
    for s in range(seqs):
        rows = pl.ds(s * span, span)
        mask = key_mask(counts[0, s], span)
        for pair in range(group // 2):
            both = []
            for half in range(2):
                head = pair * 2 + half
                lanes = pl.ds(head * HD, HD)
                query = q_out[rows, lanes] * HD ** (-0.5)
                scores = dot(k_out[rows, lanes], query, 1, 1) + mask
                highest = jnp.max(scores, axis=0, keepdims=True)
                expo = jnp.exp(scores - highest)
                summed = jnp.sum(expo, axis=0, keepdims=True)
                probs = (expo * (1.0 / summed)).astype(BF16)
                both.append(dot(v_out[rows, lanes], probs, 0, 0))
                lse[0, s, pl.ds(head, 1), :] = highest + jnp.log(summed)
            both = jnp.concatenate(both, axis=0)
            ctx[rows, pl.ds(pair * 2 * HD, 2 * HD)] = both.T.astype(BF16)


def attend(counts, x, w_qkv, q_bias, v_bias, seqs, span):
    rows, width = x.shape
    group = 4
    cols = group * HD
    steps = width // cols
    piece = pl.BlockSpec((rows, cols), lambda g: (0, g))
    bias = line(cols, lambda g: (g,))
    weight = [pl.BlockSpec((width, cols), lambda g, k=k: (0, k * steps + g)) for k in range(3)]
    return pl.pallas_call(
        partial(attend_body, seqs, span, group),
        grid=(steps,),
        in_specs=[SMEM, fixed((rows, width)), *weight, bias, bias],
        out_specs=[piece] * 4 + [pl.BlockSpec((1, seqs, group, span), lambda g: (g, 0, 0, 0))],
        out_shape=[shape((rows, width), BF16)] * 4 + [shape((steps, seqs, group, span), F32)],
        compiler_params=params(),
        cost_estimate=LIGHT,
        name="attend",
    )(counts, x, w_qkv, w_qkv, w_qkv, q_bias, v_bias)


def norm_parts(value):
    centre = value - jnp.mean(value, axis=-1, keepdims=True)
    spread = jnp.mean(centre * centre, axis=-1, keepdims=True)
    scale = lax.rsqrt(spread + NORM_EPS)
    return centre * scale, scale


def gelu_parts(u):
    a = jnp.abs(u)
    t = 1.0 / (1.0 + (0.3275911 * ROOT_HALF) * a)
    poly = t * (0.254829592 + t * (-0.284496736 + t * (1.421413741 + t * (-1.453152027 + t * 1.061405429))))
    bell = jnp.exp(-0.5 * (u * u))
    tail = (0.5 * poly) * bell
    cdf = jnp.where(u >= 0.0, 1.0 - tail, tail)
    return u * cdf, cdf + u * (INV_ROOT_2PI * bell)


def feed_body(tile, span, chunk, counts, x, ctx, w_out, w_up, w_down, ob, g1, b1, ub, db,
              hid_t, hat1, sc1, act, slope, hat2, sc2, sums):
    step = pl.program_id(0)
    attn = dot(ctx[...], w_out[...]) + row(ob)
    xhat, scale = norm_parts(x[...].astype(F32) + attn)
    hat1[...] = xhat
    sc1[...] = scale
    hidden = xhat * row(g1) + row(b1)
    low = hidden.astype(BF16)
    hid_t[...] = low.T
    total = hidden + row(db)
    for j in range(w_up.shape[1] // chunk):
        cols = pl.ds(j * chunk, chunk)
        upper = dot(low, w_up[:, cols]) + ub[cols].reshape(1, chunk)
        active, grad = gelu_parts(upper)
        active = active.astype(BF16)
        act[:, cols] = active
        slope[:, cols] = grad.astype(slope.dtype)
        total = total + dot(active, w_down[cols, :])
    xhat, scale = norm_parts(total)
    hat2[...] = xhat
    sc2[...] = scale
    seq = step * tile // span
    place = lax.broadcasted_iota(jnp.int32, (tile, 1), 0) + lax.rem(step * tile, span)
    part = jnp.sum(jnp.where(place < counts[0, seq], xhat, 0.0), axis=0, keepdims=True)

    @pl.when(step == 0)
    def _():
        sums[...] = jnp.zeros_like(sums)

    sums[pl.ds(seq, 1), :] += part


def feed(counts, x, ctx, w_out, w_up, w_down, ob, g1, b1, ub, db, seqs, span, slope_kind):
    rows, width = x.shape
    ff = w_up.shape[1]
    tile = 256
    by = lambda cols: pl.BlockSpec((tile, cols), lambda i: (i, 0))
    return pl.pallas_call(
        partial(feed_body, tile, span, 768),
        grid=(rows // tile,),
        in_specs=[SMEM, by(width), by(width), fixed((width, width)), fixed((width, ff)), fixed((ff, width)),
                  line(width), line(width), line(width), line(ff), line(width)],
        out_specs=[pl.BlockSpec((width, tile), lambda i: (0, i)), by(width), by(1), by(ff), by(ff), by(width), by(1),
                   pl.BlockSpec((seqs, width), lambda i: (0, 0))],
        out_shape=[shape((width, rows), BF16), shape((rows, width), F32), shape((rows, 1), F32),
                   shape((rows, ff), BF16), shape((rows, ff), slope_kind), shape((rows, width), F32),
                   shape((rows, 1), F32), shape((seqs, width), F32)],
        compiler_params=params(),
        cost_estimate=LIGHT,
        name="feed",
    )(counts, x, ctx, w_out, w_up, w_down, ob, g1, b1, ub, db)


def loss_body(n_dp, towers, seqs, span, bits, counts, own, pos, every, sums, g2, hat2, sc2,
              loss, dres, ddown, small, scratch):
    count = n_dp * towers * seqs
    pairs = pos.shape[0]
    rows = every[...]
    inv = lax.rsqrt(jnp.sum(rows * rows, axis=-1, keepdims=True) + NORM_EPS)
    unit = rows * inv
    full = lax.Precision.HIGHEST
    logits = lax.dot_general(unit, unit, (((1,), (1,)), ((), ())), precision=full,
                             preferred_element_type=F32) / SOFTMAX_TEMP

    def place(i):
        block, j = i // seqs, lax.rem(i, seqs)
        device = jnp.full_like(block, own[0, 0])
        for n, bit in enumerate(bits):
            device = device ^ (((block >> n) & 1) * bit)
        dp, tower = device // towers, lax.rem(device, towers)
        half = towers // 2
        return tower < half, lax.rem(tower, half) * (n_dp * seqs) + dp * seqs + j

    is_query, query = place(lax.broadcasted_iota(jnp.int32, (count, 1), 0))
    key_is_query, key = place(lax.broadcasted_iota(jnp.int32, (1, count), 1))
    is_key = jnp.logical_not(key_is_query)
    lookup = lax.broadcasted_iota(jnp.int32, (count, pairs), 1) == query
    wanted = jnp.sum(jnp.where(lookup, row(pos).astype(F32), 0.0), axis=1, keepdims=True)
    hit = (key.astype(F32) == wanted) & is_key & is_query
    inside = is_key & is_query
    shown = jnp.where(is_key, logits, MASKED)
    highest = jnp.max(shown, axis=1, keepdims=True)
    expo = jnp.where(inside, jnp.exp(shown - highest), 0.0)
    summed = jnp.sum(expo, axis=1, keepdims=True)
    safe = jnp.where(is_query, summed, 1.0)
    picked = jnp.sum(jnp.where(hit, logits, 0.0), axis=1, keepdims=True)
    each = jnp.where(is_query, highest + jnp.log(safe) - picked, 0.0)
    loss[...] = jnp.sum(each, axis=0, keepdims=True) / pairs
    grad = (expo / safe - jnp.where(hit, 1.0, 0.0)) / (pairs * SOFTMAX_TEMP)
    dunit = lax.dot_general(grad, unit, (((1,), (0,)), ((), ())), precision=full, preferred_element_type=F32)
    dunit += lax.dot_general(grad, unit, (((0,), (0,)), ((), ())), precision=full, preferred_element_type=F32)
    inner = jnp.sum(dunit * rows, axis=-1, keepdims=True)
    scratch[...] = inv * dunit - rows * (inv * inv * inv * inner)

    width = rows.shape[1]
    small[...] = jnp.zeros_like(small)
    for s in range(seqs):
        pooled = scratch[pl.ds(s, 1), :]
        n = counts[0, s]
        dout = pooled / n.astype(F32)
        small[0:1, :] += dout * sums[s:s + 1, :]
        small[1:2, :] += pooled
        dhat = dout * row(g2)
        first = jnp.mean(dhat, axis=-1, keepdims=True)
        total = jnp.zeros((1, width), F32)
        tile = span // 2
        for part in range(2):
            at = pl.ds(s * span + part * tile, tile)
            xhat = hat2[at, :]
            second = jnp.mean(dhat * xhat, axis=-1, keepdims=True)
            live = lax.broadcasted_iota(jnp.int32, (tile, 1), 0) + part * tile < n
            scale = jnp.where(live, sc2[at, :], 0.0)
            value = scale * (dhat - first - xhat * second)
            dres[at, :] = value
            low = value.astype(BF16)
            ddown[at, :] = low
            total += jnp.sum(low.astype(F32), axis=0, keepdims=True)
        small[2:3, :] += total


def loss_step(counts, own, pos, every, sums, g2, hat2, sc2, n_dp, towers, seqs, span, bits):
    rows, width = hat2.shape
    return pl.pallas_call(
        partial(loss_body, n_dp, towers, seqs, span, bits),
        in_specs=[SMEM, SMEM] + [VMEM] * 6,
        out_specs=[VMEM] * 4,
        out_shape=[shape((1, 1), F32), shape((rows, width), F32), shape((rows, width), BF16), shape((8, width), F32)],
        scratch_shapes=[pltpu.VMEM(every.shape, F32)],
        compiler_params=params(),
        cost_estimate=LIGHT,
        name="loss",
    )(counts, own, pos, every, sums, g2, hat2, sc2)


def slope_body(ddown, slope, w_down, dupper, upb):
    value = (slope[...].astype(F32) * dot(ddown[...], w_down[...], 1, 1)).astype(BF16)
    dupper[...] = value
    upb[...] = jnp.sum(value.astype(F32), axis=0, keepdims=True)


def slope_back(ddown, slope, w_down, dep):
    rows, width = ddown.shape
    ff = slope.shape[1]
    tile = 512
    by = pl.BlockSpec((rows, tile), lambda i: (0, i))
    return call(
        slope_body, dep, (ff // tile,), [fixed((rows, width)), by, pl.BlockSpec((tile, width), lambda i: (i, 0))],
        [by, pl.BlockSpec((1, tile), lambda i: (0, i))], [shape((rows, ff), BF16), shape((1, ff), F32)],
        name="slope_back",
    )(ddown, slope, w_down)


def share(value, j, place, send, keep):
    rows = value.shape[0]

    @pl.when(place[j] < 2)
    def _():
        send[pl.ds(pl.multiple_of(place[j] * rows, rows), rows), :] = value

    @pl.when(place[j] >= 2)
    def _():
        keep[pl.ds(pl.multiple_of((place[j] - 2) * rows, rows), rows), :] = value


def up_send_body(which, a0, a1, a2, a3, b, out):
    out[...] = dot(jnp.concatenate([a0[...], a1[...], a2[...], a3[...]], axis=0), b[...])


def up_keep_body(which, place, a0, a1, a2, a3, b, came, send, keep):
    value = dot(jnp.concatenate([a0[...], a1[...], a2[...], a3[...]], axis=0), b[...])
    rows = a0.shape[0]
    for j in range(4):
        at = pl.ds(j * rows, rows)
        share(value[j * rows:(j + 1) * rows] + came[at, :], j, place, send, keep)


def up_grad(which, a, b, place=None, came=None, dep=None):
    m, k = a.shape
    n = b.shape[1]
    rows, tile = m // 8, 512
    ins = [pl.BlockSpec((rows, k), lambda i, w, *_, j=j: (2 * j + w[0], 0)) for j in range(4)]
    ins.append(pl.BlockSpec((k, tile), lambda i, *_: (0, i)))
    by = lambda r: pl.BlockSpec((r, tile), lambda i, *_: (0, i))
    if came is None:
        return call(up_send_body, dep, (n // tile,), ins, by(m // 2), shape((m // 2, n), F32), scalars=1,
                    name="up_send")(which, a, a, a, a, b)
    return call(up_keep_body, dep, (n // tile,), ins + [by(m // 2)], [by(m // 4)] * 2,
                [shape((m // 4, n), F32)] * 2, scalars=2, name="up_keep")(which, place, a, a, a, a, b, came)


def down_send_body(which, a, b, out):
    out[...] = dot(a[...], b[...], 0, 0)


def down_keep_body(which, order, a, b, came, send, keep):
    value = dot(a[...], b[...], 0, 0) + came[...]
    step = pl.program_id(0)

    @pl.when(step < 2)
    def _():
        send[...] = value

    @pl.when(step >= 2)
    def _():
        keep[...] = value


def down_grad(which, a, b, order=None, came=None, dep=None):
    rows, m = a.shape
    n = b.shape[1]
    tile = m // 8
    block = (tile, n)
    if came is None:
        return call(down_send_body, dep, (4,),
                    [pl.BlockSpec((rows, tile), lambda i, w: (0, 2 * i + w[0])), fixed((rows, n))],
                    pl.BlockSpec(block, lambda i, w: (i, 0)), shape((m // 2, n), F32), scalars=1,
                    name="down_send")(which, a, b)
    return call(down_keep_body, dep, (4,),
                [pl.BlockSpec((rows, tile), lambda i, w, o: (0, 2 * o[i] + w[0])), fixed((rows, n)),
                 pl.BlockSpec(block, lambda i, w, o: (o[i], 0))],
                [pl.BlockSpec(block, lambda i, w, o: (jnp.minimum(i, 1), 0)),
                 pl.BlockSpec(block, lambda i, w, o: (jnp.maximum(i - 2, 0), 0))],
                [shape((m // 4, n), F32)] * 2, scalars=2, name="down_keep")(which, order, a, b, came)


MORE = 16


def last_products(x, ctx, dattn, parts):
    span = parts[0].shape[0]
    seqs = len(parts) // 3
    for kind in range(3):
        value = None
        for s in range(seqs):
            term = dot(x[pl.ds(s * span, span), :], parts[s * 3 + kind][...], 0, 0)
            value = term if value is None else value + term
        yield value
    yield dot(ctx[...], dattn[...], 0, 0)


def last_small(which, small, kind):
    if kind:
        return jnp.zeros(small.shape, F32)
    return jnp.where(which[0] == 0, small[...], 0.0)


def last_send_body(which, x, ctx, dattn, small, *rest):
    parts, out = rest[:-1], rest[-1]
    rows = x.shape[1]
    for kind, value in enumerate(last_products(x, ctx, dattn, parts)):
        at = kind * (rows + MORE)
        out[pl.ds(at, rows), :] = value
        out[pl.ds(at + rows, MORE), :] = last_small(which, small, kind)


def last_keep_body(which, place, x, ctx, dattn, small, came, *rest):
    parts, send, keep = rest[:-2], rest[-2], rest[-1]
    rows = x.shape[1]
    size = rows + MORE
    for kind, value in enumerate(last_products(x, ctx, dattn, parts)):
        at = kind * size
        value = value + came[pl.ds(at, rows), :]
        more = last_small(which, small, kind) + came[pl.ds(at + rows, MORE), :]

        def put(out, spot):
            start = pl.multiple_of(spot * size, 8)
            out[pl.ds(start, rows), :] = value
            out[pl.ds(pl.multiple_of(start + rows, 8), MORE), :] = more

        pl.when(place[kind] < 2)(lambda: put(send, place[kind]))
        pl.when(place[kind] >= 2)(lambda: put(keep, place[kind] - 2))


def last_grad(which, x, ctx, dattn, small, parts, place=None, came=None, dep=None):
    rows, width = x.shape
    half = width // 2
    size = half + MORE
    whole = lambda v: pl.BlockSpec(v.shape, lambda i, *_: (0, 0), pipeline_mode=pl.Buffered(1))
    part = pl.BlockSpec((rows, half), lambda i, w, *_: (0, w[0]), pipeline_mode=pl.Buffered(1))
    out = lambda r: pl.BlockSpec((r, width), lambda i, *_: (0, 0), pipeline_mode=pl.Buffered(1))
    ins = [part, part, whole(dattn), whole(small)]
    if came is None:
        return call(last_send_body, dep, (1,), ins + [whole(v) for v in parts], out(4 * size),
                    shape((4 * size, width), F32), scalars=1, name="last_send")(which, x, ctx, dattn, small, *parts)
    return call(last_keep_body, dep, (1,), ins + [whole(came)] + [whole(v) for v in parts], [out(2 * size)] * 2,
                [shape((2 * size, width), F32)] * 2, scalars=2, name="last_keep")(
                    which, place, x, ctx, dattn, small, came, *parts)


def middle_body(dupper, w_up, dres, hat1, sc1, g1, w_out, dres1, dattn, dctx, small):
    dhid = dres[...] + dot(dupper[...], w_up[...], 1, 1)
    xhat = hat1[...]

    @pl.when(pl.program_id(0) == 0)
    def _():
        small[...] = jnp.zeros_like(small)

    small[1:2, :] += jnp.sum(dhid * xhat, axis=0, keepdims=True)
    small[2:3, :] += jnp.sum(dhid, axis=0, keepdims=True)
    dhat = dhid * row(g1)
    first = jnp.mean(dhat, axis=-1, keepdims=True)
    second = jnp.mean(dhat * xhat, axis=-1, keepdims=True)
    value = sc1[...] * (dhat - first - xhat * second)
    dres1[...] = value
    low = value.astype(BF16)
    dattn[...] = low
    small[0:1, :] += jnp.sum(low.astype(F32), axis=0, keepdims=True)
    dctx[...] = dot(low, w_out[...], 1, 1).astype(BF16)


def middle_back(dupper, w_up, dres, hat1, sc1, g1, w_out, dep):
    rows, width = dres.shape
    ff = dupper.shape[1]
    tile = 256
    by = lambda cols: pl.BlockSpec((tile, cols), lambda i: (i, 0))
    return call(
        middle_body, dep, (rows // tile,),
        [by(ff), fixed((width, ff)), by(width), by(width), by(1), line(width), fixed((width, width))],
        [by(width), by(width), by(width),
         pl.BlockSpec((8, width), lambda i: (0, 0))],
        [shape((rows, width), F32), shape((rows, width), BF16), shape((rows, width), BF16),
         shape((8, width), F32)], name="middle_back",
    )(dupper, w_up, dres, hat1, sc1, g1, w_out)


def attend_back_body(seq, span, group, counts, q, k, v, dctx, lse, dep, dq, dk, dv, qsum, vsum):
    mask = key_mask(counts[0, seq], span)
    for pair in range(group // 2):
        turned, keys, values = [], [], []
        for half in range(2):
            head = pair * 2 + half
            lanes = pl.ds(head * HD, HD)
            query = q[:, lanes] * HD ** (-0.5)
            key = k[:, lanes]
            grad = dctx[:, lanes]
            scores = dot(key, query, 1, 1) + mask
            probs = jnp.exp(scores - lse[0, 0, pl.ds(head, 1), :])
            dprobs = dot(v[:, lanes], grad, 1, 1)
            values.append(dot(probs.astype(BF16), grad))
            inner = jnp.sum(probs * dprobs, axis=0, keepdims=True)
            dscores = (probs * (dprobs - inner)).astype(BF16)
            keys.append(dot(dscores, query))
            turned.append(dot(key, dscores, 0, 0))
        cols = pl.ds(pair * 2 * HD, 2 * HD)
        low = (jnp.concatenate(turned, axis=0).T * HD ** (-0.5)).astype(BF16)
        dq[:, cols] = low
        qsum[:, cols] = jnp.sum(low.astype(F32), axis=0, keepdims=True)
        dk[:, cols] = jnp.concatenate(keys, axis=1).astype(BF16)
        low = jnp.concatenate(values, axis=1).astype(BF16)
        dv[:, cols] = low
        vsum[:, cols] = jnp.sum(low.astype(F32), axis=0, keepdims=True)


def attend_back(seq, counts, q, k, v, dctx, lse, span, dep):
    width = q.shape[1]
    group = 4
    cols = group * HD
    piece = pl.BlockSpec((span, cols), lambda g: (seq, g))
    mine = pl.BlockSpec((span, cols), lambda g: (0, g))
    line = pl.BlockSpec((1, cols), lambda g: (0, g))
    return pl.pallas_call(
        partial(attend_back_body, seq, span, group),
        grid=(width // cols,),
        in_specs=[SMEM] + [piece] * 4 + [pl.BlockSpec((1, 1, group, span), lambda g: (g, seq, 0, 0)), ANY],
        out_specs=[mine] * 3 + [line] * 2,
        out_shape=[shape((span, width), BF16)] * 3 + [shape((1, width), F32)] * 2,
        compiler_params=params(),
        cost_estimate=LIGHT,
        name="attend_back",
    )(counts, q, k, v, dctx, lse, dep)


def token_body(steps, dres1, wq, wk, wv, dep, *rest):
    parts, out = rest[:-1], rest[-1]
    for s in range(len(parts) // 3):
        at = pl.ds(s * parts[0].shape[0], parts[0].shape[0])
        total = dres1[at, :]
        for part, weight in zip(parts[s * 3:s * 3 + 3], (wq, wk, wv)):
            total = total + dot(part[...], weight[...], 1, 1)
        out[at, :] = total


def token_grad(dres1, w_qkv, parts, dep):
    rows, width = dres1.shape
    span = parts[0].shape[0]
    full = pl.BlockSpec((span, width), lambda i: (0, 0), pipeline_mode=pl.Buffered(1))
    tile = 256
    steps = width // tile
    by = pl.BlockSpec((rows, tile), lambda i: (0, i))
    weight = [pl.BlockSpec((tile, width), lambda i, k=k: (i, k)) for k in range(3)]
    return pl.pallas_call(
        partial(token_body, steps),
        grid=(steps,),
        in_specs=[by, *weight, ANY] + [full] * len(parts),
        out_specs=by,
        out_shape=shape((rows, width), F32),
        compiler_params=params(),
        cost_estimate=LIGHT,
        name="token_grad",
    )(dres1, w_qkv, w_qkv, w_qkv, dep, *parts)


def add_split_body(steps, bit, held, came, send, keep):
    step = pl.program_id(0)
    value = held[...] + came[...]

    @pl.when(step < steps)
    def _():
        send[...] = value

    @pl.when(step >= steps)
    def _():
        keep[...] = value


def block_rows(rows, cols):
    best = 8
    for r in range(8, rows + 1, 8):
        if rows % r == 0 and r * cols * 4 <= MIB:
            best = r
    return best


def add_split(bit, held, came, dep=None):
    rows, cols = held.shape
    half = rows // 2
    tile = block_rows(half, cols)
    steps = half // tile

    def at(i, b):
        first = i < steps
        return jnp.where(first, (1 - b[0]) * steps + i, b[0] * steps + i - steps), 0

    block = (tile, cols)
    return call(
        partial(add_split_body, steps), dep, (2 * steps,), [pl.BlockSpec(block, at)] * 2,
        [pl.BlockSpec(block, lambda i, b: (jnp.minimum(i, steps - 1), 0)),
         pl.BlockSpec(block, lambda i, b: (jnp.maximum(i - steps, 0), 0))],
        [shape((half, cols), F32)] * 2, scalars=1, name="add_split",
    )(bit, held, came)


def add_body(held, came, out):
    out[...] = held[...] + came[...]


def add(held, came, dep=None):
    rows, cols = held.shape
    tile = block_rows(rows, cols)
    spec = pl.BlockSpec((tile, cols), lambda i: (i, 0))
    return call(add_body, dep, (rows // tile,), [spec] * 2, spec, shape((rows, cols), F32), name="add")(held, came)


def gather_body(n, targets, earlier, places, *refs):
    pieces, outs, (held, in_sems, out_sems) = refs[:n], refs[n + earlier:-3], refs[-3:]
    rows = pieces[0].shape[0]
    reads = [pltpu.make_async_copy(piece, held.at[i], in_sems.at[i]) for i, piece in enumerate(pieces)]
    for copy in reads:
        copy.start()

    def each(i, act):
        for kind, first, height, out, column in targets:
            if kind is None:
                at = places[i] * height
            elif kind < 0:
                at = 0
            else:
                at = lax.rem(places[i], 2) * height
            cols = held.shape[2]
            copy = pltpu.make_async_copy(
                held.at[i, pl.ds(first, height), :],
                outs[out].at[pl.ds(pl.multiple_of(at, 8), height), pl.ds(column, cols)],
                out_sems.at[i, 1 if kind is not None and kind < 0 else 0])
            if kind is None:
                act(copy)
            elif kind < 0:
                pl.when(places[i] == 0)(partial(act, copy))
            else:
                pl.when(places[i] // 2 == kind)(partial(act, copy))

    for i in range(n):
        reads[i].wait()
        each(i, lambda copy: copy.start())
    for i in range(n):
        each(i, lambda copy: copy.wait())


def gather(places, pieces, outs, targets, dep=None, into=()):
    n = len(pieces)
    rows, cols = pieces[0].shape
    ins = [SMEM] + [ANY] * (n + len(into))
    body = partial(gather_body, n, targets, len(into))
    n_in = len(ins)

    def run(*refs):
        return body(*refs) if dep is None else body(*refs[:n_in], *refs[n_in + 1:])

    return pl.pallas_call(
        run, in_specs=ins + ([] if dep is None else [ANY]), out_specs=[ANY] * len(outs), out_shape=outs,
        scratch_shapes=[pltpu.VMEM((n, rows, cols), F32), pltpu.SemaphoreType.DMA((n,)),
                        pltpu.SemaphoreType.DMA((n, 2))],
        input_output_aliases={1 + n + k: k for k in range(len(into))},
        compiler_params=params(), cost_estimate=LIGHT, name="gather",
    )(places, *pieces, *into, *([] if dep is None else [dep]))


class Ring:
    def __init__(self, n_dp, towers):
        self.n_dp, self.towers = n_dp, towers
        self.dp, self.tower = lax.axis_index("dp").astype(jnp.int32), lax.axis_index("tower").astype(jnp.int32)
        self.core = self.tower & 1
        x, y = self.x, self.y = self.dp & 1, (self.tower >> 1) & 1
        self.outer = jnp.where(self.core == 0, x, y)
        self.inner = jnp.where(self.core == 0, y, x)
        self.near = (self.dp >> 1) & 1
        self.far = [b for b in (4, 8, 16, 32, 64) if b < n_dp]

    def move(self, value, partner):
        pairs = []
        for dp in range(self.n_dp):
            for tower in range(self.towers):
                to_dp, to_tower = partner(dp, tower)
                pairs.append((dp * self.towers + tower, to_dp * self.towers + to_tower))
        return lax.ppermute(value, ("dp", "tower"), pairs)

    def place(self):
        out = []
        for bx in range(2):
            for by in range(2):
                outer, inner = jnp.where(self.core == 0, bx, by), jnp.where(self.core == 0, by, bx)
                out.append(jnp.where(outer == self.outer, 2, 0) + inner)
        return jnp.stack(out).astype(jnp.int32)

    def order(self):
        out = []
        for outer in (1 - self.outer, self.outer):
            for inner in range(2):
                out.append(jnp.where(self.core == 0, outer * 2 + inner, inner * 2 + outer))
        return jnp.stack(out).astype(jnp.int32)

    def bits(self):
        bits = [1]
        while bits[0] * 2 < self.n_dp * self.towers:
            bits.insert(0, bits[0] * 2)
        return bits

    def to_index(self, value, bit):
        count = self.n_dp * self.towers
        return lax.ppermute(value, ("dp", "tower"), [(i, i ^ bit) for i in range(count)])

    def to_core(self, value):
        return self.move(value, lambda d, t: (d, t ^ 1))

    def to_outer(self, value):
        return self.move(value, lambda d, t: (d, t ^ 2) if t & 1 else (d ^ 1, t))

    def to_inner(self, value):
        return self.move(value, lambda d, t: (d ^ 1, t) if t & 1 else (d, t ^ 2))

    def to_dp(self, value, bit):
        return self.move(value, lambda d, t: (d ^ bit, t))


class Sum:
    def __init__(self, ring, send):
        self.ring = ring
        self.came = ring.to_core(send)

    def s1(self, send, keep):
        self.keep = keep
        self.came = self.ring.to_outer(send)
        return keep

    def s2(self, dep):
        send, self.keep = add_split(self.ring.inner.reshape(1), self.keep, self.came, dep)
        self.came = self.ring.to_inner(send)
        return self.keep

    def s3(self, dep):
        send, self.keep = add_split(self.ring.near.reshape(1), self.keep, self.came, dep)
        self.came = self.ring.to_dp(send, 2)
        return self.keep

    def s4(self, dep):
        self.keep = add(self.keep, self.came, dep)
        for bit in self.ring.far[:-1]:
            self.keep = self.keep + self.ring.to_dp(self.keep, bit)
        self.came = self.ring.to_dp(self.keep, self.ring.far[-1])
        return self.keep

    def s5(self, dep):
        self.keep = add(self.keep, self.came, dep)
        self.came = self.ring.to_dp(self.keep, 2)
        return self.keep

    def s6(self, dep):
        ring = self.ring
        places = jnp.stack([ring.near, 1 - ring.near])
        rows, cols = self.keep.shape
        targets = [(None, 0, rows, 0, 0)]
        (own,) = gather(places, [self.keep, self.came], [shape((2 * rows, cols), F32)], targets, dep)
        self.pieces = [own, ring.to_inner(own), ring.to_outer(own)]
        return own

    def s7(self, outs, targets, dep, into=()):
        ring = self.ring
        own, inner, outer = self.pieces
        mine = [own, inner, outer, ring.to_outer(inner)]
        pieces = mine + [ring.to_core(v) for v in mine]
        c = ring.core
        places = []
        for core in (c, 1 - c):
            inner_step = jnp.where(core == 0, 2, 4)
            base = ring.x * 4 + ring.y * 2
            places += [(base ^ step) + core for step in (0 * inner_step, inner_step, 6 - inner_step, 6 + 0 * inner_step)]
        return gather(jnp.stack(places), pieces, outs, targets, dep, into)


def local(n_dp, towers, tokens, lengths, positive, w_qkv, q_bias, v_bias, w_out, out_bias, norm1_gain, norm1_bias,
          w_up, up_bias, w_down, down_bias, norm2_gain, norm2_bias):
    seqs, span, width = tokens.shape[1:]
    ff = up_bias.shape[0]
    x = tokens.reshape(seqs * span, width)
    ring = Ring(n_dp, towers)
    mine, other = ring.core.reshape(1), (1 - ring.core).reshape(1)
    place = ring.place()
    q, k, v, ctx, lse = attend(lengths, x, w_qkv, q_bias, v_bias, seqs, span)
    hid_t, hat1, sc1, act, slope, hat2, sc2, sums = feed(
        lengths, x, ctx, w_out, w_up, w_down, out_bias, norm1_gain, norm1_bias, up_bias, down_bias, seqs, span, F32)
    pooled = sums * norm2_gain / lengths[0][:, None].astype(F32) + norm2_bias
    every, bits = pooled, ring.bits()
    for bit in bits:
        every = jnp.concatenate([every, ring.to_index(every, bit)], axis=0)
    own = (lax.axis_index("dp") * towers + lax.axis_index("tower")).astype(jnp.int32).reshape(1, 1)
    loss, dres, ddown, small2 = loss_step(lengths, own, positive, every, sums, norm2_gain, hat2, sc2,
                                          n_dp, towers, seqs, span, bits)
    send = down_grad(other, act, ddown)
    down = Sum(ring, send)
    dupper, upb = slope_back(ddown, slope, w_down, send)
    send, keep = down_grad(mine, act, ddown, ring.order(), down.came, dupper)
    dep = down.s1(send, keep)
    send = up_grad(other, hid_t, dupper, dep=dep)
    up = Sum(ring, send)
    dres1, dattn, dctx, small1 = middle_back(dupper, w_up, dres, hat1, sc1, norm1_gain, w_out, send)
    dep = down.s2(dattn)
    send, keep = up_grad(mine, hid_t, dupper, place, up.came, dep)
    dep = up.s1(send, keep)
    back0 = attend_back(0, lengths, q, k, v, dctx, lse, span, dep)
    dep = down.s3(back0[0])
    back1 = attend_back(1, lengths, q, k, v, dctx, lse, span, dep)
    dep = down.s4(back1[0])
    dep = up.s2(dep)
    parts = list(back0[:3] + back1[:3])
    smalls = jnp.concatenate([back0[3] + back1[3], back0[4] + back1[4], small1[:3], upb.reshape(-1, width), small2[:3]], axis=0)
    lines = smalls.shape[0]
    smalls = jnp.pad(smalls, ((0, MORE - lines), (0, 0)))
    send = last_grad(other, x, ctx, dattn, smalls, parts, dep=dep)
    last = Sum(ring, send)
    dep = up.s3(send)
    grad_tokens = token_grad(dres1, w_qkv, parts, dep)
    dep = down.s5(grad_tokens)
    send, keep = last_grad(mine, x, ctx, dattn, smalls, parts, place, last.came, dep)
    dep = last.s1(send, keep)
    dep = up.s4(dep)
    dep = down.s6(dep)
    dep = up.s5(dep)
    dep = last.s2(dep)
    dep = up.s6(dep)
    dep = last.s3(dep)
    dep = last.s4(dep)
    rows = width // 2
    (g1,) = down.s7([shape((ff, width), F32)], [(None, 0, ff // 8, 0, 0)], dep)
    dep = last.s5(g1)
    (g2,) = up.s7([shape((width, ff), F32)], [(None, 0, width // 8, 0, 0)], dep)
    dep = last.s6(g2)
    qkv, out, tail = last.s7(
        [shape((width, 3 * width), F32), shape((width, width), F32), shape((MORE, width), F32)],
        [(0, 0, rows, 0, 0), (1, 0, rows, 0, width), (2, 0, rows, 0, 2 * width), (3, 0, rows, 1, 0), (-1, rows, MORE, 2, 0)],
        dep)
    return outputs(loss, grad_tokens.reshape(tokens.shape), g1, g2, qkv, out, tail[:lines], width)


def outputs(loss, grad_tokens, down, up, qkv, out, smalls, width):
    lines = smalls.reshape(-1, width)
    n = up.shape[1] // width
    return (loss[0, 0], grad_tokens, qkv, lines[0], lines[1], out, lines[2], lines[3], lines[4], up,
            lines[5:5 + n].reshape(-1), down, lines[7 + n], lines[5 + n], lines[6 + n])


def solution(mesh):
    split = P("tower", "dp", None, None)
    in_specs = (split, P("tower", "dp")) + (P(),) * 14
    out_specs = (P(), split) + (P(),) * 13
    body = partial(local, mesh.shape["dp"], mesh.shape["tower"])
    return jax.shard_map(body, mesh=mesh, in_specs=in_specs, out_specs=out_specs, check_vma=False)
```

```python
from functools import partial

import jax
import jax.numpy as jnp
from jax import lax
from jax.experimental import pallas as pl
from jax.experimental.pallas import tpu as pltpu
from jax.sharding import PartitionSpec as P

HD = 64
SOFTMAX_TEMP = 0.01
NORM_EPS = 1e-06
MASKED = -1e30
F32 = jnp.float32
BF16 = jnp.bfloat16
ROOT_HALF = 0.7071067811865476
INV_ROOT_2PI = 0.3989422804014327
MIB = 1024 * 1024

SMEM = pl.BlockSpec(memory_space=pltpu.SMEM)
VMEM = pl.BlockSpec(memory_space=pltpu.VMEM)
ANY = pl.BlockSpec(memory_space=pl.ANY)


SCALE = 6.0
MICROSECONDS = {"down_send": 7, "down_keep": 9, "slope_back": 13, "up_send": 8, "up_keep": 10, "middle_back": 16,
                "attend_back": 12, "last_send": 8, "last_keep": 12, "token_grad": 9, "add_split": 4, "add": 2,
                "gather": 5}


def cost(name):
    return pl.CostEstimate(flops=max(1, int(1.1e9 * SCALE * MICROSECONDS.get(name, 1))), bytes_accessed=1, transcendentals=0)


def params():
    return pltpu.CompilerParams(vmem_limit_bytes=62 * MIB)


def call(body, dep, grid, in_specs, out_specs, out_shape, scratch=(), scalars=0, name=None, aliases=None):
    dep = [] if dep is None else list(dep)
    n_in = scalars + len(in_specs)

    def run(*refs):
        return body(*refs[:n_in], *refs[n_in + len(dep):])

    spec = pltpu.PrefetchScalarGridSpec(
        num_scalar_prefetch=scalars, grid=grid, in_specs=list(in_specs) + [ANY] * len(dep),
        out_specs=out_specs, scratch_shapes=scratch)
    made = pl.pallas_call(run, grid_spec=spec, out_shape=out_shape, compiler_params=params(), cost_estimate=cost(name),
                          input_output_aliases=aliases or {}, name=name)
    return lambda *args: made(*args, *dep)


def shape(dims, kind):
    return jax.ShapeDtypeStruct(dims, kind)


def line(cols, index=lambda *_: (0,)):
    return pl.BlockSpec((cols,), index)


def row(ref):
    return ref[...].reshape(1, -1)


def fixed(dims):
    return pl.BlockSpec(dims, lambda *_: (0,) * len(dims), pipeline_mode=pl.Buffered(1))


def dot(a, b, ca=1, cb=0):
    return lax.dot_general(a, b, (((ca,), (cb,)), ((), ())), preferred_element_type=F32)


def key_mask(count, span):
    place = lax.broadcasted_iota(jnp.int32, (span, 1), 0)
    return jnp.where(place < count, 0.0, MASKED)


def attend_body(seqs, span, group, counts, x, wq, wk, wv, qb, vb, q_out, k_out, v_out, ctx, lse):
    q_out[...] = (dot(x[...], wq[...]) + row(qb)).astype(BF16)
    k_out[...] = dot(x[...], wk[...]).astype(BF16)
    v_out[...] = (dot(x[...], wv[...]) + row(vb)).astype(BF16)
    for s in range(seqs):
        rows = pl.ds(s * span, span)
        mask = key_mask(counts[0, s], span)
        for pair in range(group // 2):
            both = []
            for half in range(2):
                head = pair * 2 + half
                lanes = pl.ds(head * HD, HD)
                query = q_out[rows, lanes] * HD ** (-0.5)
                scores = dot(k_out[rows, lanes], query, 1, 1) + mask
                highest = jnp.max(scores, axis=0, keepdims=True)
                expo = jnp.exp(scores - highest)
                summed = jnp.sum(expo, axis=0, keepdims=True)
                probs = (expo * (1.0 / summed)).astype(BF16)
                both.append(dot(v_out[rows, lanes], probs, 0, 0))
                lse[0, s, pl.ds(head, 1), :] = highest + jnp.log(summed)
            both = jnp.concatenate(both, axis=0)
            ctx[rows, pl.ds(pair * 2 * HD, 2 * HD)] = both.T.astype(BF16)


def attend(counts, x, w_qkv, q_bias, v_bias, seqs, span):
    rows, width = x.shape
    group = 4
    cols = group * HD
    steps = width // cols
    piece = pl.BlockSpec((rows, cols), lambda g: (0, g))
    bias = line(cols, lambda g: (g,))
    weight = [pl.BlockSpec((width, cols), lambda g, k=k: (0, k * steps + g)) for k in range(3)]
    return pl.pallas_call(
        partial(attend_body, seqs, span, group),
        grid=(steps,),
        in_specs=[SMEM, fixed((rows, width)), *weight, bias, bias],
        out_specs=[piece] * 4 + [pl.BlockSpec((1, seqs, group, span), lambda g: (g, 0, 0, 0))],
        out_shape=[shape((rows, width), BF16)] * 4 + [shape((steps, seqs, group, span), F32)],
        compiler_params=params(),
        cost_estimate=cost(""),
        name="attend",
    )(counts, x, w_qkv, w_qkv, w_qkv, q_bias, v_bias)


def norm_parts(value):
    centre = value - jnp.mean(value, axis=-1, keepdims=True)
    spread = jnp.mean(centre * centre, axis=-1, keepdims=True)
    scale = lax.rsqrt(spread + NORM_EPS)
    return centre * scale, scale


def gelu_parts(u):
    bell = jnp.exp(-0.5 * (u * u))
    cdf = 0.5 + 0.5 * lax.erf(u * ROOT_HALF)
    return u * cdf, cdf + u * (INV_ROOT_2PI * bell)


def feed_body(tile, span, chunk, counts, x, ctx, w_out, w_up, w_down, ob, g1, b1, ub, db,
              hid_t, hat1, sc1, act, slope, hat2, sc2, sums):
    step = pl.program_id(0)
    attn = dot(ctx[...], w_out[...]) + row(ob)
    xhat, scale = norm_parts(x[...].astype(F32) + attn)
    hat1[...] = xhat
    sc1[...] = scale
    hidden = xhat * row(g1) + row(b1)
    low = hidden.astype(BF16)
    hid_t[...] = low.T
    total = hidden + row(db)
    for j in range(w_up.shape[1] // chunk):
        cols = pl.ds(j * chunk, chunk)
        upper = dot(low, w_up[:, cols]) + ub[cols].reshape(1, chunk)
        active, grad = gelu_parts(upper)
        active = active.astype(BF16)
        act[:, cols] = active
        slope[:, cols] = grad.astype(slope.dtype)
        total = total + dot(active, w_down[cols, :])
    xhat, scale = norm_parts(total)
    hat2[...] = xhat
    sc2[...] = scale
    seq = step * tile // span
    place = lax.broadcasted_iota(jnp.int32, (tile, 1), 0) + lax.rem(step * tile, span)
    part = jnp.sum(jnp.where(place < counts[0, seq], xhat, 0.0), axis=0, keepdims=True)

    @pl.when(step == 0)
    def _():
        sums[...] = jnp.zeros_like(sums)

    sums[pl.ds(seq, 1), :] += part


def feed(counts, x, ctx, w_out, w_up, w_down, ob, g1, b1, ub, db, seqs, span, slope_kind):
    rows, width = x.shape
    ff = w_up.shape[1]
    tile = 256
    by = lambda cols: pl.BlockSpec((tile, cols), lambda i: (i, 0))
    return pl.pallas_call(
        partial(feed_body, tile, span, 768),
        grid=(rows // tile,),
        in_specs=[SMEM, by(width), by(width), fixed((width, width)), fixed((width, ff)), fixed((ff, width)),
                  line(width), line(width), line(width), line(ff), line(width)],
        out_specs=[pl.BlockSpec((width, tile), lambda i: (0, i)), by(width), by(1), by(ff), by(ff), by(width), by(1),
                   pl.BlockSpec((seqs, width), lambda i: (0, 0))],
        out_shape=[shape((width, rows), BF16), shape((rows, width), F32), shape((rows, 1), F32),
                   shape((rows, ff), BF16), shape((rows, ff), slope_kind), shape((rows, width), F32),
                   shape((rows, 1), F32), shape((seqs, width), F32)],
        compiler_params=params(),
        cost_estimate=cost(""),
        name="feed",
    )(counts, x, ctx, w_out, w_up, w_down, ob, g1, b1, ub, db)


def loss_body(n_dp, towers, seqs, span, bits, counts, own, pos, low, high, sums, g2, hat2, sc2,
              loss, dres, ddown, small, scratch):
    count = n_dp * towers * seqs
    pairs = pos.shape[0]
    rows = jnp.concatenate([low[...], high[...]], axis=0)
    inv = lax.rsqrt(jnp.sum(rows * rows, axis=-1, keepdims=True) + NORM_EPS)
    unit = rows * inv
    full = lax.Precision.HIGHEST
    logits = lax.dot_general(unit, unit, (((1,), (1,)), ((), ())), precision=full,
                             preferred_element_type=F32) / SOFTMAX_TEMP

    def place(i):
        block, j = i // seqs, lax.rem(i, seqs)
        device = jnp.full_like(block, own[0, 0])
        for n, bit in enumerate(bits):
            device = device ^ (((block >> n) & 1) * bit)
        dp, tower = device // towers, lax.rem(device, towers)
        half = towers // 2
        return tower < half, lax.rem(tower, half) * (n_dp * seqs) + dp * seqs + j

    is_query, query = place(lax.broadcasted_iota(jnp.int32, (count, 1), 0))
    key_is_query, key = place(lax.broadcasted_iota(jnp.int32, (1, count), 1))
    is_key = jnp.logical_not(key_is_query)
    lookup = lax.broadcasted_iota(jnp.int32, (count, pairs), 1) == query
    wanted = jnp.sum(jnp.where(lookup, row(pos).astype(F32), 0.0), axis=1, keepdims=True)
    hit = (key.astype(F32) == wanted) & is_key & is_query
    inside = is_key & is_query
    shown = jnp.where(is_key, logits, MASKED)
    highest = jnp.max(shown, axis=1, keepdims=True)
    expo = jnp.where(inside, jnp.exp(shown - highest), 0.0)
    summed = jnp.sum(expo, axis=1, keepdims=True)
    safe = jnp.where(is_query, summed, 1.0)
    picked = jnp.sum(jnp.where(hit, logits, 0.0), axis=1, keepdims=True)
    each = jnp.where(is_query, highest + jnp.log(safe) - picked, 0.0)
    loss[...] = jnp.sum(each, axis=0, keepdims=True) / pairs
    grad = (expo / safe - jnp.where(hit, 1.0, 0.0)) / (pairs * SOFTMAX_TEMP)
    dunit = lax.dot_general(grad, unit, (((1,), (0,)), ((), ())), precision=full, preferred_element_type=F32)
    dunit += lax.dot_general(grad, unit, (((0,), (0,)), ((), ())), precision=full, preferred_element_type=F32)
    inner = jnp.sum(dunit * rows, axis=-1, keepdims=True)
    scratch[...] = inv * dunit - rows * (inv * inv * inv * inner)

    width = rows.shape[1]
    small[...] = jnp.zeros_like(small)
    for s in range(seqs):
        pooled = scratch[pl.ds(s, 1), :]
        n = counts[0, s]
        dout = pooled / n.astype(F32)
        small[0:1, :] += dout * sums[s:s + 1, :]
        small[1:2, :] += pooled
        dhat = dout * row(g2)
        first = jnp.mean(dhat, axis=-1, keepdims=True)
        total = jnp.zeros((1, width), F32)
        tile = span // 2
        for part in range(2):
            at = pl.ds(s * span + part * tile, tile)
            xhat = hat2[at, :]
            second = jnp.mean(dhat * xhat, axis=-1, keepdims=True)
            live = lax.broadcasted_iota(jnp.int32, (tile, 1), 0) + part * tile < n
            scale = jnp.where(live, sc2[at, :], 0.0)
            value = scale * (dhat - first - xhat * second)
            dres[at, :] = value
            low = value.astype(BF16)
            ddown[at, :] = low
            total += jnp.sum(low.astype(F32), axis=0, keepdims=True)
        small[2:3, :] += total


def loss_step(counts, own, pos, low, high, sums, g2, hat2, sc2, n_dp, towers, seqs, span, bits):
    rows, width = hat2.shape
    return pl.pallas_call(
        partial(loss_body, n_dp, towers, seqs, span, bits),
        in_specs=[SMEM, SMEM] + [VMEM] * 7,
        out_specs=[VMEM] * 4,
        out_shape=[shape((1, 1), F32), shape((rows, width), F32), shape((rows, width), BF16), shape((8, width), F32)],
        scratch_shapes=[pltpu.VMEM((2 * low.shape[0], width), F32)],
        compiler_params=params(),
        cost_estimate=cost(""),
        name="loss",
    )(counts, own, pos, low, high, sums, g2, hat2, sc2)


def slope_body(ddown, slope, w_down, dupper, upb):
    value = (slope[...].astype(F32) * dot(ddown[...], w_down[...], 1, 1)).astype(BF16)
    dupper[...] = value
    upb[...] = jnp.sum(value.astype(F32), axis=0, keepdims=True)


def slope_back(ddown, slope, w_down, dep):
    rows, width = ddown.shape
    ff = slope.shape[1]
    tile = 768
    by = pl.BlockSpec((rows, tile), lambda i: (0, i))
    return call(
        slope_body, dep, (ff // tile,), [fixed((rows, width)), by, pl.BlockSpec((tile, width), lambda i: (i, 0))],
        [by, pl.BlockSpec((1, tile), lambda i: (0, i))], [shape((rows, ff), BF16), shape((1, ff), F32)],
        name="slope_back",
    )(ddown, slope, w_down)


def share(value, j, place, send, keep):
    rows = value.shape[0]

    @pl.when(place[j] < 2)
    def _():
        send[pl.ds(pl.multiple_of(place[j] * rows, rows), rows), :] = value

    @pl.when(place[j] >= 2)
    def _():
        keep[pl.ds(pl.multiple_of((place[j] - 2) * rows, rows), rows), :] = value


def up_send_body(which, a0, a1, a2, a3, b, *outs):
    value = dot(jnp.concatenate([a0[...], a1[...], a2[...], a3[...]], axis=0), b[...])
    rows = a0.shape[0]
    for j in range(4):
        outs[j][...] = value[j * rows:(j + 1) * rows]


def up_keep_body(which, place, a0, a1, a2, a3, b, *rest):
    came, (send, keep) = rest[:4], rest[4:]
    value = dot(jnp.concatenate([a0[...], a1[...], a2[...], a3[...]], axis=0), b[...])
    rows = a0.shape[0]
    for j in range(4):
        share(value[j * rows:(j + 1) * rows] + came[j][...], j, place, send, keep)


def up_grad(which, a, b, columns, place=None, came=None, dep=None):
    m, k = a.shape
    start, n = columns
    rows, tile = m // 8, 768
    ins = [pl.BlockSpec((rows, k), lambda i, w, *_, j=j: (2 * j + w[0], 0)) for j in range(4)]
    ins.append(pl.BlockSpec((k, tile), lambda i, *_: (0, i + start // tile)))
    by = lambda r: pl.BlockSpec((r, tile), lambda i, *_: (0, i))
    if came is None:
        return call(up_send_body, dep, (n // tile,), ins, [by(rows)] * 4, [shape((rows, n), F32)] * 4, scalars=1,
                    name="up_send")(which, a, a, a, a, b)
    return call(up_keep_body, dep, (n // tile,), ins + [by(rows)] * 4, [by(m // 4)] * 2,
                [shape((m // 4, n), F32)] * 2, scalars=2, name="up_keep")(which, place, a, a, a, a, b, *came)


def down_send_body(which, a, b, *outs):
    value = dot(a[...], b[...], 0, 0)
    for j, out in enumerate(outs):
        @pl.when(pl.program_id(0) == j)
        def _(out=out):
            out[...] = value


def down_keep_body(which, order, a, b, *rest):
    came, (send, keep) = rest[:4], rest[4:]
    step = pl.program_id(0)
    out = dot(a[...], b[...], 0, 0)
    for j, one in enumerate(came):
        @pl.when((order[step] == j) & (step < 2))
        def _(one=one):
            send[...] = out + one[...]

        @pl.when((order[step] == j) & (step >= 2))
        def _(one=one):
            keep[...] = out + one[...]


def down_grad(which, a, b, order=None, came=None, dep=None):
    rows, m = a.shape
    n = b.shape[1]
    tile = m // 8
    block = (tile, n)
    if came is None:
        return call(down_send_body, dep, (4,),
                    [pl.BlockSpec((rows, tile), lambda i, w: (0, 2 * i + w[0])), fixed((rows, n))],
                    [pl.BlockSpec(block, lambda i, w: (0, 0))] * 4, [shape(block, F32)] * 4, scalars=1,
                    name="down_send")(which, a, b)
    return call(down_keep_body, dep, (4,),
                [pl.BlockSpec((rows, tile), lambda i, w, o: (0, 2 * o[i] + w[0])), fixed((rows, n))] + [fixed(block)] * 4,
                [pl.BlockSpec(block, lambda i, w, o: (jnp.minimum(i, 1), 0)),
                 pl.BlockSpec(block, lambda i, w, o: (jnp.maximum(i - 2, 0), 0))],
                [shape((m // 4, n), F32)] * 2, scalars=2, name="down_keep")(which, order, a, b, *came)


MORE = 16


def last_products(x, ctx, dattn, parts):
    span = parts[0].shape[0]
    seqs = len(parts) // 3
    for kind in range(3):
        value = None
        for s in range(seqs):
            term = dot(x[pl.ds(s * span, span), :], parts[s * 3 + kind][...], 0, 0)
            value = term if value is None else value + term
        yield value
    yield dot(ctx[...], dattn[...], 0, 0)


def last_small(which, smalls, kind):
    width = smalls[-1].shape[1]
    if kind:
        return jnp.zeros((MORE, width), F32)
    small1, upb, small2 = (v[...] for v in smalls[-3:])
    sums = [v[...] for v in smalls[:-3]]
    seqs = len(sums) // 2
    lines = [sum(sums[:seqs]), sum(sums[seqs:]), small1[:3]]
    lines += [upb[:, i:i + width] for i in range(0, upb.shape[1], width)] + [small2[:3]]
    lines = jnp.concatenate(lines, axis=0)
    lines = jnp.concatenate([lines, jnp.zeros((MORE - lines.shape[0], width), F32)], axis=0)
    return jnp.where(which[0] == 0, lines, 0.0)


def last_send_body(seqs, which, x, ctx, dattn, *rest):
    outs, smalls, parts = rest[-4:], rest[:2 * seqs + 3], rest[2 * seqs + 3:-4]
    rows = x.shape[1]
    for kind, value in enumerate(last_products(x, ctx, dattn, parts)):
        outs[kind][pl.ds(0, rows), :] = value
        outs[kind][pl.ds(rows, MORE), :] = last_small(which, smalls, kind)


def last_keep_body(seqs, which, place, x, ctx, dattn, *rest):
    send, keep = rest[-2:]
    smalls, came, parts = rest[:2 * seqs + 3], rest[2 * seqs + 3:2 * seqs + 7], rest[2 * seqs + 7:-2]
    rows = x.shape[1]
    size = rows + MORE
    for kind, value in enumerate(last_products(x, ctx, dattn, parts)):
        value = value + came[kind][pl.ds(0, rows), :]
        more = last_small(which, smalls, kind) + came[kind][pl.ds(rows, MORE), :]

        def put(out, spot):
            start = pl.multiple_of(spot * size, 8)
            out[pl.ds(start, rows), :] = value
            out[pl.ds(pl.multiple_of(start + rows, 8), MORE), :] = more

        pl.when(place[kind] < 2)(lambda: put(send, place[kind]))
        pl.when(place[kind] >= 2)(lambda: put(keep, place[kind] - 2))


def last_grad(which, x, ctx, dattn, smalls, parts, place=None, came=None, dep=None):
    rows, width = x.shape
    half = width // 2
    size = half + MORE
    seqs = len(parts) // 3
    whole = lambda v: pl.BlockSpec(v.shape, lambda i, *_: (0, 0), pipeline_mode=pl.Buffered(1))
    part = pl.BlockSpec((rows, half), lambda i, w, *_: (0, w[0]), pipeline_mode=pl.Buffered(1))
    out = lambda r: pl.BlockSpec((r, width), lambda i, *_: (0, 0), pipeline_mode=pl.Buffered(1))
    ins = [part, part, whole(dattn)]
    if came is None:
        return call(partial(last_send_body, seqs), dep, (1,), ins + [whole(v) for v in [*smalls, *parts]], [out(size)] * 4,
                    [shape((size, width), F32)] * 4, scalars=1, name="last_send")(which, x, ctx, dattn, *smalls, *parts)
    return call(partial(last_keep_body, seqs), dep, (1,), ins + [whole(v) for v in [*smalls, *came, *parts]], [out(2 * size)] * 2,
                [shape((2 * size, width), F32)] * 2, scalars=2, name="last_keep")(
                    which, place, x, ctx, dattn, *smalls, *came, *parts)


def middle_body(dupper, w_up, dres, hat1, sc1, g1, w_out, dres1, dattn, dctx, small):
    dhid = dres[...] + dot(dupper[...], w_up[...], 1, 1)
    xhat = hat1[...]

    @pl.when(pl.program_id(0) == 0)
    def _():
        small[...] = jnp.zeros_like(small)

    small[1:2, :] += jnp.sum(dhid * xhat, axis=0, keepdims=True)
    small[2:3, :] += jnp.sum(dhid, axis=0, keepdims=True)
    dhat = dhid * row(g1)
    first = jnp.mean(dhat, axis=-1, keepdims=True)
    second = jnp.mean(dhat * xhat, axis=-1, keepdims=True)
    value = sc1[...] * (dhat - first - xhat * second)
    dres1[...] = value
    low = value.astype(BF16)
    dattn[...] = low
    small[0:1, :] += jnp.sum(low.astype(F32), axis=0, keepdims=True)
    dctx[...] = dot(low, w_out[...], 1, 1).astype(BF16)


def middle_back(dupper, w_up, dres, hat1, sc1, g1, w_out, dep):
    rows, width = dres.shape
    ff = dupper.shape[1]
    tile = 256
    by = lambda cols: pl.BlockSpec((tile, cols), lambda i: (i, 0))
    return call(
        middle_body, dep, (rows // tile,),
        [by(ff), fixed((width, ff)), by(width), by(width), by(1), line(width), fixed((width, width))],
        [by(width), by(width), by(width),
         pl.BlockSpec((8, width), lambda i: (0, 0))],
        [shape((rows, width), F32), shape((rows, width), BF16), shape((rows, width), BF16),
         shape((8, width), F32)], name="middle_back",
    )(dupper, w_up, dres, hat1, sc1, g1, w_out)


def attend_back_body(seq, span, group, counts, q, k, v, dctx, lse, dq, dk, dv, qsum, vsum):
    mask = key_mask(counts[0, seq], span)
    for pair in range(group // 2):
        turned, keys, values = [], [], []
        for half in range(2):
            head = pair * 2 + half
            lanes = pl.ds(head * HD, HD)
            query = q[:, lanes] * HD ** (-0.5)
            key = k[:, lanes]
            grad = dctx[:, lanes]
            scores = dot(key, query, 1, 1) + mask
            probs = jnp.exp(scores - lse[0, 0, pl.ds(head, 1), :])
            dprobs = dot(v[:, lanes], grad, 1, 1)
            values.append(dot(probs.astype(BF16), grad))
            inner = jnp.sum(probs * dprobs, axis=0, keepdims=True)
            dscores = (probs * (dprobs - inner)).astype(BF16)
            keys.append(dot(dscores, query))
            turned.append(dot(key, dscores, 0, 0))
        cols = pl.ds(pair * 2 * HD, 2 * HD)
        low = (jnp.concatenate(turned, axis=0).T * HD ** (-0.5)).astype(BF16)
        dq[:, cols] = low
        qsum[:, cols] = jnp.sum(low.astype(F32), axis=0, keepdims=True)
        dk[:, cols] = jnp.concatenate(keys, axis=1).astype(BF16)
        low = jnp.concatenate(values, axis=1).astype(BF16)
        dv[:, cols] = low
        vsum[:, cols] = jnp.sum(low.astype(F32), axis=0, keepdims=True)


def attend_back(seq, counts, q, k, v, dctx, lse, span, dep):
    width = q.shape[1]
    group = 4
    cols = group * HD
    piece = pl.BlockSpec((span, cols), lambda g: (seq, g))
    mine = pl.BlockSpec((span, cols), lambda g: (0, g))
    sums = pl.BlockSpec((1, cols), lambda g: (0, g))
    return call(
        partial(attend_back_body, seq, span, group), dep, (width // cols,),
        [SMEM] + [piece] * 4 + [pl.BlockSpec((1, 1, group, span), lambda g: (g, seq, 0, 0))],
        [mine] * 3 + [sums] * 2, [shape((span, width), BF16)] * 3 + [shape((1, width), F32)] * 2, name="attend_back",
    )(counts, q, k, v, dctx, lse)


def token_body(dres1, wq, wk, wv, *rest):
    parts, out = rest[:-1], rest[-1]
    for s in range(len(parts) // 3):
        at = pl.ds(s * parts[0].shape[0], parts[0].shape[0])
        total = dres1[at, :]
        for part, weight in zip(parts[s * 3:s * 3 + 3], (wq, wk, wv)):
            total = total + dot(part[...], weight[...], 1, 1)
        out[at, :] = total


def token_grad(dres1, w_qkv, parts, dep):
    rows, width = dres1.shape
    span = parts[0].shape[0]
    tile = 256
    by = pl.BlockSpec((rows, tile), lambda i: (0, i))
    weight = [pl.BlockSpec((tile, width), lambda i, k=k: (i, k)) for k in range(3)]
    return call(token_body, dep, (width // tile,), [by, *weight] + [fixed((span, width))] * len(parts), by,
                shape((rows, width), F32), name="token_grad")(dres1, w_qkv, w_qkv, w_qkv, *parts)


def add_split_body(steps, bit, held, came, send, keep):
    step = pl.program_id(0)
    value = held[...] + came[...]

    @pl.when(step < steps)
    def _():
        send[...] = value

    @pl.when(step >= steps)
    def _():
        keep[...] = value


def block_rows(rows, cols):
    best = 8
    for r in range(8, rows + 1, 8):
        if rows % r == 0 and r * cols * 4 <= MIB:
            best = r
    return best


def add_split(bit, held, came, dep=None):
    rows, cols = held.shape
    half = rows // 2
    tile = block_rows(half, cols)
    steps = half // tile

    def at(i, b):
        first = i < steps
        return jnp.where(first, (1 - b[0]) * steps + i, b[0] * steps + i - steps), 0

    block = (tile, cols)
    return call(
        partial(add_split_body, steps), dep, (2 * steps,), [pl.BlockSpec(block, at)] * 2,
        [pl.BlockSpec(block, lambda i, b: (jnp.minimum(i, steps - 1), 0)),
         pl.BlockSpec(block, lambda i, b: (jnp.maximum(i - steps, 0), 0))],
        [shape((half, cols), F32)] * 2, scalars=1, name="add_split",
    )(bit, held, came)


def add_body(held, came, out):
    out[...] = held[...] + came[...]


def add(held, came, dep=None):
    rows, cols = held.shape
    tile = block_rows(rows, cols)
    spec = pl.BlockSpec((tile, cols), lambda i: (i, 0))
    return call(add_body, dep, (rows // tile,), [spec] * 2, spec, shape((rows, cols), F32), name="add")(held, came)


def gather_body(n, places, *refs):
    pieces, out, (held, in_sems, out_sems) = refs[:n], refs[n], refs[n + 1:]
    rows = pieces[0].shape[0]
    reads = [pltpu.make_async_copy(piece, held.at[i], in_sems.at[i]) for i, piece in enumerate(pieces)]
    for copy in reads:
        copy.start()
    writes = []
    for i in range(n):
        reads[i].wait()
        at = pl.multiple_of(places[i] * rows, 8)
        writes.append(pltpu.make_async_copy(held.at[i], out.at[pl.ds(at, rows), :], out_sems.at[i]))
        writes[-1].start()
    for copy in writes:
        copy.wait()


def gather(places, pieces, dep=None):
    n = len(pieces)
    rows, cols = pieces[0].shape
    return call(
        partial(gather_body, n), dep, (), [SMEM] + [ANY] * n, ANY, shape((n * rows, cols), F32),
        scratch=[pltpu.VMEM((n, rows, cols), F32), pltpu.SemaphoreType.DMA((n,)), pltpu.SemaphoreType.DMA((n,))],
        name="gather",
    )(places, *pieces)


def spread_body(blocks, moves, lines, whole, *refs):
    outs, (held, in_sems, out_sems) = refs[:-3], refs[-3:]
    size = whole.shape[0] // blocks
    cols = whole.shape[1]
    reads = [pltpu.make_async_copy(whole.at[pl.ds(i * size, size), :], held.at[pl.ds(i * size, size), :], in_sems.at[i])
             for i in range(blocks)]
    for copy in reads:
        copy.start()
    writes = []
    for i in range(blocks):
        reads[i].wait()
        first, rows, out, row, col = moves[i]
        copy = pltpu.make_async_copy(
            held.at[pl.ds(first, rows), :], outs[out].at[pl.ds(row, rows), pl.ds(col, cols)], out_sems.at[i])
        copy.start()
        writes.append(copy)
    first = len(outs) - len(lines)
    for out, (row, count) in zip(outs[first:], lines):
        for k in range(count):
            out[pl.ds(k * cols, cols)] = held[pl.ds(row + k, 1), :].reshape(cols)
    for copy in writes:
        copy.wait()


def spread(whole, blocks, moves, outs, lines=(), dep=None):
    cols = whole.shape[1]
    return call(
        partial(spread_body, blocks, moves, lines), dep, (), [ANY], [ANY] * len(outs) + [VMEM] * len(lines),
        list(outs) + [shape((count * cols,), F32) for _, count in lines],
        scratch=[pltpu.VMEM(whole.shape, F32), pltpu.SemaphoreType.DMA((blocks,)), pltpu.SemaphoreType.DMA((blocks,))],
        name="spread",
    )(whole)


COLUMNS = {"B": (0, 3072)}
AT_ONCE = ("A", "C")
ORDER = (
    "down_send", "slope", "down_keep", "upsB", "middle", "a2:A", "upkB", "ab0", "a3:A", "ab1", "last_send", "a2:B",
    "a4:A", "last_keep", "a3:B", "a5:A", "a4:B", "a2:C", "a5:B", "a3:C", "gE:B", "a4:C", "token", "h8:B", "h7:B",
    "h9:B", "a5:C", "copy_down", "fin:B", "cut_last",
)


class Ring:
    def __init__(self, n_dp, towers):
        self.n_dp, self.towers = n_dp, towers
        self.dp, self.tower = lax.axis_index("dp").astype(jnp.int32), lax.axis_index("tower").astype(jnp.int32)
        self.core = self.tower & 1
        x, y = self.x, self.y = self.dp & 1, (self.tower >> 1) & 1
        self.outer = jnp.where(self.core == 0, x, y)
        self.inner = jnp.where(self.core == 0, y, x)
        self.near = (self.dp >> 1) & 1
        self.far = [b for b in (4, 8, 16, 32, 64) if b < n_dp]

    def move(self, value, partner):
        pairs = []
        for dp in range(self.n_dp):
            for tower in range(self.towers):
                to_dp, to_tower = partner(dp, tower)
                pairs.append((dp * self.towers + tower, to_dp * self.towers + to_tower))
        return lax.ppermute(value, ("dp", "tower"), pairs)

    def place(self):
        out = []
        for bx in range(2):
            for by in range(2):
                outer, inner = jnp.where(self.core == 0, bx, by), jnp.where(self.core == 0, by, bx)
                out.append(jnp.where(outer == self.outer, 2, 0) + inner)
        return jnp.stack(out).astype(jnp.int32)

    def order(self):
        out = []
        for outer in (1 - self.outer, self.outer):
            for inner in range(2):
                out.append(jnp.where(self.core == 0, outer * 2 + inner, inner * 2 + outer))
        return jnp.stack(out).astype(jnp.int32)

    def bits(self):
        bits = [1]
        while bits[0] * 2 < self.n_dp * self.towers:
            bits.insert(0, bits[0] * 2)
        return bits

    def to_index(self, value, bit):
        count = self.n_dp * self.towers
        return lax.ppermute(value, ("dp", "tower"), [(i, i ^ bit) for i in range(count)])

    def gather(self, value):
        groups = []
        for far in range(self.n_dp // 4):
            groups.append([(far * 4 + near * 2 + x) * self.towers + y * 2 + core
                           for x in range(2) for y in range(2) for core in range(2) for near in range(2)])
        return lax.all_gather(value, ("dp", "tower"), axis_index_groups=groups, tiled=True)

    def to_core(self, value):
        return self.move(value, lambda d, t: (d, t ^ 1))

    def to_outer(self, value):
        return self.move(value, lambda d, t: (d, t ^ 2) if t & 1 else (d ^ 1, t))

    def to_inner(self, value):
        return self.move(value, lambda d, t: (d ^ 1, t) if t & 1 else (d, t ^ 2))

    def to_dp(self, value, bit):
        return self.move(value, lambda d, t: (d ^ bit, t))


class Sum:
    def __init__(self, ring, send, at_once):
        self.ring, self.at_once = ring, at_once
        self.came = [ring.to_core(v) for v in send]

    def out(self, send, keep):
        self.keep = keep
        self.came = self.ring.to_outer(send)
        return [keep]

    def a2(self, dep):
        send, self.keep = add_split(self.ring.inner.reshape(1), self.keep, self.came, dep)
        self.came = self.ring.to_inner(send)
        return [self.keep]

    def a3(self, dep):
        send, self.keep = add_split(self.ring.near.reshape(1), self.keep, self.came, dep)
        self.came = self.ring.to_dp(send, 2)
        return [self.keep]

    def a4(self, dep):
        self.keep = add(self.keep, self.came, dep)
        for bit in self.ring.far[:-1]:
            self.keep = self.keep + self.ring.to_dp(self.keep, bit)
        self.came = self.ring.to_dp(self.keep, self.ring.far[-1])
        return [self.keep]

    def a5(self, dep):
        self.keep = add(self.keep, self.came, dep)
        if self.at_once:
            self.whole = self.ring.gather(self.keep)
        else:
            self.came = self.ring.to_dp(self.keep, 2)
        return [self.keep]

    def gE(self, dep):
        ring = self.ring
        own = gather(jnp.stack([ring.near, 1 - ring.near]), [self.keep, self.came], dep)
        self.own, self.inner, self.outer = own, ring.to_inner(own), ring.to_outer(own)
        self.own_c = ring.to_core(own)
        return [own]

    def h7(self, dep):
        self.both, self.inner_c = self.ring.to_outer(self.inner), self.ring.to_core(self.inner)
        return dep + [self.inner]

    def h8(self, dep):
        self.outer_c = self.ring.to_core(self.outer)
        return dep + [self.outer]

    def h9(self, dep):
        self.both_c = self.ring.to_core(self.both)
        return dep + [self.both]

    def fin(self, dep):
        ring = self.ring
        pieces = [self.own, self.inner, self.outer, self.both, self.own_c, self.inner_c, self.outer_c, self.both_c]
        places = []
        for core in (ring.core, 1 - ring.core):
            inner_step = jnp.where(core == 0, 2, 4)
            base = ring.x * 4 + ring.y * 2
            places += [(base ^ step) + core for step in (0 * inner_step, inner_step, 6 - inner_step, 6 + 0 * inner_step)]
        self.whole = gather(jnp.stack(places), pieces, dep)
        return [self.whole]


def local(n_dp, towers, tokens, lengths, positive, w_qkv, q_bias, v_bias, w_out, out_bias, norm1_gain, norm1_bias,
          w_up, up_bias, w_down, down_bias, norm2_gain, norm2_bias):
    seqs, span, width = tokens.shape[1:]
    ff = up_bias.shape[0]
    x = tokens.reshape(seqs * span, width)
    ring = Ring(n_dp, towers)
    mine, other = ring.core.reshape(1), (1 - ring.core).reshape(1)
    place = ring.place()
    q, k, v, ctx, lse = attend(lengths, x, w_qkv, q_bias, v_bias, seqs, span)
    hid_t, hat1, sc1, act, slope, hat2, sc2, sums = feed(
        lengths, x, ctx, w_out, w_up, w_down, out_bias, norm1_gain, norm1_bias, up_bias, down_bias, seqs, span, F32)
    pooled = sums * norm2_gain / lengths[0][:, None].astype(F32) + norm2_bias
    every, bits = pooled, ring.bits()
    for bit in bits[:-1]:
        every = jnp.concatenate([every, ring.to_index(every, bit)], axis=0)
    own = (lax.axis_index("dp") * towers + lax.axis_index("tower")).astype(jnp.int32).reshape(1, 1)
    loss, dres, ddown, small2 = loss_step(lengths, own, positive, every, ring.to_index(every, bits[-1]), sums, norm2_gain, hat2, sc2,
                                          n_dp, towers, seqs, span, bits)
    sums_of, made = {}, {}

    def down_send(dep):
        send = down_grad(other, act, ddown, dep=dep)
        sums_of["A"] = Sum(ring, send, "A" in AT_ONCE)
        return [send[0]]

    def down_keep(dep):
        return sums_of["A"].out(*down_grad(mine, act, ddown, ring.order(), sums_of["A"].came, dep))

    def slope_step(dep):
        made["dupper"], made["upb"] = slope_back(ddown, slope, w_down, dep)
        return [made["upb"]]

    def middle(dep):
        made["dres1"], made["dattn"], made["dctx"], made["small1"] = middle_back(
            made["dupper"], w_up, dres, hat1, sc1, norm1_gain, w_out, dep)
        return [made["small1"]]

    def attention(s):
        def step(dep):
            made[s] = attend_back(s, lengths, q, k, v, made["dctx"], lse, span, dep)
            return [made[s][3]]
        return step

    def last_inputs():
        parts = [v for s in range(seqs) for v in made[s][:3]]
        smalls = [made[s][k] for k in (3, 4) for s in range(seqs)] + [made["small1"], made["upb"], small2]
        return made["dattn"], smalls, parts

    def last_send(dep):
        send = last_grad(other, x, ctx, *last_inputs(), dep=dep)
        sums_of["C"] = Sum(ring, send, "C" in AT_ONCE)
        return [send[0]]

    def last_keep(dep):
        return sums_of["C"].out(*last_grad(mine, x, ctx, *last_inputs(), place, sums_of["C"].came, dep))

    def token(dep):
        made["tokens"] = token_grad(made["dres1"], w_qkv, [v for s in range(seqs) for v in made[s][:3]], dep)
        return [made["tokens"]]

    def up_send(name):
        def step(dep):
            send = up_grad(other, hid_t, made["dupper"], COLUMNS[name], dep=dep)
            sums_of[name] = Sum(ring, send, name in AT_ONCE)
            return [send[0]]
        return step

    def up_keep(name):
        def step(dep):
            return sums_of[name].out(*up_grad(mine, hid_t, made["dupper"], COLUMNS[name], place, sums_of[name].came, dep))
        return step

    def copy_down(dep):
        rows = ff // 8
        (made["A"],) = spread(sums_of["A"].whole, 8, [(i * rows, rows, 0, i * rows, 0) for i in range(8)],
                              [shape((ff, width), F32)], dep=dep)
        return [made["A"]]

    def copy_up(dep):
        rows = width // 8
        (made["B"],) = spread(sums_of["B"].whole, 8, [(i * rows, rows, 0, i * rows, 0) for i in range(8)],
                              [shape((width, ff), F32)], dep=dep)
        return [made["B"]]

    def cut_last(dep):
        rows, size = width // 2, width // 2 + MORE
        moves = [(i * size, rows, i // 6, i % 2 * rows, (i // 2 % 3) * width) for i in range(8)]
        lines = [(rows + i, 1) for i in range(5)] + [(rows + 5, ff // width)]
        lines += [(rows + 5 + ff // width + i, 1) for i in range(3)]
        made["C"] = spread(sums_of["C"].whole, 8, moves, [shape((width, 3 * width), F32), shape((width, width), F32)],
                           lines, dep)
        return [made["C"][1]]

    steps = {"down_send": down_send, "slope": slope_step, "down_keep": down_keep, "middle": middle, "token": token,
             "copy_down": copy_down, "copy_up": copy_up, "cut_last": cut_last, "last_send": last_send, "last_keep": last_keep}
    steps.update({f"ab{s}": attention(s) for s in range(seqs)})
    for name in COLUMNS:
        steps["ups" + name], steps["upk" + name] = up_send(name), up_keep(name)
    dep = []
    for word in ORDER:
        what, _, name = word.partition(":")
        if what == "all":
            dep = dep + [sums_of[name].whole]
        elif name:
            dep = getattr(sums_of[name], what)(dep)
        else:
            dep = steps[what](dep)
    up = [sums_of[name].whole for name in COLUMNS]
    up = made["B"] if "B" in made else up[0] if len(up) == 1 else jnp.concatenate(up, axis=1)
    down = made["A"] if "A" in made else sums_of["A"].whole
    qkv, out, q_sum, v_sum, out_sum, gain1, shift1, up_sum, gain2, shift2, down_sum = made["C"]
    return (loss[0, 0], made["tokens"].reshape(tokens.shape), qkv, q_sum, v_sum, out, out_sum, gain1, shift1,
            up, up_sum, down, down_sum, gain2, shift2)


def solution(mesh):
    split = P("tower", "dp", None, None)
    in_specs = (split, P("tower", "dp")) + (P(),) * 14
    out_specs = (P(), split) + (P(),) * 13
    body = partial(local, mesh.shape["dp"], mesh.shape["tower"])
    return jax.shard_map(body, mesh=mesh, in_specs=in_specs, out_specs=out_specs, check_vma=False)
```

```python
from functools import partial

import jax
import jax.numpy as jnp
from jax import lax
from jax.experimental import pallas as pl
from jax.experimental.pallas import tpu as pltpu
from jax.sharding import PartitionSpec as P

HD = 64
SOFTMAX_TEMP = 0.01
NORM_EPS = 1e-06
MASKED = -1e30
F32 = jnp.float32
BF16 = jnp.bfloat16
ROOT_HALF = 0.7071067811865476
INV_ROOT_2PI = 0.3989422804014327
MIB = 1024 * 1024

SMEM = pl.BlockSpec(memory_space=pltpu.SMEM)
VMEM = pl.BlockSpec(memory_space=pltpu.VMEM)
ANY = pl.BlockSpec(memory_space=pl.ANY)


SCALE = 6.0
MICROSECONDS = {"down_send": 4, "down_keep": 5, "slope_back": 13, "up_send": 8, "up_keep": 10, "middle_back": 16,
                "attend_back": 12, "last_send": 4, "last_keep": 5, "token_grad": 9, "add_split": 4, "add": 2,
                "gather": 5}


def cost(name):
    return pl.CostEstimate(flops=max(1, int(1.1e9 * SCALE * MICROSECONDS.get(name, 1))), bytes_accessed=1, transcendentals=0)


def params():
    return pltpu.CompilerParams(vmem_limit_bytes=62 * MIB)


def call(body, dep, grid, in_specs, out_specs, out_shape, scratch=(), scalars=0, name=None, aliases=None):
    dep = [] if dep is None else list(dep)
    n_in = scalars + len(in_specs)

    def run(*refs):
        return body(*refs[:n_in], *refs[n_in + len(dep):])

    spec = pltpu.PrefetchScalarGridSpec(
        num_scalar_prefetch=scalars, grid=grid, in_specs=list(in_specs) + [ANY] * len(dep),
        out_specs=out_specs, scratch_shapes=scratch)
    made = pl.pallas_call(run, grid_spec=spec, out_shape=out_shape, compiler_params=params(), cost_estimate=cost(name),
                          input_output_aliases=aliases or {}, name=name)
    return lambda *args: made(*args, *dep)


def shape(dims, kind):
    return jax.ShapeDtypeStruct(dims, kind)


def line(cols, index=lambda *_: (0,)):
    return pl.BlockSpec((cols,), index)


def row(ref):
    return ref[...].reshape(1, -1)


def fixed(dims):
    return pl.BlockSpec(dims, lambda *_: (0,) * len(dims), pipeline_mode=pl.Buffered(1))


def dot(a, b, ca=1, cb=0):
    return lax.dot_general(a, b, (((ca,), (cb,)), ((), ())), preferred_element_type=F32)


def key_mask(count, span):
    place = lax.broadcasted_iota(jnp.int32, (span, 1), 0)
    return jnp.where(place < count, 0.0, MASKED)


def attend_body(seqs, span, group, counts, x, wq, wk, wv, qb, vb, q_out, k_out, v_out, ctx, lse):
    q_out[...] = (dot(x[...], wq[...]) + row(qb)).astype(BF16)
    k_out[...] = dot(x[...], wk[...]).astype(BF16)
    v_out[...] = (dot(x[...], wv[...]) + row(vb)).astype(BF16)
    for s in range(seqs):
        rows = pl.ds(s * span, span)
        mask = key_mask(counts[0, s], span)
        for pair in range(group // 2):
            both = []
            for half in range(2):
                head = pair * 2 + half
                lanes = pl.ds(head * HD, HD)
                query = q_out[rows, lanes] * HD ** (-0.5)
                scores = dot(k_out[rows, lanes], query, 1, 1) + mask
                highest = jnp.max(scores, axis=0, keepdims=True)
                expo = jnp.exp(scores - highest)
                summed = jnp.sum(expo, axis=0, keepdims=True)
                both.append(dot(v_out[rows, lanes], expo.astype(BF16), 0, 0) * (1.0 / summed))
                lse[0, s, pl.ds(head, 1), :] = highest + jnp.log(summed)
            both = jnp.concatenate(both, axis=0)
            ctx[rows, pl.ds(pair * 2 * HD, 2 * HD)] = both.T.astype(BF16)


def attend(counts, x, w_qkv, q_bias, v_bias, seqs, span):
    rows, width = x.shape
    group = 4
    cols = group * HD
    steps = width // cols
    piece = pl.BlockSpec((rows, cols), lambda g: (0, g))
    bias = line(cols, lambda g: (g,))
    weight = [pl.BlockSpec((width, cols), lambda g, k=k: (0, k * steps + g)) for k in range(3)]
    return pl.pallas_call(
        partial(attend_body, seqs, span, group),
        grid=(steps,),
        in_specs=[SMEM, fixed((rows, width)), *weight, bias, bias],
        out_specs=[piece] * 4 + [pl.BlockSpec((1, seqs, group, span), lambda g: (g, 0, 0, 0))],
        out_shape=[shape((rows, width), BF16)] * 4 + [shape((steps, seqs, group, span), F32)],
        compiler_params=params(),
        cost_estimate=cost(""),
        name="attend",
    )(counts, x, w_qkv, w_qkv, w_qkv, q_bias, v_bias)


def norm_parts(value):
    centre = value - jnp.mean(value, axis=-1, keepdims=True)
    spread = jnp.mean(centre * centre, axis=-1, keepdims=True)
    scale = lax.rsqrt(spread + NORM_EPS)
    return centre * scale, scale


def gelu_parts(u):
    bell = jnp.exp(-0.5 * (u * u))
    cdf = 0.5 + 0.5 * lax.erf(u * ROOT_HALF)
    return u * cdf, cdf + u * (INV_ROOT_2PI * bell)


def feed_body(tile, span, chunk, counts, x, ctx, w_out, w_up, w_down, ob, g1, b1, ub, db, g2, b2,
              hid_t, hat1, sc1, act, slope, hat2, sc2, sums, pooled):
    step = pl.program_id(0)
    attn = dot(ctx[...], w_out[...]) + row(ob)
    xhat, scale = norm_parts(x[...].astype(F32) + attn)
    hat1[...] = xhat
    sc1[...] = scale
    hidden = xhat * row(g1) + row(b1)
    low = hidden.astype(BF16)
    hid_t[...] = low.T
    total = hidden + row(db)
    for j in range(w_up.shape[1] // chunk):
        cols = pl.ds(j * chunk, chunk)
        upper = dot(low, w_up[:, cols]) + ub[cols].reshape(1, chunk)
        active, grad = gelu_parts(upper)
        active = active.astype(BF16)
        act[:, cols] = active
        slope[:, cols] = grad.astype(slope.dtype)
        total = total + dot(active, w_down[cols, :])
    xhat, scale = norm_parts(total)
    hat2[...] = xhat
    sc2[...] = scale
    seq = step * tile // span
    place = lax.broadcasted_iota(jnp.int32, (tile, 1), 0) + lax.rem(step * tile, span)
    part = jnp.sum(jnp.where(place < counts[0, seq], xhat, 0.0), axis=0, keepdims=True)

    @pl.when(step == 0)
    def _():
        sums[...] = jnp.zeros_like(sums)

    sums[pl.ds(seq, 1), :] += part

    @pl.when(step == pl.num_programs(0) - 1)
    def _():
        for s in range(sums.shape[0]):
            pooled[s:s + 1, :] = sums[s:s + 1, :] * row(g2) / counts[0, s].astype(F32) + row(b2)


def feed(counts, x, ctx, w_out, w_up, w_down, ob, g1, b1, ub, db, g2, b2, seqs, span, slope_kind):
    rows, width = x.shape
    ff = w_up.shape[1]
    tile = 256
    by = lambda cols: pl.BlockSpec((tile, cols), lambda i: (i, 0))
    return pl.pallas_call(
        partial(feed_body, tile, span, 768),
        grid=(rows // tile,),
        in_specs=[SMEM, by(width), by(width), fixed((width, width)), fixed((width, ff)), fixed((ff, width)),
                  line(width), line(width), line(width), line(ff), line(width), line(width), line(width)],
        out_specs=[pl.BlockSpec((width, tile), lambda i: (0, i)), by(width), by(1), by(ff), by(ff), by(width), by(1),
                   pl.BlockSpec((seqs, width), lambda i: (0, 0)), pl.BlockSpec((seqs, width), lambda i: (0, 0))],
        out_shape=[shape((width, rows), BF16), shape((rows, width), F32), shape((rows, 1), F32),
                   shape((rows, ff), BF16), shape((rows, ff), slope_kind), shape((rows, width), F32),
                   shape((rows, 1), F32), shape((seqs, width), F32), shape((seqs, width), F32)],
        compiler_params=params(),
        cost_estimate=cost(""),
        name="feed",
    )(counts, x, ctx, w_out, w_up, w_down, ob, g1, b1, ub, db, g2, b2)


def loss_body(n_dp, towers, seqs, span, bits, counts, own, pos, low, high, sums, g2, hat_from, sc2,
              loss, dres_to, ddown_to, small, scratch, hat2, dres, ddown, sems):
    count = n_dp * towers * seqs
    pairs = pos.shape[0]
    tile = span // 2
    total_rows = seqs * span
    reads = [pltpu.make_async_copy(hat_from.at[pl.ds(i, tile), :], hat2.at[pl.ds(i, tile), :], sems.at[0, i // tile])
             for i in range(0, total_rows, tile)]
    for copy in reads:
        copy.start()
    writes = []
    rows = jnp.concatenate([low[...], high[...]], axis=0)
    inv = lax.rsqrt(jnp.sum(rows * rows, axis=-1, keepdims=True) + NORM_EPS)
    unit = rows * inv
    full = lax.Precision.HIGHEST
    logits = lax.dot_general(unit, unit, (((1,), (1,)), ((), ())), precision=full,
                             preferred_element_type=F32) / SOFTMAX_TEMP

    def place(i):
        block, j = i // seqs, lax.rem(i, seqs)
        device = jnp.full_like(block, own[0, 0])
        for n, bit in enumerate(bits):
            device = device ^ (((block >> n) & 1) * bit)
        dp, tower = device // towers, lax.rem(device, towers)
        half = towers // 2
        return tower < half, lax.rem(tower, half) * (n_dp * seqs) + dp * seqs + j

    is_query, query = place(lax.broadcasted_iota(jnp.int32, (count, 1), 0))
    key_is_query, key = place(lax.broadcasted_iota(jnp.int32, (1, count), 1))
    is_key = jnp.logical_not(key_is_query)
    lookup = lax.broadcasted_iota(jnp.int32, (count, pairs), 1) == query
    wanted = jnp.sum(jnp.where(lookup, row(pos).astype(F32), 0.0), axis=1, keepdims=True)
    hit = (key.astype(F32) == wanted) & is_key & is_query
    inside = is_key & is_query
    shown = jnp.where(is_key, logits, MASKED)
    highest = jnp.max(shown, axis=1, keepdims=True)
    expo = jnp.where(inside, jnp.exp(shown - highest), 0.0)
    summed = jnp.sum(expo, axis=1, keepdims=True)
    safe = jnp.where(is_query, summed, 1.0)
    picked = jnp.sum(jnp.where(hit, logits, 0.0), axis=1, keepdims=True)
    each = jnp.where(is_query, highest + jnp.log(safe) - picked, 0.0)
    loss[...] = jnp.sum(each, axis=0, keepdims=True) / pairs
    grad = (expo / safe - jnp.where(hit, 1.0, 0.0)) / (pairs * SOFTMAX_TEMP)
    dunit = lax.dot_general(grad, unit, (((1,), (0,)), ((), ())), precision=full, preferred_element_type=F32)
    dunit += lax.dot_general(grad, unit, (((0,), (0,)), ((), ())), precision=full, preferred_element_type=F32)
    inner = jnp.sum(dunit * rows, axis=-1, keepdims=True)
    scratch[...] = inv * dunit - rows * (inv * inv * inv * inner)

    width = rows.shape[1]
    small[...] = jnp.zeros_like(small)
    for s in range(seqs):
        pooled = scratch[pl.ds(s, 1), :]
        n = counts[0, s]
        dout = pooled / n.astype(F32)
        small[0:1, :] += dout * sums[s:s + 1, :]
        small[1:2, :] += pooled
        dhat = dout * row(g2)
        first = jnp.mean(dhat, axis=-1, keepdims=True)
        total = jnp.zeros((1, width), F32)
        for part in range(2):
            at = pl.ds(s * span + part * tile, tile)
            reads[s * 2 + part].wait()
            xhat = hat2[at, :]
            second = jnp.mean(dhat * xhat, axis=-1, keepdims=True)
            live = lax.broadcasted_iota(jnp.int32, (tile, 1), 0) + part * tile < n
            scale = jnp.where(live, sc2[at, :], 0.0)
            value = scale * (dhat - first - xhat * second)
            dres[at, :] = value
            low = value.astype(BF16)
            ddown[at, :] = low
            total += jnp.sum(low.astype(F32), axis=0, keepdims=True)
            for k, (left, to) in enumerate(((dres, dres_to), (ddown, ddown_to))):
                writes.append(pltpu.make_async_copy(left.at[at, :], to.at[at, :], sems.at[1 + k, s * 2 + part]))
                writes[-1].start()
        small[2:3, :] += total
    for copy in writes:
        copy.wait()


def loss_step(counts, own, pos, low, high, sums, g2, hat2, sc2, n_dp, towers, seqs, span, bits):
    rows, width = hat2.shape
    return pl.pallas_call(
        partial(loss_body, n_dp, towers, seqs, span, bits),
        in_specs=[SMEM, SMEM] + [VMEM] * 5 + [ANY, VMEM],
        out_specs=[VMEM, ANY, ANY, VMEM],
        out_shape=[shape((1, 1), F32), shape((rows, width), F32), shape((rows, width), BF16), shape((8, width), F32)],
        scratch_shapes=[pltpu.VMEM((2 * low.shape[0], width), F32), pltpu.VMEM((rows, width), F32),
                        pltpu.VMEM((rows, width), F32), pltpu.VMEM((rows, width), BF16),
                        pltpu.SemaphoreType.DMA((3, 2 * seqs))],
        compiler_params=params(),
        cost_estimate=cost(""),
        name="loss",
    )(counts, own, pos, low, high, sums, g2, hat2, sc2)


def slope_body(ddown, slope, w_down, dupper, upb):
    value = (slope[...].astype(F32) * dot(ddown[...], w_down[...], 1, 1)).astype(BF16)
    dupper[...] = value
    upb[...] = jnp.sum(value.astype(F32), axis=0, keepdims=True)


def slope_back(ddown, slope, w_down, dep):
    rows, width = ddown.shape
    ff = slope.shape[1]
    tile = 768
    by = pl.BlockSpec((rows, tile), lambda i: (0, i))
    return call(
        slope_body, dep, (ff // tile,), [fixed((rows, width)), by, pl.BlockSpec((tile, width), lambda i: (i, 0))],
        [by, pl.BlockSpec((1, tile), lambda i: (0, i))], [shape((rows, ff), BF16), shape((1, ff), F32)],
        name="slope_back",
    )(ddown, slope, w_down)


def share(value, j, place, send, keep):
    rows = value.shape[0]

    @pl.when(place[j] < 2)
    def _():
        send[pl.ds(pl.multiple_of(place[j] * rows, rows), rows), :] = value

    @pl.when(place[j] >= 2)
    def _():
        keep[pl.ds(pl.multiple_of((place[j] - 2) * rows, rows), rows), :] = value


def up_send_body(which, a0, a1, a2, a3, b, *outs):
    value = dot(jnp.concatenate([a0[...], a1[...], a2[...], a3[...]], axis=0), b[...])
    rows = a0.shape[0]
    for j in range(4):
        outs[j][...] = value[j * rows:(j + 1) * rows]


def up_keep_body(which, place, a0, a1, a2, a3, b, *rest):
    came, (send, keep) = rest[:4], rest[4:]
    value = dot(jnp.concatenate([a0[...], a1[...], a2[...], a3[...]], axis=0), b[...])
    rows = a0.shape[0]
    for j in range(4):
        share(value[j * rows:(j + 1) * rows] + came[j][...], j, place, send, keep)


def up_grad(which, a, b, columns, place=None, came=None, dep=None):
    m, k = a.shape
    start, n = columns
    rows, tile = m // 8, 768
    ins = [pl.BlockSpec((rows, k), lambda i, w, *_, j=j: (2 * j + w[0], 0)) for j in range(4)]
    ins.append(pl.BlockSpec((k, tile), lambda i, *_: (0, i + start // tile)))
    by = lambda r: pl.BlockSpec((r, tile), lambda i, *_: (0, i))
    if came is None:
        return call(up_send_body, dep, (n // tile,), ins, [by(rows)] * 4, [shape((rows, n), F32)] * 4, scalars=1,
                    name="up_send")(which, a, a, a, a, b)
    return call(up_keep_body, dep, (n // tile,), ins + [by(rows)] * 4, [by(m // 4)] * 2,
                [shape((m // 4, n), F32)] * 2, scalars=2, name="up_keep")(which, place, a, a, a, a, b, *came)


def down_send_body(blocks, a, b, *outs):
    value = dot(a[...], b[...], 0, 0)
    for j, out in enumerate(outs):
        @pl.when(pl.program_id(0) == j)
        def _(out=out):
            out[...] = value


def down_keep_body(blocks, a, b, *rest):
    came, out = rest[:2], rest[2]
    value = dot(a[...], b[...], 0, 0)
    for j, one in enumerate(came):
        @pl.when(pl.program_id(0) == j)
        def _(one=one):
            out[...] = value + one[...]


def down_grad(blocks, a, b, came=None, dep=None):
    rows, m = a.shape
    n = b.shape[1]
    tile = m // 8
    block = (tile, n)
    ins = [pl.BlockSpec((rows, tile), lambda i, w: (0, w[i])), fixed((rows, n))]
    if came is None:
        return call(down_send_body, dep, (2,), ins, [pl.BlockSpec(block, lambda i, w: (0, 0))] * 2, [shape(block, F32)] * 2,
                    scalars=1, name="down_send")(blocks, a, b)
    return call(down_keep_body, dep, (2,), ins + [fixed(block)] * 2, pl.BlockSpec(block, lambda i, w: (i, 0)),
                shape((2 * tile, n), F32), scalars=1, name="down_keep")(blocks, a, b, *came)


MORE = 16


def last_small(which, kind, smalls):
    width = smalls[-1].shape[1]
    small1, upb, small2 = (v[...] for v in smalls[-3:])
    sums = [v[...] for v in smalls[:-3]]
    seqs = len(sums) // 2
    lines = [sum(sums[:seqs]), sum(sums[seqs:]), small1[:3]]
    lines += [upb[:, i:i + width] for i in range(0, upb.shape[1], width)] + [small2[:3]]
    lines = jnp.concatenate(lines, axis=0)
    lines = jnp.concatenate([lines, jnp.zeros((MORE - lines.shape[0], width), F32)], axis=0)
    return jnp.where((which[0] == 0) & (kind == 0), lines, 0.0)


def last_body(seqs, keeping, which, kinds, *refs):
    refs = list(refs)
    x, ctx, dattn = refs[:3]
    smalls, refs = refs[3:2 * seqs + 6], refs[2 * seqs + 6:]
    came, refs = (refs[:2], refs[2:]) if keeping else (None, refs)
    parts, refs = refs[:3 * seqs], refs[3 * seqs:]
    outs, refs = (refs[:1], refs[1:]) if keeping else (refs[:2], refs[2:])
    left, right, held, done, sems = refs
    half = left.shape[2]
    span = parts[0].shape[0]
    size = half + MORE
    cols = pl.ds(pl.multiple_of(which[0] * half, half), half)

    def reads(n, act):
        for kind in range(4):
            def load(kind=kind):
                act(pltpu.make_async_copy((ctx if kind == 3 else x).at[:, cols], left.at[n], sems.at[0, n]))
                if kind == 3:
                    act(pltpu.make_async_copy(dattn, right.at[n], sems.at[1, n]))
                else:
                    for s in range(seqs):
                        act(pltpu.make_async_copy(
                            parts[s * 3 + kind], right.at[n, pl.ds(s * span, span), :], sems.at[1 + s, n]))
            pl.when(kinds[n] == kind)(load)
        if keeping:
            act(pltpu.make_async_copy(came[n], held.at[n], sems.at[seqs + 1, n]))

    for n in range(2):
        reads(n, lambda copy: copy.start())
    writes = []
    for n in range(2):
        reads(n, lambda copy: copy.wait())
        value = dot(left[n], right[n], 0, 0)
        extra = last_small(which, kinds[n], smalls)
        if keeping:
            value = value + held[n, pl.ds(0, half), :]
            extra = extra + held[n, pl.ds(half, MORE), :]
        done[n, pl.ds(0, half), :] = value
        done[n, pl.ds(half, MORE), :] = extra
        to = outs[0].at[pl.ds(n * size, size), :] if keeping else outs[n]
        writes.append(pltpu.make_async_copy(done.at[n], to, sems.at[seqs + 2, n]))
        writes[-1].start()
    for copy in writes:
        copy.wait()


def last_grad(which, kinds, x, ctx, dattn, smalls, parts, came=None, dep=None):
    rows, width = x.shape
    half = width // 2
    size = half + MORE
    seqs = len(parts) // 3
    keeping = came is not None
    scratch = [pltpu.VMEM((2, rows, half), BF16), pltpu.VMEM((2, rows, width), BF16), pltpu.VMEM((2, size, width), F32),
               pltpu.VMEM((2, size, width), F32), pltpu.SemaphoreType.DMA((seqs + 3, 2))]
    ins = [ANY] * 3 + [VMEM] * len(smalls) + [ANY] * (len(parts) + (2 if keeping else 0))
    outs = [shape((2 * size, width), F32)] if keeping else [shape((size, width), F32)] * 2
    made = call(partial(last_body, seqs, keeping), dep, (), ins, [ANY] * len(outs), outs, scratch=scratch,
                scalars=2, name="last_keep" if keeping else "last_send")
    return made(which, kinds, x, ctx, dattn, *smalls, *(came if keeping else []), *parts)


def middle_body(dupper, w_up, dres, hat1, sc1, g1, w_out, dres1, dattn, dctx, small):
    dhid = dres[...] + dot(dupper[...], w_up[...], 1, 1)
    xhat = hat1[...]

    @pl.when(pl.program_id(0) == 0)
    def _():
        small[...] = jnp.zeros_like(small)

    small[1:2, :] += jnp.sum(dhid * xhat, axis=0, keepdims=True)
    small[2:3, :] += jnp.sum(dhid, axis=0, keepdims=True)
    dhat = dhid * row(g1)
    first = jnp.mean(dhat, axis=-1, keepdims=True)
    second = jnp.mean(dhat * xhat, axis=-1, keepdims=True)
    value = sc1[...] * (dhat - first - xhat * second)
    dres1[...] = value
    low = value.astype(BF16)
    dattn[...] = low
    small[0:1, :] += jnp.sum(low.astype(F32), axis=0, keepdims=True)
    dctx[...] = dot(low, w_out[...], 1, 1).astype(BF16)


def middle_back(dupper, w_up, dres, hat1, sc1, g1, w_out, dep):
    rows, width = dres.shape
    ff = dupper.shape[1]
    tile = 256
    by = lambda cols: pl.BlockSpec((tile, cols), lambda i: (i, 0))
    return call(
        middle_body, dep, (rows // tile,),
        [by(ff), fixed((width, ff)), by(width), by(width), by(1), line(width), fixed((width, width))],
        [by(width), by(width), by(width),
         pl.BlockSpec((8, width), lambda i: (0, 0))],
        [shape((rows, width), F32), shape((rows, width), BF16), shape((rows, width), BF16),
         shape((8, width), F32)], name="middle_back",
    )(dupper, w_up, dres, hat1, sc1, g1, w_out)


def attend_back_body(seq, span, group, counts, q, k, v, dctx, lse, dq, dk, dv, qsum, vsum):
    mask = key_mask(counts[0, seq], span)
    for pair in range(group // 2):
        turned, keys, values = [], [], []
        for half in range(2):
            head = pair * 2 + half
            lanes = pl.ds(head * HD, HD)
            query = q[:, lanes] * HD ** (-0.5)
            key = k[:, lanes]
            grad = dctx[:, lanes]
            scores = dot(key, query, 1, 1) + mask
            probs = jnp.exp(scores - lse[0, 0, pl.ds(head, 1), :])
            dprobs = dot(v[:, lanes], grad, 1, 1)
            values.append(dot(probs.astype(BF16), grad))
            inner = jnp.sum(probs * dprobs, axis=0, keepdims=True)
            dscores = (probs * (dprobs - inner)).astype(BF16)
            keys.append(dot(dscores, query))
            turned.append(dot(key, dscores, 0, 0))
        cols = pl.ds(pair * 2 * HD, 2 * HD)
        low = (jnp.concatenate(turned, axis=0).T * HD ** (-0.5)).astype(BF16)
        dq[:, cols] = low
        qsum[:, cols] = jnp.sum(low.astype(F32), axis=0, keepdims=True)
        dk[:, cols] = jnp.concatenate(keys, axis=1).astype(BF16)
        low = jnp.concatenate(values, axis=1).astype(BF16)
        dv[:, cols] = low
        vsum[:, cols] = jnp.sum(low.astype(F32), axis=0, keepdims=True)


def attend_back(seq, counts, q, k, v, dctx, lse, span, dep):
    width = q.shape[1]
    group = 4
    cols = group * HD
    piece = pl.BlockSpec((span, cols), lambda g: (seq, g))
    mine = pl.BlockSpec((span, cols), lambda g: (0, g))
    sums = pl.BlockSpec((1, cols), lambda g: (0, g))
    return call(
        partial(attend_back_body, seq, span, group), dep, (width // cols,),
        [SMEM] + [piece] * 4 + [pl.BlockSpec((1, 1, group, span), lambda g: (g, seq, 0, 0))],
        [mine] * 3 + [sums] * 2, [shape((span, width), BF16)] * 3 + [shape((1, width), F32)] * 2, name="attend_back",
    )(counts, q, k, v, dctx, lse)


def token_body(dres1, wq, wk, wv, *rest):
    parts, out = rest[:-1], rest[-1]
    for s in range(len(parts) // 3):
        at = pl.ds(s * parts[0].shape[0], parts[0].shape[0])
        total = dres1[at, :]
        for part, weight in zip(parts[s * 3:s * 3 + 3], (wq, wk, wv)):
            total = total + dot(part[...], weight[...], 1, 1)
        out[at, :] = total


def token_grad(dres1, w_qkv, parts, dep):
    rows, width = dres1.shape
    span = parts[0].shape[0]
    tile = 256
    by = pl.BlockSpec((rows, tile), lambda i: (0, i))
    weight = [pl.BlockSpec((tile, width), lambda i, k=k: (i, k)) for k in range(3)]
    return call(token_body, dep, (width // tile,), [by, *weight] + [fixed((span, width))] * len(parts), by,
                shape((rows, width), F32), name="token_grad")(dres1, w_qkv, w_qkv, w_qkv, *parts)


def add_split_body(steps, bit, held, came, send, keep):
    step = pl.program_id(0)
    value = held[...] + came[...]

    @pl.when(step < steps)
    def _():
        send[...] = value

    @pl.when(step >= steps)
    def _():
        keep[...] = value


def block_rows(rows, cols):
    best = 8
    for r in range(8, rows + 1, 8):
        if rows % r == 0 and r * cols * 4 <= MIB:
            best = r
    return best


def add_split(bit, held, came, dep=None):
    rows, cols = held.shape
    half = rows // 2
    tile = block_rows(half, cols)
    steps = half // tile

    def at(i, b):
        first = i < steps
        return jnp.where(first, (1 - b[0]) * steps + i, b[0] * steps + i - steps), 0

    block = (tile, cols)
    return call(
        partial(add_split_body, steps), dep, (2 * steps,), [pl.BlockSpec(block, at)] * 2,
        [pl.BlockSpec(block, lambda i, b: (jnp.minimum(i, steps - 1), 0)),
         pl.BlockSpec(block, lambda i, b: (jnp.maximum(i - steps, 0), 0))],
        [shape((half, cols), F32)] * 2, scalars=1, name="add_split",
    )(bit, held, came)


def add_body(held, came, out):
    out[...] = held[...] + came[...]


def add(held, came, dep=None):
    rows, cols = held.shape
    tile = block_rows(rows, cols)
    spec = pl.BlockSpec((tile, cols), lambda i: (i, 0))
    return call(add_body, dep, (rows // tile,), [spec] * 2, spec, shape((rows, cols), F32), name="add")(held, came)


def gather_body(n, places, *refs):
    pieces, out, (held, in_sems, out_sems) = refs[:n], refs[n], refs[n + 1:]
    rows = pieces[0].shape[0]
    reads = [pltpu.make_async_copy(piece, held.at[i], in_sems.at[i]) for i, piece in enumerate(pieces)]
    for copy in reads:
        copy.start()
    writes = []
    for i in range(n):
        reads[i].wait()
        at = pl.multiple_of(places[i] * rows, 8)
        writes.append(pltpu.make_async_copy(held.at[i], out.at[pl.ds(at, rows), :], out_sems.at[i]))
        writes[-1].start()
    for copy in writes:
        copy.wait()


def gather(places, pieces, dep=None):
    n = len(pieces)
    rows, cols = pieces[0].shape
    return call(
        partial(gather_body, n), dep, (), [SMEM] + [ANY] * n, ANY, shape((n * rows, cols), F32),
        scratch=[pltpu.VMEM((n, rows, cols), F32), pltpu.SemaphoreType.DMA((n,)), pltpu.SemaphoreType.DMA((n,))],
        name="gather",
    )(places, *pieces)


def spread_body(blocks, moves, lines, whole, *refs):
    outs, (held, in_sems, out_sems) = refs[:-3], refs[-3:]
    size = whole.shape[0] // blocks
    cols = whole.shape[1]
    reads = [pltpu.make_async_copy(whole.at[pl.ds(i * size, size), :], held.at[pl.ds(i * size, size), :], in_sems.at[i])
             for i in range(blocks)]
    for copy in reads:
        copy.start()
    writes = []
    for i in range(blocks):
        reads[i].wait()
        first, rows, out, row, col = moves[i]
        copy = pltpu.make_async_copy(
            held.at[pl.ds(first, rows), :], outs[out].at[pl.ds(row, rows), pl.ds(col, cols)], out_sems.at[i])
        copy.start()
        writes.append(copy)
    first = len(outs) - len(lines)
    for out, (row, count) in zip(outs[first:], lines):
        for k in range(count):
            out[pl.ds(k * cols, cols)] = held[pl.ds(row + k, 1), :].reshape(cols)
    for copy in writes:
        copy.wait()


def spread(whole, blocks, moves, outs, lines=(), dep=None):
    cols = whole.shape[1]
    return call(
        partial(spread_body, blocks, moves, lines), dep, (), [ANY], [ANY] * len(outs) + [VMEM] * len(lines),
        list(outs) + [shape((count * cols,), F32) for _, count in lines],
        scratch=[pltpu.VMEM(whole.shape, F32), pltpu.SemaphoreType.DMA((blocks,)), pltpu.SemaphoreType.DMA((blocks,))],
        name="spread",
    )(whole)


COLUMNS = {"B": (0, 3072)}
AT_ONCE = ("A", "C")
ORDER = (
    "down_s0", "down_s1", "down_k0", "slope", "down_k1", "upsB", "a2:A", "middle", "z3:A", "upkB", "ab0", "ab1",
    "last_s0", "last_s1", "a2:B", "last_k0", "z5:A", "last_k1", "a3:B", "a4:B", "a2:C", "a5:B", "a3:C", "gE:B",
    "a4:C", "token", "h8:B", "h7:B", "h9:B", "a5:C", "copy_down", "fin:B", "cut_last",
)


class Ring:
    def __init__(self, n_dp, towers):
        self.n_dp, self.towers = n_dp, towers
        self.dp, self.tower = lax.axis_index("dp").astype(jnp.int32), lax.axis_index("tower").astype(jnp.int32)
        self.core = self.tower & 1
        x, y = self.x, self.y = self.dp & 1, (self.tower >> 1) & 1
        self.outer = jnp.where(self.core == 0, x, y)
        self.inner = jnp.where(self.core == 0, y, x)
        self.near = (self.dp >> 1) & 1
        self.far = [b for b in (4, 8, 16, 32, 64) if b < n_dp]

    def move(self, value, partner):
        pairs = []
        for dp in range(self.n_dp):
            for tower in range(self.towers):
                to_dp, to_tower = partner(dp, tower)
                pairs.append((dp * self.towers + tower, to_dp * self.towers + to_tower))
        return lax.ppermute(value, ("dp", "tower"), pairs)

    def place(self):
        out = []
        for bx in range(2):
            for by in range(2):
                outer, inner = jnp.where(self.core == 0, bx, by), jnp.where(self.core == 0, by, bx)
                out.append(jnp.where(outer == self.outer, 2, 0) + inner)
        return jnp.stack(out).astype(jnp.int32)

    def order(self, core):
        mine = jnp.where(core == 0, self.x, self.y)
        out = []
        for outer in (1 - mine, mine):
            for inner in range(2):
                out.append(jnp.where(core == 0, outer * 2 + inner, inner * 2 + outer))
        return jnp.stack(out).astype(jnp.int32)

    def bits(self):
        bits = [1]
        while bits[0] * 2 < self.n_dp * self.towers:
            bits.insert(0, bits[0] * 2)
        return bits

    def to_index(self, value, bit):
        count = self.n_dp * self.towers
        return lax.ppermute(value, ("dp", "tower"), [(i, i ^ bit) for i in range(count)])

    def gather(self, value):
        groups = []
        for far in range(self.n_dp // 4):
            groups.append([(far * 4 + near * 2 + x) * self.towers + y * 2 + core
                           for x in range(2) for y in range(2) for core in range(2) for near in range(2)])
        return lax.all_gather(value, ("dp", "tower"), axis_index_groups=groups, tiled=True)

    def along_z(self, value):
        far = self.n_dp // 2
        groups = [[(z * 2 + x) * self.towers + t for z in range(far)] for x in range(2) for t in range(self.towers)]
        return lax.psum(value, ("dp", "tower"), axis_index_groups=groups)

    def gather_plane(self, value):
        groups = [[(z * 2 + x) * self.towers + t for x in range(2) for t in range(self.towers)]
                  for z in range(self.n_dp // 2)]
        return lax.all_gather(value, ("dp", "tower"), axis_index_groups=groups, tiled=True)

    def to_core(self, value):
        return self.move(value, lambda d, t: (d, t ^ 1))

    def to_outer(self, value):
        return self.move(value, lambda d, t: (d, t ^ 2) if t & 1 else (d ^ 1, t))

    def to_inner(self, value):
        return self.move(value, lambda d, t: (d ^ 1, t) if t & 1 else (d, t ^ 2))

    def to_dp(self, value, bit):
        return self.move(value, lambda d, t: (d ^ bit, t))


class Sum:
    def __init__(self, ring, at_once):
        self.ring, self.at_once, self.from_core = ring, at_once, []

    def core(self, send):
        self.from_core += [self.ring.to_core(v) for v in send]
        return [send[0]]

    def out(self, send, keep=None):
        self.keep = keep
        self.came = self.ring.to_outer(send)
        return [send if keep is None else keep]

    def rest(self, keep):
        self.keep = keep
        return [keep]

    def a2(self, dep):
        send, self.keep = add_split(self.ring.inner.reshape(1), self.keep, self.came, dep)
        self.came = self.ring.to_inner(send)
        return [self.keep]

    def a3(self, dep):
        send, self.keep = add_split(self.ring.near.reshape(1), self.keep, self.came, dep)
        self.came = self.ring.to_dp(send, 2)
        return [self.keep]

    def z3(self, dep):
        self.keep = add(self.keep, self.came, dep)
        self.summed = self.ring.along_z(self.keep)
        return [self.keep]

    def z5(self, dep):
        self.whole = self.ring.gather_plane(self.summed)
        return dep + [self.summed]

    def a4(self, dep):
        self.keep = add(self.keep, self.came, dep)
        for bit in self.ring.far[:-1]:
            self.keep = self.keep + self.ring.to_dp(self.keep, bit)
        self.came = self.ring.to_dp(self.keep, self.ring.far[-1])
        return [self.keep]

    def a5(self, dep):
        self.keep = add(self.keep, self.came, dep)
        if self.at_once:
            self.whole = self.ring.gather(self.keep)
        else:
            self.came = self.ring.to_dp(self.keep, 2)
        return [self.keep]

    def gE(self, dep):
        ring = self.ring
        own = gather(jnp.stack([ring.near, 1 - ring.near]), [self.keep, self.came], dep)
        self.own, self.inner, self.outer = own, ring.to_inner(own), ring.to_outer(own)
        self.own_c = ring.to_core(own)
        return [own]

    def h7(self, dep):
        self.both, self.inner_c = self.ring.to_outer(self.inner), self.ring.to_core(self.inner)
        return dep + [self.inner]

    def h8(self, dep):
        self.outer_c = self.ring.to_core(self.outer)
        return dep + [self.outer]

    def h9(self, dep):
        self.both_c = self.ring.to_core(self.both)
        return dep + [self.both]

    def fin(self, dep):
        ring = self.ring
        pieces = [self.own, self.inner, self.outer, self.both, self.own_c, self.inner_c, self.outer_c, self.both_c]
        places = []
        for core in (ring.core, 1 - ring.core):
            inner_step = jnp.where(core == 0, 2, 4)
            base = ring.x * 4 + ring.y * 2
            places += [(base ^ step) + core for step in (0 * inner_step, inner_step, 6 - inner_step, 6 + 0 * inner_step)]
        self.whole = gather(jnp.stack(places), pieces, dep)
        return [self.whole]


def local(n_dp, towers, tokens, lengths, positive, w_qkv, q_bias, v_bias, w_out, out_bias, norm1_gain, norm1_bias,
          w_up, up_bias, w_down, down_bias, norm2_gain, norm2_bias):
    seqs, span, width = tokens.shape[1:]
    ff = up_bias.shape[0]
    x = tokens.reshape(seqs * span, width)
    ring = Ring(n_dp, towers)
    mine, other = ring.core.reshape(1), (1 - ring.core).reshape(1)
    place = ring.place()
    q, k, v, ctx, lse = attend(lengths, x, w_qkv, q_bias, v_bias, seqs, span)
    hid_t, hat1, sc1, act, slope, hat2, sc2, sums, pooled = feed(
        lengths, x, ctx, w_out, w_up, w_down, out_bias, norm1_gain, norm1_bias, up_bias, down_bias, norm2_gain,
        norm2_bias, seqs, span, BF16)
    every, bits = pooled, ring.bits()
    for pair in range(0, len(bits) - 1, 2):
        first, second = bits[pair:pair + 2]
        every = jnp.concatenate(
            [every] + [ring.to_index(every, bit) for bit in (first, second, first | second)], axis=0)
    for bit in bits[len(bits) // 2 * 2:-1]:
        every = jnp.concatenate([every, ring.to_index(every, bit)], axis=0)
    half = every.shape[0] // 2
    halves = (every, ring.to_index(every, bits[-1])) if len(bits) % 2 else (every[:half], every[half:])
    own = (lax.axis_index("dp") * towers + lax.axis_index("tower")).astype(jnp.int32).reshape(1, 1)
    loss, dres, ddown, small2 = loss_step(lengths, own, positive, *halves, sums, norm2_gain, hat2, sc2,
                                          n_dp, towers, seqs, span, bits)
    sums_of, made = {}, {}

    for name in ("A", "C", *COLUMNS):
        sums_of[name] = Sum(ring, name in AT_ONCE)
    theirs, ours = ring.order(1 - ring.core), ring.order(ring.core)

    def down_send(n):
        def step(dep):
            return sums_of["A"].core(down_grad(2 * theirs[2 * n:2 * n + 2] + 1 - ring.core, act, ddown, dep=dep))
        return step

    def down_keep(n):
        def step(dep):
            one = sums_of["A"]
            got = down_grad(2 * ours[2 * n:2 * n + 2] + ring.core, act, ddown, one.from_core[2 * n:2 * n + 2], dep)
            return one.rest(got) if n else one.out(got)
        return step

    def slope_step(dep):
        made["dupper"], made["upb"] = slope_back(ddown, slope, w_down, dep)
        return [made["upb"]]

    def middle(dep):
        made["dres1"], made["dattn"], made["dctx"], made["small1"] = middle_back(
            made["dupper"], w_up, dres, hat1, sc1, norm1_gain, w_out, dep)
        return [made["small1"]]

    def attention(s):
        def step(dep):
            made[s] = attend_back(s, lengths, q, k, v, made["dctx"], lse, span, dep)
            return [made[s][3]]
        return step

    def last_inputs():
        parts = [v for s in range(seqs) for v in made[s][:3]]
        smalls = [made[s][k] for k in (3, 4) for s in range(seqs)] + [made["small1"], made["upb"], small2]
        return made["dattn"], smalls, parts

    def last_send(n):
        def step(dep):
            return sums_of["C"].core(last_grad(other, theirs[2 * n:2 * n + 2], x, ctx, *last_inputs(), dep=dep))
        return step

    def last_keep(n):
        def step(dep):
            one = sums_of["C"]
            (got,) = last_grad(mine, ours[2 * n:2 * n + 2], x, ctx, *last_inputs(), one.from_core[2 * n:2 * n + 2], dep)
            return one.rest(got) if n else one.out(got)
        return step

    def token(dep):
        made["tokens"] = token_grad(made["dres1"], w_qkv, [v for s in range(seqs) for v in made[s][:3]], dep)
        return [made["tokens"]]

    def up_send(name):
        def step(dep):
            return sums_of[name].core(up_grad(other, hid_t, made["dupper"], COLUMNS[name], dep=dep))
        return step

    def up_keep(name):
        def step(dep):
            one = sums_of[name]
            return one.out(*up_grad(mine, hid_t, made["dupper"], COLUMNS[name], place, one.from_core, dep))
        return step

    def copy_down(dep):
        rows = ff // 8
        (made["A"],) = spread(sums_of["A"].whole, 8, [(i * rows, rows, 0, i * rows, 0) for i in range(8)],
                              [shape((ff, width), F32)], dep=dep)
        return [made["A"]]

    def copy_up(dep):
        rows = width // 8
        (made["B"],) = spread(sums_of["B"].whole, 8, [(i * rows, rows, 0, i * rows, 0) for i in range(8)],
                              [shape((width, ff), F32)], dep=dep)
        return [made["B"]]

    def cut_last(dep):
        rows, size = width // 2, width // 2 + MORE
        moves = [(i * size, rows, i // 6, i % 2 * rows, (i // 2 % 3) * width) for i in range(8)]
        lines = [(rows + i, 1) for i in range(5)] + [(rows + 5, ff // width)]
        lines += [(rows + 5 + ff // width + i, 1) for i in range(3)]
        made["C"] = spread(sums_of["C"].whole, 8, moves, [shape((width, 3 * width), F32), shape((width, width), F32)],
                           lines, dep)
        return [made["C"][1]]

    steps = {"slope": slope_step, "middle": middle, "token": token, "copy_down": copy_down, "copy_up": copy_up,
             "cut_last": cut_last}
    for n in range(2):
        steps.update({f"down_s{n}": down_send(n), f"down_k{n}": down_keep(n),
                      f"last_s{n}": last_send(n), f"last_k{n}": last_keep(n)})
    steps.update({f"ab{s}": attention(s) for s in range(seqs)})
    for name in COLUMNS:
        steps["ups" + name], steps["upk" + name] = up_send(name), up_keep(name)
    dep = []
    for word in ORDER:
        what, _, name = word.partition(":")
        if what == "all":
            dep = dep + [sums_of[name].whole]
        elif name:
            dep = getattr(sums_of[name], what)(dep)
        else:
            dep = steps[what](dep)
    up = [sums_of[name].whole for name in COLUMNS]
    up = made["B"] if "B" in made else up[0] if len(up) == 1 else jnp.concatenate(up, axis=1)
    down = made["A"] if "A" in made else sums_of["A"].whole
    qkv, out, q_sum, v_sum, out_sum, gain1, shift1, up_sum, gain2, shift2, down_sum = made["C"]
    return (loss[0, 0], made["tokens"].reshape(tokens.shape), qkv, q_sum, v_sum, out, out_sum, gain1, shift1,
            up, up_sum, down, down_sum, gain2, shift2)


def solution(mesh):
    split = P("tower", "dp", None, None)
    in_specs = (split, P("tower", "dp")) + (P(),) * 14
    out_specs = (P(), split) + (P(),) * 13
    body = partial(local, mesh.shape["dp"], mesh.shape["tower"])
    return jax.shard_map(body, mesh=mesh, in_specs=in_specs, out_specs=out_specs, check_vma=False)
```

```python
from functools import partial

import jax
import jax.numpy as jnp
from jax import lax
from jax.experimental import pallas as pl
from jax.experimental.pallas import tpu as pltpu
from jax.sharding import PartitionSpec as P

HD = 64
SOFTMAX_TEMP = 0.01
NORM_EPS = 1e-06
MASKED = -1e30
F32 = jnp.float32
BF16 = jnp.bfloat16
ROOT_HALF = 0.7071067811865476
INV_ROOT_2PI = 0.3989422804014327
MIB = 1024 * 1024

SMEM = pl.BlockSpec(memory_space=pltpu.SMEM)
VMEM = pl.BlockSpec(memory_space=pltpu.VMEM)
ANY = pl.BlockSpec(memory_space=pl.ANY)


SCALE = 6.0
MICROSECONDS = {"down_send": 4, "down_keep": 5, "slope_back": 13, "up_send": 8, "up_keep": 10, "middle_back": 16,
                "attend_back": 12, "last_send": 4, "last_keep": 5, "token_grad": 9, "add_split": 4, "add": 2,
                "gather": 5}


def cost(name):
    return pl.CostEstimate(flops=max(1, int(1.1e9 * SCALE * MICROSECONDS.get(name, 1))), bytes_accessed=1, transcendentals=0)


def params():
    return pltpu.CompilerParams(vmem_limit_bytes=62 * MIB)


def call(body, dep, grid, in_specs, out_specs, out_shape, scratch=(), scalars=0, name=None, aliases=None):
    dep = [] if dep is None else list(dep)
    n_in = scalars + len(in_specs)

    def run(*refs):
        return body(*refs[:n_in], *refs[n_in + len(dep):])

    spec = pltpu.PrefetchScalarGridSpec(
        num_scalar_prefetch=scalars, grid=grid, in_specs=list(in_specs) + [ANY] * len(dep),
        out_specs=out_specs, scratch_shapes=scratch)
    made = pl.pallas_call(run, grid_spec=spec, out_shape=out_shape, compiler_params=params(), cost_estimate=cost(name),
                          input_output_aliases=aliases or {}, name=name)
    return lambda *args: made(*args, *dep)


def shape(dims, kind):
    return jax.ShapeDtypeStruct(dims, kind)


def line(cols, index=lambda *_: (0,)):
    return pl.BlockSpec((cols,), index)


def row(ref):
    return ref[...].reshape(1, -1)


def fixed(dims):
    return pl.BlockSpec(dims, lambda *_: (0,) * len(dims), pipeline_mode=pl.Buffered(1))


def dot(a, b, ca=1, cb=0):
    return lax.dot_general(a, b, (((ca,), (cb,)), ((), ())), preferred_element_type=F32)


def key_mask(count, span):
    place = lax.broadcasted_iota(jnp.int32, (span, 1), 0)
    return jnp.where(place < count, 0.0, MASKED)


def attend_body(seqs, span, group, counts, x, wq, wk, wv, qb, vb, q_out, k_out, v_out, ctx, lse):
    q_out[...] = (dot(x[...], wq[...]) + row(qb)).astype(BF16)
    k_out[...] = dot(x[...], wk[...]).astype(BF16)
    v_out[...] = (dot(x[...], wv[...]) + row(vb)).astype(BF16)
    for s in range(seqs):
        rows = pl.ds(s * span, span)
        mask = key_mask(counts[0, s], span)
        for pair in range(group // 2):
            both = []
            for half in range(2):
                head = pair * 2 + half
                lanes = pl.ds(head * HD, HD)
                query = q_out[rows, lanes] * HD ** (-0.5)
                scores = dot(k_out[rows, lanes], query, 1, 1) + mask
                highest = jnp.max(scores, axis=0, keepdims=True)
                expo = jnp.exp(scores - highest)
                summed = jnp.sum(expo, axis=0, keepdims=True)
                both.append(dot(v_out[rows, lanes], expo.astype(BF16), 0, 0) * (1.0 / summed))
                lse[0, s, pl.ds(head, 1), :] = highest + jnp.log(summed)
            both = jnp.concatenate(both, axis=0)
            ctx[rows, pl.ds(pair * 2 * HD, 2 * HD)] = both.T.astype(BF16)


def attend(counts, x, w_qkv, q_bias, v_bias, seqs, span):
    rows, width = x.shape
    group = 4
    cols = group * HD
    steps = width // cols
    piece = pl.BlockSpec((rows, cols), lambda g: (0, g))
    bias = line(cols, lambda g: (g,))
    weight = [pl.BlockSpec((width, cols), lambda g, k=k: (0, k * steps + g)) for k in range(3)]
    return pl.pallas_call(
        partial(attend_body, seqs, span, group),
        grid=(steps,),
        in_specs=[SMEM, fixed((rows, width)), *weight, bias, bias],
        out_specs=[piece] * 4 + [pl.BlockSpec((1, seqs, group, span), lambda g: (g, 0, 0, 0))],
        out_shape=[shape((rows, width), BF16)] * 4 + [shape((steps, seqs, group, span), F32)],
        compiler_params=params(),
        cost_estimate=cost(""),
        name="attend",
    )(counts, x, w_qkv, w_qkv, w_qkv, q_bias, v_bias)


def norm_parts(value):
    centre = value - jnp.mean(value, axis=-1, keepdims=True)
    spread = jnp.mean(centre * centre, axis=-1, keepdims=True)
    scale = lax.rsqrt(spread + NORM_EPS)
    return centre * scale, scale


def gelu_parts(u):
    bell = jnp.exp(-0.5 * (u * u))
    cdf = 0.5 + 0.5 * lax.erf(u * ROOT_HALF)
    return u * cdf, cdf + u * (INV_ROOT_2PI * bell)


def feed_body(tile, span, chunk, counts, x, ctx, w_out, w_up, w_down, ob, g1, b1, ub, db, g2, b2,
              hid_t, hat1, sc1, act, slope, hat2, sc2, sums, pooled):
    step = pl.program_id(0)
    attn = dot(ctx[...], w_out[...]) + row(ob)
    xhat, scale = norm_parts(x[...].astype(F32) + attn)
    hat1[...] = xhat
    sc1[...] = scale
    hidden = xhat * row(g1) + row(b1)
    low = hidden.astype(BF16)
    hid_t[...] = low.T
    total = hidden + row(db)
    for j in range(w_up.shape[1] // chunk):
        cols = pl.ds(j * chunk, chunk)
        upper = dot(low, w_up[:, cols]) + ub[cols].reshape(1, chunk)
        active, grad = gelu_parts(upper)
        active = active.astype(BF16)
        act[:, cols] = active
        slope[:, cols] = grad.astype(slope.dtype)
        total = total + dot(active, w_down[cols, :])
    xhat, scale = norm_parts(total)
    hat2[...] = xhat
    sc2[...] = scale
    seq = step * tile // span
    place = lax.broadcasted_iota(jnp.int32, (tile, 1), 0) + lax.rem(step * tile, span)
    part = jnp.sum(jnp.where(place < counts[0, seq], xhat, 0.0), axis=0, keepdims=True)

    @pl.when(step == 0)
    def _():
        sums[...] = jnp.zeros_like(sums)

    sums[pl.ds(seq, 1), :] += part

    @pl.when(step == pl.num_programs(0) - 1)
    def _():
        for s in range(sums.shape[0]):
            pooled[s:s + 1, :] = sums[s:s + 1, :] * row(g2) / counts[0, s].astype(F32) + row(b2)


def feed(counts, x, ctx, w_out, w_up, w_down, ob, g1, b1, ub, db, g2, b2, seqs, span, slope_kind):
    rows, width = x.shape
    ff = w_up.shape[1]
    tile = 256
    by = lambda cols: pl.BlockSpec((tile, cols), lambda i: (i, 0))
    return pl.pallas_call(
        partial(feed_body, tile, span, 768),
        grid=(rows // tile,),
        in_specs=[SMEM, by(width), by(width), fixed((width, width)), fixed((width, ff)), fixed((ff, width)),
                  line(width), line(width), line(width), line(ff), line(width), line(width), line(width)],
        out_specs=[pl.BlockSpec((width, tile), lambda i: (0, i)), by(width), by(1), by(ff), by(ff), by(width), by(1),
                   pl.BlockSpec((seqs, width), lambda i: (0, 0)), pl.BlockSpec((seqs, width), lambda i: (0, 0))],
        out_shape=[shape((width, rows), BF16), shape((rows, width), F32), shape((rows, 1), F32),
                   shape((rows, ff), BF16), shape((rows, ff), slope_kind), shape((rows, width), F32),
                   shape((rows, 1), F32), shape((seqs, width), F32), shape((seqs, width), F32)],
        compiler_params=params(),
        cost_estimate=cost(""),
        name="feed",
    )(counts, x, ctx, w_out, w_up, w_down, ob, g1, b1, ub, db, g2, b2)


def loss_body(n_dp, towers, seqs, span, bits, counts, own, pos, low, high, sums, g2, hat_from, sc2,
              loss, dres_to, ddown_to, small, scratch, hat2, dres, ddown, sems):
    count = n_dp * towers * seqs
    pairs = pos.shape[0]
    tile = span // 2
    total_rows = seqs * span
    reads = [pltpu.make_async_copy(hat_from.at[pl.ds(i, tile), :], hat2.at[pl.ds(i, tile), :], sems.at[0, i // tile])
             for i in range(0, total_rows, tile)]
    for copy in reads:
        copy.start()
    writes = []
    rows = jnp.concatenate([low[...], high[...]], axis=0)
    inv = lax.rsqrt(jnp.sum(rows * rows, axis=-1, keepdims=True) + NORM_EPS)
    unit = rows * inv
    full = lax.Precision.HIGHEST
    logits = lax.dot_general(unit, unit, (((1,), (1,)), ((), ())), precision=full,
                             preferred_element_type=F32) / SOFTMAX_TEMP

    def place(i):
        block, j = i // seqs, lax.rem(i, seqs)
        device = jnp.full_like(block, own[0, 0])
        for n, bit in enumerate(bits):
            device = device ^ (((block >> n) & 1) * bit)
        dp, tower = device // towers, lax.rem(device, towers)
        half = towers // 2
        return tower < half, lax.rem(tower, half) * (n_dp * seqs) + dp * seqs + j

    is_query, query = place(lax.broadcasted_iota(jnp.int32, (count, 1), 0))
    key_is_query, key = place(lax.broadcasted_iota(jnp.int32, (1, count), 1))
    is_key = jnp.logical_not(key_is_query)
    lookup = lax.broadcasted_iota(jnp.int32, (count, pairs), 1) == query
    wanted = jnp.sum(jnp.where(lookup, row(pos).astype(F32), 0.0), axis=1, keepdims=True)
    hit = (key.astype(F32) == wanted) & is_key & is_query
    inside = is_key & is_query
    shown = jnp.where(is_key, logits, MASKED)
    highest = jnp.max(shown, axis=1, keepdims=True)
    expo = jnp.where(inside, jnp.exp(shown - highest), 0.0)
    summed = jnp.sum(expo, axis=1, keepdims=True)
    safe = jnp.where(is_query, summed, 1.0)
    picked = jnp.sum(jnp.where(hit, logits, 0.0), axis=1, keepdims=True)
    each = jnp.where(is_query, highest + jnp.log(safe) - picked, 0.0)
    loss[...] = jnp.sum(each, axis=0, keepdims=True) / pairs
    grad = (expo / safe - jnp.where(hit, 1.0, 0.0)) / (pairs * SOFTMAX_TEMP)
    dunit = lax.dot_general(grad, unit, (((1,), (0,)), ((), ())), precision=full, preferred_element_type=F32)
    dunit += lax.dot_general(grad, unit, (((0,), (0,)), ((), ())), precision=full, preferred_element_type=F32)
    inner = jnp.sum(dunit * rows, axis=-1, keepdims=True)
    scratch[...] = inv * dunit - rows * (inv * inv * inv * inner)

    width = rows.shape[1]
    small[...] = jnp.zeros_like(small)
    for s in range(seqs):
        pooled = scratch[pl.ds(s, 1), :]
        n = counts[0, s]
        dout = pooled / n.astype(F32)
        small[0:1, :] += dout * sums[s:s + 1, :]
        small[1:2, :] += pooled
        dhat = dout * row(g2)
        first = jnp.mean(dhat, axis=-1, keepdims=True)
        total = jnp.zeros((1, width), F32)
        for part in range(2):
            at = pl.ds(s * span + part * tile, tile)
            reads[s * 2 + part].wait()
            xhat = hat2[at, :]
            second = jnp.mean(dhat * xhat, axis=-1, keepdims=True)
            live = lax.broadcasted_iota(jnp.int32, (tile, 1), 0) + part * tile < n
            scale = jnp.where(live, sc2[at, :], 0.0)
            value = scale * (dhat - first - xhat * second)
            dres[at, :] = value
            low = value.astype(BF16)
            ddown[at, :] = low
            total += jnp.sum(low.astype(F32), axis=0, keepdims=True)
            for k, (left, to) in enumerate(((dres, dres_to), (ddown, ddown_to))):
                writes.append(pltpu.make_async_copy(left.at[at, :], to.at[at, :], sems.at[1 + k, s * 2 + part]))
                writes[-1].start()
        small[2:3, :] += total
    for copy in writes:
        copy.wait()


def loss_step(counts, own, pos, low, high, sums, g2, hat2, sc2, n_dp, towers, seqs, span, bits):
    rows, width = hat2.shape
    return pl.pallas_call(
        partial(loss_body, n_dp, towers, seqs, span, bits),
        in_specs=[SMEM, SMEM] + [VMEM] * 5 + [ANY, VMEM],
        out_specs=[VMEM, ANY, ANY, VMEM],
        out_shape=[shape((1, 1), F32), shape((rows, width), F32), shape((rows, width), BF16), shape((8, width), F32)],
        scratch_shapes=[pltpu.VMEM((2 * low.shape[0], width), F32), pltpu.VMEM((rows, width), F32),
                        pltpu.VMEM((rows, width), F32), pltpu.VMEM((rows, width), BF16),
                        pltpu.SemaphoreType.DMA((3, 2 * seqs))],
        compiler_params=params(),
        cost_estimate=cost(""),
        name="loss",
    )(counts, own, pos, low, high, sums, g2, hat2, sc2)


def slope_body(ddown, slope, w_down, dupper, upb):
    value = (slope[...].astype(F32) * dot(ddown[...], w_down[...], 1, 1)).astype(BF16)
    dupper[...] = value
    upb[...] = jnp.sum(value.astype(F32), axis=0, keepdims=True)


def slope_back(ddown, slope, w_down, dep):
    rows, width = ddown.shape
    ff = slope.shape[1]
    tile = 768
    by = pl.BlockSpec((rows, tile), lambda i: (0, i))
    return call(
        slope_body, dep, (ff // tile,), [fixed((rows, width)), by, pl.BlockSpec((tile, width), lambda i: (i, 0))],
        [by, pl.BlockSpec((1, tile), lambda i: (0, i))], [shape((rows, ff), BF16), shape((1, ff), F32)],
        name="slope_back",
    )(ddown, slope, w_down)


def share(value, j, place, send, keep):
    rows = value.shape[0]

    @pl.when(place[j] < 2)
    def _():
        send[pl.ds(pl.multiple_of(place[j] * rows, rows), rows), :] = value

    @pl.when(place[j] >= 2)
    def _():
        keep[pl.ds(pl.multiple_of((place[j] - 2) * rows, rows), rows), :] = value


def up_send_body(which, a0, a1, a2, a3, b, *outs):
    value = dot(jnp.concatenate([a0[...], a1[...], a2[...], a3[...]], axis=0), b[...])
    rows = a0.shape[0]
    for j in range(4):
        outs[j][...] = value[j * rows:(j + 1) * rows]


def up_keep_body(which, place, a0, a1, a2, a3, b, *rest):
    came, (send, keep) = rest[:4], rest[4:]
    value = dot(jnp.concatenate([a0[...], a1[...], a2[...], a3[...]], axis=0), b[...])
    rows = a0.shape[0]
    for j in range(4):
        share(value[j * rows:(j + 1) * rows] + came[j][...], j, place, send, keep)


def up_grad(which, a, b, columns, place=None, came=None, dep=None):
    m, k = a.shape
    start, n = columns
    rows, tile = m // 8, 768
    ins = [pl.BlockSpec((rows, k), lambda i, w, *_, j=j: (2 * j + w[0], 0)) for j in range(4)]
    ins.append(pl.BlockSpec((k, tile), lambda i, *_: (0, i + start // tile)))
    by = lambda r: pl.BlockSpec((r, tile), lambda i, *_: (0, i))
    if came is None:
        return call(up_send_body, dep, (n // tile,), ins, [by(rows)] * 4, [shape((rows, n), F32)] * 4, scalars=1,
                    name="up_send")(which, a, a, a, a, b)
    return call(up_keep_body, dep, (n // tile,), ins + [by(rows)] * 4, [by(m // 4)] * 2,
                [shape((m // 4, n), F32)] * 2, scalars=2, name="up_keep")(which, place, a, a, a, a, b, *came)


def down_send_body(blocks, a, b, *outs):
    value = dot(a[...], b[...], 0, 0)
    for j, out in enumerate(outs):
        @pl.when(pl.program_id(0) == j)
        def _(out=out):
            out[...] = value


def down_keep_body(blocks, a, b, *rest):
    came, out = rest[:2], rest[2]
    value = dot(a[...], b[...], 0, 0)
    for j, one in enumerate(came):
        @pl.when(pl.program_id(0) == j)
        def _(one=one):
            out[...] = value + one[...]


def down_grad(blocks, a, b, came=None, dep=None):
    rows, m = a.shape
    n = b.shape[1]
    tile = m // 8
    block = (tile, n)
    ins = [pl.BlockSpec((rows, tile), lambda i, w: (0, w[i])), fixed((rows, n))]
    if came is None:
        return call(down_send_body, dep, (2,), ins, [pl.BlockSpec(block, lambda i, w: (0, 0))] * 2, [shape(block, F32)] * 2,
                    scalars=1, name="down_send")(blocks, a, b)
    return call(down_keep_body, dep, (2,), ins + [fixed(block)] * 2, pl.BlockSpec(block, lambda i, w: (i, 0)),
                shape((2 * tile, n), F32), scalars=1, name="down_keep")(blocks, a, b, *came)


MORE = 16


def last_small(which, kind, smalls):
    width = smalls[-1].shape[1]
    small1, upb, small2 = (v[...] for v in smalls[-3:])
    sums = [v[...] for v in smalls[:-3]]
    seqs = len(sums) // 2
    lines = [sum(sums[:seqs]), sum(sums[seqs:]), small1[:3]]
    lines += [upb[:, i:i + width] for i in range(0, upb.shape[1], width)] + [small2[:3]]
    lines = jnp.concatenate(lines, axis=0)
    lines = jnp.concatenate([lines, jnp.zeros((MORE - lines.shape[0], width), F32)], axis=0)
    return jnp.where((which[0] == 0) & (kind == 0), lines, 0.0)


def last_body(seqs, keeping, which, kinds, *refs):
    refs = list(refs)
    x, ctx, dattn = refs[:3]
    smalls, refs = refs[3:2 * seqs + 6], refs[2 * seqs + 6:]
    came, refs = (refs[:2], refs[2:]) if keeping else (None, refs)
    parts, refs = refs[:3 * seqs], refs[3 * seqs:]
    outs, refs = (refs[:1], refs[1:]) if keeping else (refs[:2], refs[2:])
    left, right, held, done, sems = refs
    half = left.shape[2]
    span = parts[0].shape[0]
    size = half + MORE
    cols = pl.ds(pl.multiple_of(which[0] * half, half), half)

    def reads(n, act):
        for kind in range(4):
            def load(kind=kind):
                act(pltpu.make_async_copy((ctx if kind == 3 else x).at[:, cols], left.at[n], sems.at[0, n]))
                if kind == 3:
                    act(pltpu.make_async_copy(dattn, right.at[n], sems.at[1, n]))
                else:
                    for s in range(seqs):
                        act(pltpu.make_async_copy(
                            parts[s * 3 + kind], right.at[n, pl.ds(s * span, span), :], sems.at[1 + s, n]))
            pl.when(kinds[n] == kind)(load)
        if keeping:
            act(pltpu.make_async_copy(came[n], held.at[n], sems.at[seqs + 1, n]))

    for n in range(2):
        reads(n, lambda copy: copy.start())
    writes = []
    for n in range(2):
        reads(n, lambda copy: copy.wait())
        value = dot(left[n], right[n], 0, 0)
        extra = last_small(which, kinds[n], smalls)
        if keeping:
            value = value + held[n, pl.ds(0, half), :]
            extra = extra + held[n, pl.ds(half, MORE), :]
        done[n, pl.ds(0, half), :] = value
        done[n, pl.ds(half, MORE), :] = extra
        to = outs[0].at[pl.ds(n * size, size), :] if keeping else outs[n]
        writes.append(pltpu.make_async_copy(done.at[n], to, sems.at[seqs + 2, n]))
        writes[-1].start()
    for copy in writes:
        copy.wait()


def last_grad(which, kinds, x, ctx, dattn, smalls, parts, came=None, dep=None):
    rows, width = x.shape
    half = width // 2
    size = half + MORE
    seqs = len(parts) // 3
    keeping = came is not None
    scratch = [pltpu.VMEM((2, rows, half), BF16), pltpu.VMEM((2, rows, width), BF16), pltpu.VMEM((2, size, width), F32),
               pltpu.VMEM((2, size, width), F32), pltpu.SemaphoreType.DMA((seqs + 3, 2))]
    ins = [ANY] * 3 + [VMEM] * len(smalls) + [ANY] * (len(parts) + (2 if keeping else 0))
    outs = [shape((2 * size, width), F32)] if keeping else [shape((size, width), F32)] * 2
    made = call(partial(last_body, seqs, keeping), dep, (), ins, [ANY] * len(outs), outs, scratch=scratch,
                scalars=2, name="last_keep" if keeping else "last_send")
    return made(which, kinds, x, ctx, dattn, *smalls, *(came if keeping else []), *parts)


def middle_body(dupper, w_up, dres, hat1, sc1, g1, w_out, dres1, dattn, dctx, small):
    dhid = dres[...] + dot(dupper[...], w_up[...], 1, 1)
    xhat = hat1[...]

    @pl.when(pl.program_id(0) == 0)
    def _():
        small[...] = jnp.zeros_like(small)

    small[1:2, :] += jnp.sum(dhid * xhat, axis=0, keepdims=True)
    small[2:3, :] += jnp.sum(dhid, axis=0, keepdims=True)
    dhat = dhid * row(g1)
    first = jnp.mean(dhat, axis=-1, keepdims=True)
    second = jnp.mean(dhat * xhat, axis=-1, keepdims=True)
    value = sc1[...] * (dhat - first - xhat * second)
    dres1[...] = value
    low = value.astype(BF16)
    dattn[...] = low
    small[0:1, :] += jnp.sum(low.astype(F32), axis=0, keepdims=True)
    dctx[...] = dot(low, w_out[...], 1, 1).astype(BF16)


def middle_back(dupper, w_up, dres, hat1, sc1, g1, w_out, dep):
    rows, width = dres.shape
    ff = dupper.shape[1]
    tile = 256
    by = lambda cols: pl.BlockSpec((tile, cols), lambda i: (i, 0))
    return call(
        middle_body, dep, (rows // tile,),
        [by(ff), fixed((width, ff)), by(width), by(width), by(1), line(width), fixed((width, width))],
        [by(width), by(width), by(width),
         pl.BlockSpec((8, width), lambda i: (0, 0))],
        [shape((rows, width), F32), shape((rows, width), BF16), shape((rows, width), BF16),
         shape((8, width), F32)], name="middle_back",
    )(dupper, w_up, dres, hat1, sc1, g1, w_out)


def attend_back_body(seq, span, group, counts, q, k, v, dctx, lse, dq, dk, dv, qsum, vsum):
    mask = key_mask(counts[0, seq], span)
    for pair in range(group // 2):
        turned, keys, values = [], [], []
        for half in range(2):
            head = pair * 2 + half
            lanes = pl.ds(head * HD, HD)
            query = q[:, lanes] * HD ** (-0.5)
            key = k[:, lanes]
            grad = dctx[:, lanes]
            scores = dot(key, query, 1, 1) + mask
            probs = jnp.exp(scores - lse[0, 0, pl.ds(head, 1), :])
            dprobs = dot(v[:, lanes], grad, 1, 1)
            values.append(dot(probs.astype(BF16), grad))
            inner = jnp.sum(probs * dprobs, axis=0, keepdims=True)
            dscores = (probs * (dprobs - inner)).astype(BF16)
            keys.append(dot(dscores, query))
            turned.append(dot(key, dscores, 0, 0))
        cols = pl.ds(pair * 2 * HD, 2 * HD)
        low = (jnp.concatenate(turned, axis=0).T * HD ** (-0.5)).astype(BF16)
        dq[:, cols] = low
        qsum[:, cols] = jnp.sum(low.astype(F32), axis=0, keepdims=True)
        dk[:, cols] = jnp.concatenate(keys, axis=1).astype(BF16)
        low = jnp.concatenate(values, axis=1).astype(BF16)
        dv[:, cols] = low
        vsum[:, cols] = jnp.sum(low.astype(F32), axis=0, keepdims=True)


def attend_back(seq, counts, q, k, v, dctx, lse, span, dep):
    width = q.shape[1]
    group = 4
    cols = group * HD
    piece = pl.BlockSpec((span, cols), lambda g: (seq, g))
    mine = pl.BlockSpec((span, cols), lambda g: (0, g))
    sums = pl.BlockSpec((1, cols), lambda g: (0, g))
    return call(
        partial(attend_back_body, seq, span, group), dep, (width // cols,),
        [SMEM] + [piece] * 4 + [pl.BlockSpec((1, 1, group, span), lambda g: (g, seq, 0, 0))],
        [mine] * 3 + [sums] * 2, [shape((span, width), BF16)] * 3 + [shape((1, width), F32)] * 2, name="attend_back",
    )(counts, q, k, v, dctx, lse)


def token_body(dres1, wq, wk, wv, *rest):
    parts, out = rest[:-1], rest[-1]
    for s in range(len(parts) // 3):
        at = pl.ds(s * parts[0].shape[0], parts[0].shape[0])
        total = dres1[at, :]
        for part, weight in zip(parts[s * 3:s * 3 + 3], (wq, wk, wv)):
            total = total + dot(part[...], weight[...], 1, 1)
        out[at, :] = total


def token_grad(dres1, w_qkv, parts, dep):
    rows, width = dres1.shape
    span = parts[0].shape[0]
    tile = 256
    by = pl.BlockSpec((rows, tile), lambda i: (0, i))
    weight = [pl.BlockSpec((tile, width), lambda i, k=k: (i, k)) for k in range(3)]
    return call(token_body, dep, (width // tile,), [by, *weight] + [fixed((span, width))] * len(parts), by,
                shape((rows, width), F32), name="token_grad")(dres1, w_qkv, w_qkv, w_qkv, *parts)


def add_split_body(steps, bit, held, came, send, keep):
    step = pl.program_id(0)
    value = held[...] + came[...]

    @pl.when(step < steps)
    def _():
        send[...] = value

    @pl.when(step >= steps)
    def _():
        keep[...] = value


def block_rows(rows, cols):
    best = 8
    for r in range(8, rows + 1, 8):
        if rows % r == 0 and r * cols * 4 <= MIB:
            best = r
    return best


def add_split(bit, held, came, dep=None):
    rows, cols = held.shape
    half = rows // 2
    tile = block_rows(half, cols)
    steps = half // tile

    def at(i, b):
        first = i < steps
        return jnp.where(first, (1 - b[0]) * steps + i, b[0] * steps + i - steps), 0

    block = (tile, cols)
    return call(
        partial(add_split_body, steps), dep, (2 * steps,), [pl.BlockSpec(block, at)] * 2,
        [pl.BlockSpec(block, lambda i, b: (jnp.minimum(i, steps - 1), 0)),
         pl.BlockSpec(block, lambda i, b: (jnp.maximum(i - steps, 0), 0))],
        [shape((half, cols), F32)] * 2, scalars=1, name="add_split",
    )(bit, held, came)


def add_body(held, came, out):
    out[...] = held[...] + came[...]


def add(held, came, dep=None):
    rows, cols = held.shape
    tile = block_rows(rows, cols)
    spec = pl.BlockSpec((tile, cols), lambda i: (i, 0))
    return call(add_body, dep, (rows // tile,), [spec] * 2, spec, shape((rows, cols), F32), name="add")(held, came)


def gather_body(n, places, *refs):
    pieces, out, (held, in_sems, out_sems) = refs[:n], refs[n], refs[n + 1:]
    rows = pieces[0].shape[0]
    reads = [pltpu.make_async_copy(piece, held.at[i], in_sems.at[i]) for i, piece in enumerate(pieces)]
    for copy in reads:
        copy.start()
    writes = []
    for i in range(n):
        reads[i].wait()
        at = pl.multiple_of(places[i] * rows, 8)
        writes.append(pltpu.make_async_copy(held.at[i], out.at[pl.ds(at, rows), :], out_sems.at[i]))
        writes[-1].start()
    for copy in writes:
        copy.wait()


def gather(places, pieces, dep=None):
    n = len(pieces)
    rows, cols = pieces[0].shape
    return call(
        partial(gather_body, n), dep, (), [SMEM] + [ANY] * n, ANY, shape((n * rows, cols), F32),
        scratch=[pltpu.VMEM((n, rows, cols), F32), pltpu.SemaphoreType.DMA((n,)), pltpu.SemaphoreType.DMA((n,))],
        name="gather",
    )(places, *pieces)


def spread_body(blocks, moves, lines, whole, *refs):
    outs, (held, in_sems, out_sems) = refs[:-3], refs[-3:]
    size = whole.shape[0] // blocks
    cols = whole.shape[1]
    reads = [pltpu.make_async_copy(whole.at[pl.ds(i * size, size), :], held.at[pl.ds(i * size, size), :], in_sems.at[i])
             for i in range(blocks)]
    for copy in reads:
        copy.start()
    writes = []
    for i in range(blocks):
        reads[i].wait()
        first, rows, out, row, col = moves[i]
        copy = pltpu.make_async_copy(
            held.at[pl.ds(first, rows), :], outs[out].at[pl.ds(row, rows), pl.ds(col, cols)], out_sems.at[i])
        copy.start()
        writes.append(copy)
    first = len(outs) - len(lines)
    for out, (row, count) in zip(outs[first:], lines):
        for k in range(count):
            out[pl.ds(k * cols, cols)] = held[pl.ds(row + k, 1), :].reshape(cols)
    for copy in writes:
        copy.wait()


def spread(whole, blocks, moves, outs, lines=(), dep=None):
    cols = whole.shape[1]
    return call(
        partial(spread_body, blocks, moves, lines), dep, (), [ANY], [ANY] * len(outs) + [VMEM] * len(lines),
        list(outs) + [shape((count * cols,), F32) for _, count in lines],
        scratch=[pltpu.VMEM(whole.shape, F32), pltpu.SemaphoreType.DMA((blocks,)), pltpu.SemaphoreType.DMA((blocks,))],
        name="spread",
    )(whole)


COLUMNS = {"B": (0, 3072)}
AT_ONCE = ("A", "C")
ORDER = (
    "down_s0", "down_s1", "down_k0", "slope", "down_k1", "upsB", "a2:A", "middle", "a3:A", "upkB", "ab0", "a4:A",
    "ab1", "last_s0", "last_s1", "a2:B", "last_k0", "a5:A", "last_k1", "a3:B", "a4:B", "a2:C", "a5:B", "a3:C",
    "gE:B", "a4:C", "token", "h8:B", "h7:B", "h9:B", "a5:C", "copy_down", "fin:B", "cut_last",
)


class Ring:
    def __init__(self, n_dp, towers):
        self.n_dp, self.towers = n_dp, towers
        self.dp, self.tower = lax.axis_index("dp").astype(jnp.int32), lax.axis_index("tower").astype(jnp.int32)
        self.core = self.tower & 1
        x, y = self.x, self.y = self.dp & 1, (self.tower >> 1) & 1
        self.outer = jnp.where(self.core == 0, x, y)
        self.inner = jnp.where(self.core == 0, y, x)
        self.near = (self.dp >> 1) & 1
        self.far = [b for b in (4, 8, 16, 32, 64) if b < n_dp]

    def move(self, value, partner):
        pairs = []
        for dp in range(self.n_dp):
            for tower in range(self.towers):
                to_dp, to_tower = partner(dp, tower)
                pairs.append((dp * self.towers + tower, to_dp * self.towers + to_tower))
        return lax.ppermute(value, ("dp", "tower"), pairs)

    def place(self):
        out = []
        for bx in range(2):
            for by in range(2):
                outer, inner = jnp.where(self.core == 0, bx, by), jnp.where(self.core == 0, by, bx)
                out.append(jnp.where(outer == self.outer, 2, 0) + inner)
        return jnp.stack(out).astype(jnp.int32)

    def order(self, core):
        mine = jnp.where(core == 0, self.x, self.y)
        out = []
        for outer in (1 - mine, mine):
            for inner in range(2):
                out.append(jnp.where(core == 0, outer * 2 + inner, inner * 2 + outer))
        return jnp.stack(out).astype(jnp.int32)

    def bits(self):
        bits = [1]
        while bits[0] * 2 < self.n_dp * self.towers:
            bits.insert(0, bits[0] * 2)
        return bits

    def to_index(self, value, bit):
        count = self.n_dp * self.towers
        return lax.ppermute(value, ("dp", "tower"), [(i, i ^ bit) for i in range(count)])

    def gather(self, value):
        groups = []
        for far in range(self.n_dp // 4):
            groups.append([(far * 4 + near * 2 + x) * self.towers + y * 2 + core
                           for x in range(2) for y in range(2) for core in range(2) for near in range(2)])
        return lax.all_gather(value, ("dp", "tower"), axis_index_groups=groups, tiled=True)

    def along_z(self, value):
        far = self.n_dp // 2
        groups = [[(z * 2 + x) * self.towers + t for z in range(far)] for x in range(2) for t in range(self.towers)]
        return lax.psum(value, ("dp", "tower"), axis_index_groups=groups)

    def gather_plane(self, value):
        groups = [[(z * 2 + x) * self.towers + t for x in range(2) for t in range(self.towers)]
                  for z in range(self.n_dp // 2)]
        return lax.all_gather(value, ("dp", "tower"), axis_index_groups=groups, tiled=True)

    def to_core(self, value):
        return self.move(value, lambda d, t: (d, t ^ 1))

    def to_outer(self, value):
        return self.move(value, lambda d, t: (d, t ^ 2) if t & 1 else (d ^ 1, t))

    def to_inner(self, value):
        return self.move(value, lambda d, t: (d ^ 1, t) if t & 1 else (d, t ^ 2))

    def to_dp(self, value, bit):
        return self.move(value, lambda d, t: (d ^ bit, t))


class Sum:
    def __init__(self, ring, at_once):
        self.ring, self.at_once, self.from_core = ring, at_once, []

    def core(self, send):
        self.from_core += [self.ring.to_core(v) for v in send]
        return [send[0]]

    def out(self, send, keep=None):
        self.keep = keep
        self.came = self.ring.to_outer(send)
        return [send if keep is None else keep]

    def rest(self, keep):
        self.keep = keep
        return [keep]

    def a2(self, dep):
        send, self.keep = add_split(self.ring.inner.reshape(1), self.keep, self.came, dep)
        self.came = self.ring.to_inner(send)
        return [self.keep]

    def a3(self, dep):
        send, self.keep = add_split(self.ring.near.reshape(1), self.keep, self.came, dep)
        self.came = self.ring.to_dp(send, 2)
        return [self.keep]

    def z3(self, dep):
        self.keep = add(self.keep, self.came, dep)
        self.summed = self.ring.along_z(self.keep)
        return [self.keep]

    def z5(self, dep):
        self.whole = self.ring.gather_plane(self.summed)
        return dep + [self.summed]

    def a4(self, dep):
        self.keep = add(self.keep, self.came, dep)
        for bit in self.ring.far[:-1]:
            self.keep = self.keep + self.ring.to_dp(self.keep, bit)
        self.came = self.ring.to_dp(self.keep, self.ring.far[-1])
        return [self.keep]

    def a5(self, dep):
        self.keep = add(self.keep, self.came, dep)
        if self.at_once:
            self.whole = self.ring.gather(self.keep)
        else:
            self.came = self.ring.to_dp(self.keep, 2)
        return [self.keep]

    def gE(self, dep):
        ring = self.ring
        own = gather(jnp.stack([ring.near, 1 - ring.near]), [self.keep, self.came], dep)
        self.own, self.inner, self.outer = own, ring.to_inner(own), ring.to_outer(own)
        self.own_c = ring.to_core(own)
        return [own]

    def h7(self, dep):
        self.both, self.inner_c = self.ring.to_outer(self.inner), self.ring.to_core(self.inner)
        return dep + [self.inner]

    def h8(self, dep):
        self.outer_c = self.ring.to_core(self.outer)
        return dep + [self.outer]

    def h9(self, dep):
        self.both_c = self.ring.to_core(self.both)
        return dep + [self.both]

    def fin(self, dep):
        ring = self.ring
        pieces = [self.own, self.inner, self.outer, self.both, self.own_c, self.inner_c, self.outer_c, self.both_c]
        places = []
        for core in (ring.core, 1 - ring.core):
            inner_step = jnp.where(core == 0, 2, 4)
            base = ring.x * 4 + ring.y * 2
            places += [(base ^ step) + core for step in (0 * inner_step, inner_step, 6 - inner_step, 6 + 0 * inner_step)]
        self.whole = gather(jnp.stack(places), pieces, dep)
        return [self.whole]


def local(n_dp, towers, tokens, lengths, positive, w_qkv, q_bias, v_bias, w_out, out_bias, norm1_gain, norm1_bias,
          w_up, up_bias, w_down, down_bias, norm2_gain, norm2_bias):
    seqs, span, width = tokens.shape[1:]
    ff = up_bias.shape[0]
    x = tokens.reshape(seqs * span, width)
    ring = Ring(n_dp, towers)
    mine, other = ring.core.reshape(1), (1 - ring.core).reshape(1)
    place = ring.place()
    q, k, v, ctx, lse = attend(lengths, x, w_qkv, q_bias, v_bias, seqs, span)
    hid_t, hat1, sc1, act, slope, hat2, sc2, sums, pooled = feed(
        lengths, x, ctx, w_out, w_up, w_down, out_bias, norm1_gain, norm1_bias, up_bias, down_bias, norm2_gain,
        norm2_bias, seqs, span, BF16)
    every, bits = pooled, ring.bits()
    for pair in range(0, len(bits) - 1, 2):
        first, second = bits[pair:pair + 2]
        every = jnp.concatenate(
            [every] + [ring.to_index(every, bit) for bit in (first, second, first | second)], axis=0)
    for bit in bits[len(bits) // 2 * 2:-1]:
        every = jnp.concatenate([every, ring.to_index(every, bit)], axis=0)
    half = every.shape[0] // 2
    halves = (every, ring.to_index(every, bits[-1])) if len(bits) % 2 else (every[:half], every[half:])
    own = (lax.axis_index("dp") * towers + lax.axis_index("tower")).astype(jnp.int32).reshape(1, 1)
    loss, dres, ddown, small2 = loss_step(lengths, own, positive, *halves, sums, norm2_gain, hat2, sc2,
                                          n_dp, towers, seqs, span, bits)
    sums_of, made = {}, {}

    for name in ("A", "C", *COLUMNS):
        sums_of[name] = Sum(ring, name in AT_ONCE)
    theirs, ours = ring.order(1 - ring.core), ring.order(ring.core)

    def down_send(n):
        def step(dep):
            return sums_of["A"].core(down_grad(2 * theirs[2 * n:2 * n + 2] + 1 - ring.core, act, ddown, dep=dep))
        return step

    def down_keep(n):
        def step(dep):
            one = sums_of["A"]
            got = down_grad(2 * ours[2 * n:2 * n + 2] + ring.core, act, ddown, one.from_core[2 * n:2 * n + 2], dep)
            return one.rest(got) if n else one.out(got)
        return step

    def slope_step(dep):
        made["dupper"], made["upb"] = slope_back(ddown, slope, w_down, dep)
        return [made["upb"]]

    def middle(dep):
        made["dres1"], made["dattn"], made["dctx"], made["small1"] = middle_back(
            made["dupper"], w_up, dres, hat1, sc1, norm1_gain, w_out, dep)
        return [made["small1"]]

    def attention(s):
        def step(dep):
            made[s] = attend_back(s, lengths, q, k, v, made["dctx"], lse, span, dep)
            return [made[s][3]]
        return step

    def last_inputs():
        parts = [v for s in range(seqs) for v in made[s][:3]]
        smalls = [made[s][k] for k in (3, 4) for s in range(seqs)] + [made["small1"], made["upb"], small2]
        return made["dattn"], smalls, parts

    def last_send(n):
        def step(dep):
            return sums_of["C"].core(last_grad(other, theirs[2 * n:2 * n + 2], x, ctx, *last_inputs(), dep=dep))
        return step

    def last_keep(n):
        def step(dep):
            one = sums_of["C"]
            (got,) = last_grad(mine, ours[2 * n:2 * n + 2], x, ctx, *last_inputs(), one.from_core[2 * n:2 * n + 2], dep)
            return one.rest(got) if n else one.out(got)
        return step

    def token(dep):
        made["tokens"] = token_grad(made["dres1"], w_qkv, [v for s in range(seqs) for v in made[s][:3]], dep)
        return [made["tokens"]]

    def up_send(name):
        def step(dep):
            return sums_of[name].core(up_grad(other, hid_t, made["dupper"], COLUMNS[name], dep=dep))
        return step

    def up_keep(name):
        def step(dep):
            one = sums_of[name]
            return one.out(*up_grad(mine, hid_t, made["dupper"], COLUMNS[name], place, one.from_core, dep))
        return step

    def copy_down(dep):
        rows = ff // 8
        (made["A"],) = spread(sums_of["A"].whole, 8, [(i * rows, rows, 0, i * rows, 0) for i in range(8)],
                              [shape((ff, width), F32)], dep=dep)
        return [made["A"]]

    def copy_up(dep):
        rows = width // 8
        (made["B"],) = spread(sums_of["B"].whole, 8, [(i * rows, rows, 0, i * rows, 0) for i in range(8)],
                              [shape((width, ff), F32)], dep=dep)
        return [made["B"]]

    def cut_last(dep):
        rows, size = width // 2, width // 2 + MORE
        moves = [(i * size, rows, i // 6, i % 2 * rows, (i // 2 % 3) * width) for i in range(8)]
        lines = [(rows + i, 1) for i in range(5)] + [(rows + 5, ff // width)]
        lines += [(rows + 5 + ff // width + i, 1) for i in range(3)]
        made["C"] = spread(sums_of["C"].whole, 8, moves, [shape((width, 3 * width), F32), shape((width, width), F32)],
                           lines, dep)
        return [made["C"][1]]

    steps = {"slope": slope_step, "middle": middle, "token": token, "copy_down": copy_down, "copy_up": copy_up,
             "cut_last": cut_last}
    for n in range(2):
        steps.update({f"down_s{n}": down_send(n), f"down_k{n}": down_keep(n),
                      f"last_s{n}": last_send(n), f"last_k{n}": last_keep(n)})
    steps.update({f"ab{s}": attention(s) for s in range(seqs)})
    for name in COLUMNS:
        steps["ups" + name], steps["upk" + name] = up_send(name), up_keep(name)
    dep = []
    for word in ORDER:
        what, _, name = word.partition(":")
        if what == "all":
            dep = dep + [sums_of[name].whole]
        elif name:
            dep = getattr(sums_of[name], what)(dep)
        else:
            dep = steps[what](dep)
    up = [sums_of[name].whole for name in COLUMNS]
    up = made["B"] if "B" in made else up[0] if len(up) == 1 else jnp.concatenate(up, axis=1)
    down = made["A"] if "A" in made else sums_of["A"].whole
    qkv, out, q_sum, v_sum, out_sum, gain1, shift1, up_sum, gain2, shift2, down_sum = made["C"]
    return (loss[0, 0], made["tokens"].reshape(tokens.shape), qkv, q_sum, v_sum, out, out_sum, gain1, shift1,
            up, up_sum, down, down_sum, gain2, shift2)


def solution(mesh):
    split = P("tower", "dp", None, None)
    in_specs = (split, P("tower", "dp")) + (P(),) * 14
    out_specs = (P(), split) + (P(),) * 13
    body = partial(local, mesh.shape["dp"], mesh.shape["tower"])
    return jax.shard_map(body, mesh=mesh, in_specs=in_specs, out_specs=out_specs, check_vma=False)
```

```python
from functools import partial

import jax
import jax.numpy as jnp
from jax import lax
from jax.experimental import pallas as pl
from jax.experimental.pallas import tpu as pltpu
from jax.sharding import PartitionSpec as P

HD = 64
SOFTMAX_TEMP = 0.01
NORM_EPS = 1e-06
MASKED = -1e30
F32 = jnp.float32
BF16 = jnp.bfloat16
ROOT_HALF = 0.7071067811865476
INV_ROOT_2PI = 0.3989422804014327
MIB = 1024 * 1024

SMEM = pl.BlockSpec(memory_space=pltpu.SMEM)
VMEM = pl.BlockSpec(memory_space=pltpu.VMEM)
ANY = pl.BlockSpec(memory_space=pl.ANY)


SCALE = 6.0
MICROSECONDS = {"down_send": 4, "down_keep": 5, "slope_back": 13, "up_send": 8, "up_keep": 10, "middle_back": 16,
                "attend_back": 12, "last_send": 4, "last_keep": 5, "token_grad": 9, "add_split": 4, "add": 2,
                "gather": 5}


def cost(name):
    return pl.CostEstimate(flops=max(1, int(1.1e9 * SCALE * MICROSECONDS.get(name, 1))), bytes_accessed=1, transcendentals=0)


def params(mib=62):
    return pltpu.CompilerParams(vmem_limit_bytes=mib * MIB)


def call(body, dep, grid, in_specs, out_specs, out_shape, scratch=(), scalars=0, name=None, aliases=None):
    dep = [] if dep is None else list(dep)
    n_in = scalars + len(in_specs)

    def run(*refs):
        return body(*refs[:n_in], *refs[n_in + len(dep):])

    spec = pltpu.PrefetchScalarGridSpec(
        num_scalar_prefetch=scalars, grid=grid, in_specs=list(in_specs) + [ANY] * len(dep),
        out_specs=out_specs, scratch_shapes=scratch)
    made = pl.pallas_call(run, grid_spec=spec, out_shape=out_shape, compiler_params=params(20 if name == "add" else 62), cost_estimate=cost(name),
                          input_output_aliases=aliases or {}, name=name)
    return lambda *args: made(*args, *dep)


def shape(dims, kind):
    return jax.ShapeDtypeStruct(dims, kind)


def line(cols, index=lambda *_: (0,)):
    return pl.BlockSpec((cols,), index)


def row(ref):
    return ref[...].reshape(1, -1)


def fixed(dims):
    return pl.BlockSpec(dims, lambda *_: (0,) * len(dims), pipeline_mode=pl.Buffered(1))


def dot(a, b, ca=1, cb=0):
    return lax.dot_general(a, b, (((ca,), (cb,)), ((), ())), preferred_element_type=F32)


def key_mask(count, span):
    place = lax.broadcasted_iota(jnp.int32, (span, 1), 0)
    return jnp.where(place < count, 0.0, MASKED)


def attend_body(seqs, span, group, counts, x, wq, wk, wv, qb, vb, q_out, k_out, v_out, ctx, lse):
    q_out[...] = (dot(x[...], wq[...]) + row(qb)).astype(BF16)
    k_out[...] = dot(x[...], wk[...]).astype(BF16)
    v_out[...] = (dot(x[...], wv[...]) + row(vb)).astype(BF16)
    for s in range(seqs):
        rows = pl.ds(s * span, span)
        mask = key_mask(counts[0, s], span)
        for pair in range(group // 2):
            both = []
            for half in range(2):
                head = pair * 2 + half
                lanes = pl.ds(head * HD, HD)
                query = q_out[rows, lanes] * HD ** (-0.5)
                scores = dot(k_out[rows, lanes], query, 1, 1) + mask
                highest = jnp.max(scores, axis=0, keepdims=True)
                expo = jnp.exp(scores - highest)
                summed = jnp.sum(expo, axis=0, keepdims=True)
                both.append(dot(v_out[rows, lanes], expo.astype(BF16), 0, 0) * (1.0 / summed))
                lse[0, s, pl.ds(head, 1), :] = highest + jnp.log(summed)
            both = jnp.concatenate(both, axis=0)
            ctx[rows, pl.ds(pair * 2 * HD, 2 * HD)] = both.T.astype(BF16)


def attend(counts, x, w_qkv, q_bias, v_bias, seqs, span):
    rows, width = x.shape
    group = 4
    cols = group * HD
    steps = width // cols
    piece = pl.BlockSpec((rows, cols), lambda g: (0, g))
    bias = line(cols, lambda g: (g,))
    weight = [pl.BlockSpec((width, cols), lambda g, k=k: (0, k * steps + g)) for k in range(3)]
    return pl.pallas_call(
        partial(attend_body, seqs, span, group),
        grid=(steps,),
        in_specs=[SMEM, fixed((rows, width)), *weight, bias, bias],
        out_specs=[piece] * 4 + [pl.BlockSpec((1, seqs, group, span), lambda g: (g, 0, 0, 0))],
        out_shape=[shape((rows, width), BF16)] * 4 + [shape((steps, seqs, group, span), F32)],
        compiler_params=params(),
        cost_estimate=cost(""),
        name="attend",
    )(counts, x, w_qkv, w_qkv, w_qkv, q_bias, v_bias)


def norm_parts(value):
    centre = value - jnp.mean(value, axis=-1, keepdims=True)
    spread = jnp.mean(centre * centre, axis=-1, keepdims=True)
    scale = lax.rsqrt(spread + NORM_EPS)
    return centre * scale, scale


def gelu_parts(u):
    bell = jnp.exp(-0.5 * (u * u))
    cdf = 0.5 + 0.5 * lax.erf(u * ROOT_HALF)
    return u * cdf, cdf + u * (INV_ROOT_2PI * bell)


def feed_body(tile, span, chunk, counts, x, ctx, w_out, w_up, w_down, ob, g1, b1, ub, db, g2, b2,
              hid_t, hat1, sc1, act, slope, hat2, sc2, sums, pooled):
    step = pl.program_id(0)
    attn = dot(ctx[...], w_out[...]) + row(ob)
    xhat, scale = norm_parts(x[...].astype(F32) + attn)
    hat1[...] = xhat
    sc1[...] = scale
    hidden = xhat * row(g1) + row(b1)
    low = hidden.astype(BF16)
    hid_t[...] = low.T
    total = hidden + row(db)
    for j in range(w_up.shape[1] // chunk):
        cols = pl.ds(j * chunk, chunk)
        upper = dot(low, w_up[:, cols]) + ub[cols].reshape(1, chunk)
        active, grad = gelu_parts(upper)
        active = active.astype(BF16)
        act[:, cols] = active
        slope[:, cols] = grad.astype(slope.dtype)
        total = total + dot(active, w_down[cols, :])
    xhat, scale = norm_parts(total)
    hat2[...] = xhat
    sc2[...] = scale
    seq = step * tile // span
    place = lax.broadcasted_iota(jnp.int32, (tile, 1), 0) + lax.rem(step * tile, span)
    part = jnp.sum(jnp.where(place < counts[0, seq], xhat, 0.0), axis=0, keepdims=True)

    @pl.when(step == 0)
    def _():
        sums[...] = jnp.zeros_like(sums)

    sums[pl.ds(seq, 1), :] += part

    @pl.when(step == pl.num_programs(0) - 1)
    def _():
        for s in range(sums.shape[0]):
            pooled[s:s + 1, :] = sums[s:s + 1, :] * row(g2) / counts[0, s].astype(F32) + row(b2)


def feed(counts, x, ctx, w_out, w_up, w_down, ob, g1, b1, ub, db, g2, b2, seqs, span, slope_kind):
    rows, width = x.shape
    ff = w_up.shape[1]
    tile = 256
    by = lambda cols: pl.BlockSpec((tile, cols), lambda i: (i, 0))
    return pl.pallas_call(
        partial(feed_body, tile, span, 768),
        grid=(rows // tile,),
        in_specs=[SMEM, by(width), by(width), fixed((width, width)), fixed((width, ff)), fixed((ff, width)),
                  line(width), line(width), line(width), line(ff), line(width), line(width), line(width)],
        out_specs=[pl.BlockSpec((width, tile), lambda i: (0, i)), by(width), by(1), by(ff), by(ff), by(width), by(1),
                   pl.BlockSpec((seqs, width), lambda i: (0, 0)), pl.BlockSpec((seqs, width), lambda i: (0, 0))],
        out_shape=[shape((width, rows), BF16), shape((rows, width), F32), shape((rows, 1), F32),
                   shape((rows, ff), BF16), shape((rows, ff), slope_kind), shape((rows, width), F32),
                   shape((rows, 1), F32), shape((seqs, width), F32), shape((seqs, width), F32)],
        compiler_params=params(),
        cost_estimate=cost(""),
        name="feed",
    )(counts, x, ctx, w_out, w_up, w_down, ob, g1, b1, ub, db, g2, b2)


def loss_body(n_dp, towers, seqs, span, bits, counts, own, pos, low, high, sums, g2, hat_from, sc2,
              loss, dres_to, ddown_to, small, scratch, hat2, dres, ddown, sems):
    count = n_dp * towers * seqs
    pairs = pos.shape[0]
    tile = span // 2
    total_rows = seqs * span
    reads = [pltpu.make_async_copy(hat_from.at[pl.ds(i, tile), :], hat2.at[pl.ds(i, tile), :], sems.at[0, i // tile])
             for i in range(0, total_rows, tile)]
    for copy in reads:
        copy.start()
    writes = []
    rows = jnp.concatenate([low[...], high[...]], axis=0)
    inv = lax.rsqrt(jnp.sum(rows * rows, axis=-1, keepdims=True) + NORM_EPS)
    unit = rows * inv
    full = lax.Precision.HIGHEST
    logits = lax.dot_general(unit, unit, (((1,), (1,)), ((), ())), precision=full,
                             preferred_element_type=F32) / SOFTMAX_TEMP

    def place(i):
        block, j = i // seqs, lax.rem(i, seqs)
        device = jnp.full_like(block, own[0, 0])
        for n, bit in enumerate(bits):
            device = device ^ (((block >> n) & 1) * bit)
        dp, tower = device // towers, lax.rem(device, towers)
        half = towers // 2
        return tower < half, lax.rem(tower, half) * (n_dp * seqs) + dp * seqs + j

    is_query, query = place(lax.broadcasted_iota(jnp.int32, (count, 1), 0))
    key_is_query, key = place(lax.broadcasted_iota(jnp.int32, (1, count), 1))
    is_key = jnp.logical_not(key_is_query)
    lookup = lax.broadcasted_iota(jnp.int32, (count, pairs), 1) == query
    wanted = jnp.sum(jnp.where(lookup, row(pos).astype(F32), 0.0), axis=1, keepdims=True)
    hit = (key.astype(F32) == wanted) & is_key & is_query
    inside = is_key & is_query
    shown = jnp.where(is_key, logits, MASKED)
    highest = jnp.max(shown, axis=1, keepdims=True)
    expo = jnp.where(inside, jnp.exp(shown - highest), 0.0)
    summed = jnp.sum(expo, axis=1, keepdims=True)
    safe = jnp.where(is_query, summed, 1.0)
    picked = jnp.sum(jnp.where(hit, logits, 0.0), axis=1, keepdims=True)
    each = jnp.where(is_query, highest + jnp.log(safe) - picked, 0.0)
    loss[...] = jnp.sum(each, axis=0, keepdims=True) / pairs
    grad = (expo / safe - jnp.where(hit, 1.0, 0.0)) / (pairs * SOFTMAX_TEMP)
    dunit = lax.dot_general(grad, unit, (((1,), (0,)), ((), ())), precision=full, preferred_element_type=F32)
    dunit += lax.dot_general(grad, unit, (((0,), (0,)), ((), ())), precision=full, preferred_element_type=F32)
    inner = jnp.sum(dunit * rows, axis=-1, keepdims=True)
    scratch[...] = inv * dunit - rows * (inv * inv * inv * inner)

    width = rows.shape[1]
    small[...] = jnp.zeros_like(small)
    for s in range(seqs):
        pooled = scratch[pl.ds(s, 1), :]
        n = counts[0, s]
        dout = pooled / n.astype(F32)
        small[0:1, :] += dout * sums[s:s + 1, :]
        small[1:2, :] += pooled
        dhat = dout * row(g2)
        first = jnp.mean(dhat, axis=-1, keepdims=True)
        total = jnp.zeros((1, width), F32)
        for part in range(2):
            at = pl.ds(s * span + part * tile, tile)
            reads[s * 2 + part].wait()
            xhat = hat2[at, :]
            second = jnp.mean(dhat * xhat, axis=-1, keepdims=True)
            live = lax.broadcasted_iota(jnp.int32, (tile, 1), 0) + part * tile < n
            scale = jnp.where(live, sc2[at, :], 0.0)
            value = scale * (dhat - first - xhat * second)
            dres[at, :] = value
            low = value.astype(BF16)
            ddown[at, :] = low
            total += jnp.sum(low.astype(F32), axis=0, keepdims=True)
            for k, (left, to) in enumerate(((dres, dres_to), (ddown, ddown_to))):
                writes.append(pltpu.make_async_copy(left.at[at, :], to.at[at, :], sems.at[1 + k, s * 2 + part]))
                writes[-1].start()
        small[2:3, :] += total
    for copy in writes:
        copy.wait()


def loss_step(counts, own, pos, low, high, sums, g2, hat2, sc2, n_dp, towers, seqs, span, bits):
    rows, width = hat2.shape
    return pl.pallas_call(
        partial(loss_body, n_dp, towers, seqs, span, bits),
        in_specs=[SMEM, SMEM] + [VMEM] * 5 + [ANY, VMEM],
        out_specs=[VMEM, ANY, ANY, VMEM],
        out_shape=[shape((1, 1), F32), shape((rows, width), F32), shape((rows, width), BF16), shape((8, width), F32)],
        scratch_shapes=[pltpu.VMEM((2 * low.shape[0], width), F32), pltpu.VMEM((rows, width), F32),
                        pltpu.VMEM((rows, width), F32), pltpu.VMEM((rows, width), BF16),
                        pltpu.SemaphoreType.DMA((3, 2 * seqs))],
        compiler_params=params(),
        cost_estimate=cost(""),
        name="loss",
    )(counts, own, pos, low, high, sums, g2, hat2, sc2)


def slope_body(ddown, slope, w_down, dupper, upb):
    value = (slope[...].astype(F32) * dot(ddown[...], w_down[...], 1, 1)).astype(BF16)
    dupper[...] = value
    upb[...] = jnp.sum(value.astype(F32), axis=0, keepdims=True)


def slope_back(ddown, slope, w_down, dep):
    rows, width = ddown.shape
    ff = slope.shape[1]
    tile = 768
    by = pl.BlockSpec((rows, tile), lambda i: (0, i))
    return call(
        slope_body, dep, (ff // tile,), [fixed((rows, width)), by, pl.BlockSpec((tile, width), lambda i: (i, 0))],
        [by, pl.BlockSpec((1, tile), lambda i: (0, i))], [shape((rows, ff), BF16), shape((1, ff), F32)],
        name="slope_back",
    )(ddown, slope, w_down)


def share(value, j, place, send, keep):
    rows = value.shape[0]

    @pl.when(place[j] < 2)
    def _():
        send[pl.ds(pl.multiple_of(place[j] * rows, rows), rows), :] = value

    @pl.when(place[j] >= 2)
    def _():
        keep[pl.ds(pl.multiple_of((place[j] - 2) * rows, rows), rows), :] = value


def up_send_body(which, a0, a1, a2, a3, b, *outs):
    value = dot(jnp.concatenate([a0[...], a1[...], a2[...], a3[...]], axis=0), b[...])
    rows = a0.shape[0]
    for j in range(4):
        outs[j][...] = value[j * rows:(j + 1) * rows]


def up_keep_body(which, place, a0, a1, a2, a3, b, *rest):
    came, (send, keep) = rest[:4], rest[4:]
    value = dot(jnp.concatenate([a0[...], a1[...], a2[...], a3[...]], axis=0), b[...])
    rows = a0.shape[0]
    for j in range(4):
        share(value[j * rows:(j + 1) * rows] + came[j][...], j, place, send, keep)


def up_grad(which, a, b, columns, place=None, came=None, dep=None):
    m, k = a.shape
    start, n = columns
    rows, tile = m // 8, 768
    ins = [pl.BlockSpec((rows, k), lambda i, w, *_, j=j: (2 * j + w[0], 0)) for j in range(4)]
    ins.append(pl.BlockSpec((k, tile), lambda i, *_: (0, i + start // tile)))
    by = lambda r: pl.BlockSpec((r, tile), lambda i, *_: (0, i))
    if came is None:
        return call(up_send_body, dep, (n // tile,), ins, [by(rows)] * 4, [shape((rows, n), F32)] * 4, scalars=1,
                    name="up_send")(which, a, a, a, a, b)
    return call(up_keep_body, dep, (n // tile,), ins + [by(rows)] * 4, [by(m // 4)] * 2,
                [shape((m // 4, n), F32)] * 2, scalars=2, name="up_keep")(which, place, a, a, a, a, b, *came)


def down_send_body(blocks, a, b, *outs):
    value = dot(a[...], b[...], 0, 0)
    for j, out in enumerate(outs):
        @pl.when(pl.program_id(0) == j)
        def _(out=out):
            out[...] = value


def down_keep_body(blocks, a, b, *rest):
    came, out = rest[:2], rest[2]
    value = dot(a[...], b[...], 0, 0)
    for j, one in enumerate(came):
        @pl.when(pl.program_id(0) == j)
        def _(one=one):
            out[...] = value + one[...]


def down_grad(blocks, a, b, came=None, dep=None):
    rows, m = a.shape
    n = b.shape[1]
    tile = m // 8
    block = (tile, n)
    ins = [pl.BlockSpec((rows, tile), lambda i, w: (0, w[i])), fixed((rows, n))]
    if came is None:
        return call(down_send_body, dep, (2,), ins, [pl.BlockSpec(block, lambda i, w: (0, 0))] * 2, [shape(block, F32)] * 2,
                    scalars=1, name="down_send")(blocks, a, b)
    return call(down_keep_body, dep, (2,), ins + [fixed(block)] * 2, pl.BlockSpec(block, lambda i, w: (i, 0)),
                shape((2 * tile, n), F32), scalars=1, name="down_keep")(blocks, a, b, *came)


MORE = 16


def last_small(which, kind, smalls):
    width = smalls[-1].shape[1]
    small1, upb, small2 = (v[...] for v in smalls[-3:])
    sums = [v[...] for v in smalls[:-3]]
    seqs = len(sums) // 2
    lines = [sum(sums[:seqs]), sum(sums[seqs:]), small1[:3]]
    lines += [upb[:, i:i + width] for i in range(0, upb.shape[1], width)] + [small2[:3]]
    lines = jnp.concatenate(lines, axis=0)
    lines = jnp.concatenate([lines, jnp.zeros((MORE - lines.shape[0], width), F32)], axis=0)
    return jnp.where((which[0] == 0) & (kind == 0), lines, 0.0)


def last_body(seqs, keeping, which, kinds, *refs):
    refs = list(refs)
    x, ctx, dattn = refs[:3]
    smalls, refs = refs[3:2 * seqs + 6], refs[2 * seqs + 6:]
    came, refs = (refs[:2], refs[2:]) if keeping else (None, refs)
    parts, refs = refs[:3 * seqs], refs[3 * seqs:]
    outs, refs = (refs[:1], refs[1:]) if keeping else (refs[:2], refs[2:])
    left, right, held, done, sems = refs
    half = left.shape[2]
    span = parts[0].shape[0]
    size = half + MORE
    cols = pl.ds(pl.multiple_of(which[0] * half, half), half)

    def reads(n, act):
        for kind in range(4):
            def load(kind=kind):
                act(pltpu.make_async_copy((ctx if kind == 3 else x).at[:, cols], left.at[n], sems.at[0, n]))
                if kind == 3:
                    act(pltpu.make_async_copy(dattn, right.at[n], sems.at[1, n]))
                else:
                    for s in range(seqs):
                        act(pltpu.make_async_copy(
                            parts[s * 3 + kind], right.at[n, pl.ds(s * span, span), :], sems.at[1 + s, n]))
            pl.when(kinds[n] == kind)(load)
        if keeping:
            act(pltpu.make_async_copy(came[n], held.at[n], sems.at[seqs + 1, n]))

    for n in range(2):
        reads(n, lambda copy: copy.start())
    writes = []
    for n in range(2):
        reads(n, lambda copy: copy.wait())
        value = dot(left[n], right[n], 0, 0)
        extra = last_small(which, kinds[n], smalls)
        if keeping:
            value = value + held[n, pl.ds(0, half), :]
            extra = extra + held[n, pl.ds(half, MORE), :]
        done[n, pl.ds(0, half), :] = value
        done[n, pl.ds(half, MORE), :] = extra
        to = outs[0].at[pl.ds(n * size, size), :] if keeping else outs[n]
        writes.append(pltpu.make_async_copy(done.at[n], to, sems.at[seqs + 2, n]))
        writes[-1].start()
    for copy in writes:
        copy.wait()


def last_grad(which, kinds, x, ctx, dattn, smalls, parts, came=None, dep=None):
    rows, width = x.shape
    half = width // 2
    size = half + MORE
    seqs = len(parts) // 3
    keeping = came is not None
    scratch = [pltpu.VMEM((2, rows, half), BF16), pltpu.VMEM((2, rows, width), BF16), pltpu.VMEM((2, size, width), F32),
               pltpu.VMEM((2, size, width), F32), pltpu.SemaphoreType.DMA((seqs + 3, 2))]
    ins = [ANY] * 3 + [VMEM] * len(smalls) + [ANY] * (len(parts) + (2 if keeping else 0))
    outs = [shape((2 * size, width), F32)] if keeping else [shape((size, width), F32)] * 2
    made = call(partial(last_body, seqs, keeping), dep, (), ins, [ANY] * len(outs), outs, scratch=scratch,
                scalars=2, name="last_keep" if keeping else "last_send")
    return made(which, kinds, x, ctx, dattn, *smalls, *(came if keeping else []), *parts)


def middle_body(dupper, w_up, dres, hat1, sc1, g1, w_out, dres1, dattn, dctx, small):
    dhid = dres[...] + dot(dupper[...], w_up[...], 1, 1)
    xhat = hat1[...]

    @pl.when(pl.program_id(0) == 0)
    def _():
        small[...] = jnp.zeros_like(small)

    small[1:2, :] += jnp.sum(dhid * xhat, axis=0, keepdims=True)
    small[2:3, :] += jnp.sum(dhid, axis=0, keepdims=True)
    dhat = dhid * row(g1)
    first = jnp.mean(dhat, axis=-1, keepdims=True)
    second = jnp.mean(dhat * xhat, axis=-1, keepdims=True)
    value = sc1[...] * (dhat - first - xhat * second)
    dres1[...] = value
    low = value.astype(BF16)
    dattn[...] = low
    small[0:1, :] += jnp.sum(low.astype(F32), axis=0, keepdims=True)
    dctx[...] = dot(low, w_out[...], 1, 1).astype(BF16)


def middle_back(dupper, w_up, dres, hat1, sc1, g1, w_out, dep):
    rows, width = dres.shape
    ff = dupper.shape[1]
    tile = 256
    by = lambda cols: pl.BlockSpec((tile, cols), lambda i: (i, 0))
    return call(
        middle_body, dep, (rows // tile,),
        [by(ff), fixed((width, ff)), by(width), by(width), by(1), line(width), fixed((width, width))],
        [by(width), by(width), by(width),
         pl.BlockSpec((8, width), lambda i: (0, 0))],
        [shape((rows, width), F32), shape((rows, width), BF16), shape((rows, width), BF16),
         shape((8, width), F32)], name="middle_back",
    )(dupper, w_up, dres, hat1, sc1, g1, w_out)


def attend_back_body(seq, span, group, counts, q, k, v, dctx, lse, dq, dk, dv, qsum, vsum):
    mask = key_mask(counts[0, seq], span)
    for pair in range(group // 2):
        turned, keys, values = [], [], []
        for half in range(2):
            head = pair * 2 + half
            lanes = pl.ds(head * HD, HD)
            query = q[:, lanes] * HD ** (-0.5)
            key = k[:, lanes]
            grad = dctx[:, lanes]
            scores = dot(key, query, 1, 1) + mask
            probs = jnp.exp(scores - lse[0, 0, pl.ds(head, 1), :])
            dprobs = dot(v[:, lanes], grad, 1, 1)
            values.append(dot(probs.astype(BF16), grad))
            inner = jnp.sum(probs * dprobs, axis=0, keepdims=True)
            dscores = (probs * (dprobs - inner)).astype(BF16)
            keys.append(dot(dscores, query))
            turned.append(dot(key, dscores, 0, 0))
        cols = pl.ds(pair * 2 * HD, 2 * HD)
        low = (jnp.concatenate(turned, axis=0).T * HD ** (-0.5)).astype(BF16)
        dq[:, cols] = low
        qsum[:, cols] = jnp.sum(low.astype(F32), axis=0, keepdims=True)
        dk[:, cols] = jnp.concatenate(keys, axis=1).astype(BF16)
        low = jnp.concatenate(values, axis=1).astype(BF16)
        dv[:, cols] = low
        vsum[:, cols] = jnp.sum(low.astype(F32), axis=0, keepdims=True)


def attend_back(seq, counts, q, k, v, dctx, lse, span, dep):
    width = q.shape[1]
    group = 4
    cols = group * HD
    piece = pl.BlockSpec((span, cols), lambda g: (seq, g))
    mine = pl.BlockSpec((span, cols), lambda g: (0, g))
    sums = pl.BlockSpec((1, cols), lambda g: (0, g))
    return call(
        partial(attend_back_body, seq, span, group), dep, (width // cols,),
        [SMEM] + [piece] * 4 + [pl.BlockSpec((1, 1, group, span), lambda g: (g, seq, 0, 0))],
        [mine] * 3 + [sums] * 2, [shape((span, width), BF16)] * 3 + [shape((1, width), F32)] * 2, name="attend_back",
    )(counts, q, k, v, dctx, lse)


def token_body(dres1, wq, wk, wv, *rest):
    parts, out = rest[:-1], rest[-1]
    for s in range(len(parts) // 3):
        at = pl.ds(s * parts[0].shape[0], parts[0].shape[0])
        total = dres1[at, :]
        for part, weight in zip(parts[s * 3:s * 3 + 3], (wq, wk, wv)):
            total = total + dot(part[...], weight[...], 1, 1)
        out[at, :] = total


def token_grad(dres1, w_qkv, parts, dep):
    rows, width = dres1.shape
    span = parts[0].shape[0]
    tile = 256
    by = pl.BlockSpec((rows, tile), lambda i: (0, i))
    weight = [pl.BlockSpec((tile, width), lambda i, k=k: (i, k)) for k in range(3)]
    return call(token_body, dep, (width // tile,), [by, *weight] + [fixed((span, width))] * len(parts), by,
                shape((rows, width), F32), name="token_grad")(dres1, w_qkv, w_qkv, w_qkv, *parts)


def add_split_body(steps, bit, held, came, send, keep):
    step = pl.program_id(0)
    value = held[...] + came[...]

    @pl.when(step < steps)
    def _():
        send[...] = value

    @pl.when(step >= steps)
    def _():
        keep[...] = value


def block_rows(rows, cols):
    best = 8
    for r in range(8, rows + 1, 8):
        if rows % r == 0 and r * cols * 4 <= MIB:
            best = r
    return best


def add_split(bit, held, came, dep=None):
    rows, cols = held.shape
    half = rows // 2
    tile = block_rows(half, cols)
    steps = half // tile

    def at(i, b):
        first = i < steps
        return jnp.where(first, (1 - b[0]) * steps + i, b[0] * steps + i - steps), 0

    block = (tile, cols)
    return call(
        partial(add_split_body, steps), dep, (2 * steps,), [pl.BlockSpec(block, at)] * 2,
        [pl.BlockSpec(block, lambda i, b: (jnp.minimum(i, steps - 1), 0)),
         pl.BlockSpec(block, lambda i, b: (jnp.maximum(i - steps, 0), 0))],
        [shape((half, cols), F32)] * 2, scalars=1, name="add_split",
    )(bit, held, came)


def add_body(held, came, out):
    out[...] = held[...] + came[...]


def add(held, came, dep=None):
    rows, cols = held.shape
    tile = block_rows(rows, cols)
    spec = pl.BlockSpec((tile, cols), lambda i: (i, 0))
    return call(add_body, dep, (rows // tile,), [spec] * 2, spec, shape((rows, cols), F32), name="add")(held, came)


def gather_body(n, places, *refs):
    pieces, out, (held, in_sems, out_sems) = refs[:n], refs[n], refs[n + 1:]
    rows = pieces[0].shape[0]
    reads = [pltpu.make_async_copy(piece, held.at[i], in_sems.at[i]) for i, piece in enumerate(pieces)]
    for copy in reads:
        copy.start()
    writes = []
    for i in range(n):
        reads[i].wait()
        at = pl.multiple_of(places[i] * rows, 8)
        writes.append(pltpu.make_async_copy(held.at[i], out.at[pl.ds(at, rows), :], out_sems.at[i]))
        writes[-1].start()
    for copy in writes:
        copy.wait()


def gather(places, pieces, dep=None):
    n = len(pieces)
    rows, cols = pieces[0].shape
    return call(
        partial(gather_body, n), dep, (), [SMEM] + [ANY] * n, ANY, shape((n * rows, cols), F32),
        scratch=[pltpu.VMEM((n, rows, cols), F32), pltpu.SemaphoreType.DMA((n,)), pltpu.SemaphoreType.DMA((n,))],
        name="gather",
    )(places, *pieces)


def spread_body(blocks, moves, lines, whole, *refs):
    outs, (held, in_sems, out_sems) = refs[:-3], refs[-3:]
    size = whole.shape[0] // blocks
    cols = whole.shape[1]
    reads = [pltpu.make_async_copy(whole.at[pl.ds(i * size, size), :], held.at[pl.ds(i * size, size), :], in_sems.at[i])
             for i in range(blocks)]
    for copy in reads:
        copy.start()
    writes = []
    for i in range(blocks):
        reads[i].wait()
        first, rows, out, row, col = moves[i]
        copy = pltpu.make_async_copy(
            held.at[pl.ds(first, rows), :], outs[out].at[pl.ds(row, rows), pl.ds(col, cols)], out_sems.at[i])
        copy.start()
        writes.append(copy)
    first = len(outs) - len(lines)
    for out, (row, count) in zip(outs[first:], lines):
        for k in range(count):
            out[pl.ds(k * cols, cols)] = held[pl.ds(row + k, 1), :].reshape(cols)
    for copy in writes:
        copy.wait()


def spread(whole, blocks, moves, outs, lines=(), dep=None):
    cols = whole.shape[1]
    return call(
        partial(spread_body, blocks, moves, lines), dep, (), [ANY], [ANY] * len(outs) + [VMEM] * len(lines),
        list(outs) + [shape((count * cols,), F32) for _, count in lines],
        scratch=[pltpu.VMEM(whole.shape, F32), pltpu.SemaphoreType.DMA((blocks,)), pltpu.SemaphoreType.DMA((blocks,))],
        name="spread",
    )(whole)


COLUMNS = {"B": (0, 3072)}
AT_ONCE = ("A", "C")
ORDER = (
    "down_s0", "down_s1", "down_k0", "slope", "down_k1", "upsB", "a2:A", "middle", "a3:A", "upkB", "ab0", "a4:A",
    "ab1", "last_s0", "last_s1", "a2:B", "last_k0", "a5:A", "last_k1", "a3:B", "a4:B", "a2:C", "a5:B", "a3:C",
    "gE:B", "a4:C", "token", "h8:B", "h7:B", "h9:B", "a5:C", "copy_down", "fin:B", "cut_last",
)


class Ring:
    def __init__(self, n_dp, towers):
        self.n_dp, self.towers = n_dp, towers
        self.dp, self.tower = lax.axis_index("dp").astype(jnp.int32), lax.axis_index("tower").astype(jnp.int32)
        self.core = self.tower & 1
        x, y = self.x, self.y = self.dp & 1, (self.tower >> 1) & 1
        self.outer = jnp.where(self.core == 0, x, y)
        self.inner = jnp.where(self.core == 0, y, x)
        self.near = (self.dp >> 1) & 1
        self.far = [b for b in (4, 8, 16, 32, 64) if b < n_dp]

    def move(self, value, partner):
        pairs = []
        for dp in range(self.n_dp):
            for tower in range(self.towers):
                to_dp, to_tower = partner(dp, tower)
                pairs.append((dp * self.towers + tower, to_dp * self.towers + to_tower))
        return lax.ppermute(value, ("dp", "tower"), pairs)

    def place(self):
        out = []
        for bx in range(2):
            for by in range(2):
                outer, inner = jnp.where(self.core == 0, bx, by), jnp.where(self.core == 0, by, bx)
                out.append(jnp.where(outer == self.outer, 2, 0) + inner)
        return jnp.stack(out).astype(jnp.int32)

    def order(self, core):
        mine = jnp.where(core == 0, self.x, self.y)
        out = []
        for outer in (1 - mine, mine):
            for inner in range(2):
                out.append(jnp.where(core == 0, outer * 2 + inner, inner * 2 + outer))
        return jnp.stack(out).astype(jnp.int32)

    def bits(self):
        bits = [1]
        while bits[0] * 2 < self.n_dp * self.towers:
            bits.insert(0, bits[0] * 2)
        return bits

    def to_index(self, value, bit):
        count = self.n_dp * self.towers
        return lax.ppermute(value, ("dp", "tower"), [(i, i ^ bit) for i in range(count)])

    def gather(self, value):
        groups = []
        for far in range(self.n_dp // 4):
            groups.append([(far * 4 + near * 2 + x) * self.towers + y * 2 + core
                           for x in range(2) for y in range(2) for core in range(2) for near in range(2)])
        return lax.all_gather(value, ("dp", "tower"), axis_index_groups=groups, tiled=True)

    def along_z(self, value):
        far = self.n_dp // 2
        groups = [[(z * 2 + x) * self.towers + t for z in range(far)] for x in range(2) for t in range(self.towers)]
        return lax.psum(value, ("dp", "tower"), axis_index_groups=groups)

    def gather_plane(self, value):
        groups = [[(z * 2 + x) * self.towers + t for x in range(2) for t in range(self.towers)]
                  for z in range(self.n_dp // 2)]
        return lax.all_gather(value, ("dp", "tower"), axis_index_groups=groups, tiled=True)

    def to_core(self, value):
        return self.move(value, lambda d, t: (d, t ^ 1))

    def to_outer(self, value):
        return self.move(value, lambda d, t: (d, t ^ 2) if t & 1 else (d ^ 1, t))

    def to_inner(self, value):
        return self.move(value, lambda d, t: (d ^ 1, t) if t & 1 else (d, t ^ 2))

    def to_dp(self, value, bit):
        return self.move(value, lambda d, t: (d ^ bit, t))


class Sum:
    def __init__(self, ring, at_once):
        self.ring, self.at_once, self.from_core = ring, at_once, []

    def core(self, send):
        self.from_core += [self.ring.to_core(v) for v in send]
        return [send[0]]

    def out(self, send, keep=None):
        self.keep = keep
        self.came = self.ring.to_outer(send)
        return [send if keep is None else keep]

    def rest(self, keep):
        self.keep = keep
        return [keep]

    def a2(self, dep):
        send, self.keep = add_split(self.ring.inner.reshape(1), self.keep, self.came, dep)
        self.came = self.ring.to_inner(send)
        return [self.keep]

    def a3(self, dep):
        send, self.keep = add_split(self.ring.near.reshape(1), self.keep, self.came, dep)
        self.came = self.ring.to_dp(send, 2)
        return [self.keep]

    def z3(self, dep):
        self.keep = add(self.keep, self.came, dep)
        self.summed = self.ring.along_z(self.keep)
        return [self.keep]

    def z5(self, dep):
        self.whole = self.ring.gather_plane(self.summed)
        return dep + [self.summed]

    def a4(self, dep):
        self.keep = add(self.keep, self.came, dep)
        for bit in self.ring.far[:-1]:
            self.keep = self.keep + self.ring.to_dp(self.keep, bit)
        self.came = self.ring.to_dp(self.keep, self.ring.far[-1])
        return [self.keep]

    def a5(self, dep):
        self.keep = add(self.keep, self.came, dep)
        if self.at_once:
            self.whole = self.ring.gather(self.keep)
        else:
            self.came = self.ring.to_dp(self.keep, 2)
        return [self.keep]

    def gE(self, dep):
        ring = self.ring
        own = gather(jnp.stack([ring.near, 1 - ring.near]), [self.keep, self.came], dep)
        self.own, self.inner, self.outer = own, ring.to_inner(own), ring.to_outer(own)
        self.own_c = ring.to_core(own)
        return [own]

    def h7(self, dep):
        self.both, self.inner_c = self.ring.to_outer(self.inner), self.ring.to_core(self.inner)
        return dep + [self.inner]

    def h8(self, dep):
        self.outer_c = self.ring.to_core(self.outer)
        return dep + [self.outer]

    def h9(self, dep):
        self.both_c = self.ring.to_core(self.both)
        return dep + [self.both]

    def fin(self, dep):
        ring = self.ring
        pieces = [self.own, self.inner, self.outer, self.both, self.own_c, self.inner_c, self.outer_c, self.both_c]
        places = []
        for core in (ring.core, 1 - ring.core):
            inner_step = jnp.where(core == 0, 2, 4)
            base = ring.x * 4 + ring.y * 2
            places += [(base ^ step) + core for step in (0 * inner_step, inner_step, 6 - inner_step, 6 + 0 * inner_step)]
        self.whole = gather(jnp.stack(places), pieces, dep)
        return [self.whole]


def local(n_dp, towers, tokens, lengths, positive, w_qkv, q_bias, v_bias, w_out, out_bias, norm1_gain, norm1_bias,
          w_up, up_bias, w_down, down_bias, norm2_gain, norm2_bias):
    seqs, span, width = tokens.shape[1:]
    ff = up_bias.shape[0]
    x = tokens.reshape(seqs * span, width)
    ring = Ring(n_dp, towers)
    mine, other = ring.core.reshape(1), (1 - ring.core).reshape(1)
    place = ring.place()
    q, k, v, ctx, lse = attend(lengths, x, w_qkv, q_bias, v_bias, seqs, span)
    hid_t, hat1, sc1, act, slope, hat2, sc2, sums, pooled = feed(
        lengths, x, ctx, w_out, w_up, w_down, out_bias, norm1_gain, norm1_bias, up_bias, down_bias, norm2_gain,
        norm2_bias, seqs, span, BF16)
    every, bits = pooled, ring.bits()
    for pair in range(0, len(bits) - 1, 2):
        first, second = bits[pair:pair + 2]
        every = jnp.concatenate(
            [every] + [ring.to_index(every, bit) for bit in (first, second, first | second)], axis=0)
    for bit in bits[len(bits) // 2 * 2:-1]:
        every = jnp.concatenate([every, ring.to_index(every, bit)], axis=0)
    half = every.shape[0] // 2
    halves = (every, ring.to_index(every, bits[-1])) if len(bits) % 2 else (every[:half], every[half:])
    own = (lax.axis_index("dp") * towers + lax.axis_index("tower")).astype(jnp.int32).reshape(1, 1)
    loss, dres, ddown, small2 = loss_step(lengths, own, positive, *halves, sums, norm2_gain, hat2, sc2,
                                          n_dp, towers, seqs, span, bits)
    sums_of, made = {}, {}

    for name in ("A", "C", *COLUMNS):
        sums_of[name] = Sum(ring, name in AT_ONCE)
    theirs, ours = ring.order(1 - ring.core), ring.order(ring.core)

    def down_send(n):
        def step(dep):
            return sums_of["A"].core(down_grad(2 * theirs[2 * n:2 * n + 2] + 1 - ring.core, act, ddown, dep=dep))
        return step

    def down_keep(n):
        def step(dep):
            one = sums_of["A"]
            got = down_grad(2 * ours[2 * n:2 * n + 2] + ring.core, act, ddown, one.from_core[2 * n:2 * n + 2], dep)
            return one.rest(got) if n else one.out(got)
        return step

    def slope_step(dep):
        made["dupper"], made["upb"] = slope_back(ddown, slope, w_down, dep)
        return [made["upb"]]

    def middle(dep):
        made["dres1"], made["dattn"], made["dctx"], made["small1"] = middle_back(
            made["dupper"], w_up, dres, hat1, sc1, norm1_gain, w_out, dep)
        return [made["small1"]]

    def attention(s):
        def step(dep):
            made[s] = attend_back(s, lengths, q, k, v, made["dctx"], lse, span, dep)
            return [made[s][3]]
        return step

    def last_inputs():
        parts = [v for s in range(seqs) for v in made[s][:3]]
        smalls = [made[s][k] for k in (3, 4) for s in range(seqs)] + [made["small1"], made["upb"], small2]
        return made["dattn"], smalls, parts

    def last_send(n):
        def step(dep):
            return sums_of["C"].core(last_grad(other, theirs[2 * n:2 * n + 2], x, ctx, *last_inputs(), dep=dep))
        return step

    def last_keep(n):
        def step(dep):
            one = sums_of["C"]
            (got,) = last_grad(mine, ours[2 * n:2 * n + 2], x, ctx, *last_inputs(), one.from_core[2 * n:2 * n + 2], dep)
            return one.rest(got) if n else one.out(got)
        return step

    def token(dep):
        made["tokens"] = token_grad(made["dres1"], w_qkv, [v for s in range(seqs) for v in made[s][:3]], dep)
        return [made["tokens"]]

    def up_send(name):
        def step(dep):
            return sums_of[name].core(up_grad(other, hid_t, made["dupper"], COLUMNS[name], dep=dep))
        return step

    def up_keep(name):
        def step(dep):
            one = sums_of[name]
            return one.out(*up_grad(mine, hid_t, made["dupper"], COLUMNS[name], place, one.from_core, dep))
        return step

    def copy_down(dep):
        rows = ff // 8
        (made["A"],) = spread(sums_of["A"].whole, 8, [(i * rows, rows, 0, i * rows, 0) for i in range(8)],
                              [shape((ff, width), F32)], dep=dep)
        return [made["A"]]

    def copy_up(dep):
        rows = width // 8
        (made["B"],) = spread(sums_of["B"].whole, 8, [(i * rows, rows, 0, i * rows, 0) for i in range(8)],
                              [shape((width, ff), F32)], dep=dep)
        return [made["B"]]

    def cut_last(dep):
        rows, size = width // 2, width // 2 + MORE
        moves = [(i * size, rows, i // 6, i % 2 * rows, (i // 2 % 3) * width) for i in range(8)]
        lines = [(rows + i, 1) for i in range(5)] + [(rows + 5, ff // width)]
        lines += [(rows + 5 + ff // width + i, 1) for i in range(3)]
        made["C"] = spread(sums_of["C"].whole, 8, moves, [shape((width, 3 * width), F32), shape((width, width), F32)],
                           lines, dep)
        return [made["C"][1]]

    steps = {"slope": slope_step, "middle": middle, "token": token, "copy_down": copy_down, "copy_up": copy_up,
             "cut_last": cut_last}
    for n in range(2):
        steps.update({f"down_s{n}": down_send(n), f"down_k{n}": down_keep(n),
                      f"last_s{n}": last_send(n), f"last_k{n}": last_keep(n)})
    steps.update({f"ab{s}": attention(s) for s in range(seqs)})
    for name in COLUMNS:
        steps["ups" + name], steps["upk" + name] = up_send(name), up_keep(name)
    dep = []
    for word in ORDER:
        what, _, name = word.partition(":")
        if what == "all":
            dep = dep + [sums_of[name].whole]
        elif name:
            dep = getattr(sums_of[name], what)(dep)
        else:
            dep = steps[what](dep)
    up = [sums_of[name].whole for name in COLUMNS]
    up = made["B"] if "B" in made else up[0] if len(up) == 1 else jnp.concatenate(up, axis=1)
    down = made["A"] if "A" in made else sums_of["A"].whole
    qkv, out, q_sum, v_sum, out_sum, gain1, shift1, up_sum, gain2, shift2, down_sum = made["C"]
    return (loss[0, 0], made["tokens"].reshape(tokens.shape), qkv, q_sum, v_sum, out, out_sum, gain1, shift1,
            up, up_sum, down, down_sum, gain2, shift2)


def solution(mesh):
    split = P("tower", "dp", None, None)
    in_specs = (split, P("tower", "dp")) + (P(),) * 14
    out_specs = (P(), split) + (P(),) * 13
    body = partial(local, mesh.shape["dp"], mesh.shape["tower"])
    return jax.shard_map(body, mesh=mesh, in_specs=in_specs, out_specs=out_specs, check_vma=False)
```
